256 devices in a mesh: sec: 16 (over x_hi, y, core), tile: 16 (over x_lo, z).
Axes of the slice: x: 4 (x_hi: 2, x_lo: 2; x = x_hi * 2 + x_lo), y: 4, z: 8, core: 2. Of those that a mesh axis runs over, the one named last changes fastest.
Arguments:
- sections: float32 [16, 2, 256, 2560], P('sec', None, None, 'tile'), may hold values from -6 to 6
- prior: float32 [2, 256, 2560], P(None, None, 'tile'), may hold values from -6 to 6
Outputs:
- peak_maps: float32 [16, 2, 1, 64, 256, 256], P('sec', None, None, 'tile')
The draws below stay inside these ranges and needn't reach their ends.
All inputs are finite; a program needn't handle non-finite values.
Results may differ from the reference program's by a relative error of at most 0.0097.
Values may be sent and summed in bfloat16 or wider, within the bound.
A program may use at most 64 MiB of HBM per device.

```python
import math
import jax
import jax.numpy as jnp
from jax import lax

PATCH = 256
STRIDE = 40
PR = 1
HALO = 108
ROWS = 256
WIDTH = 2560
NPC = 64
NSEC = 16


def level_of(own_key, dims, pieces, low, top_value):
    gain, own = 1.0, jax.random.fold_in(own_key, 6)
    for axis_at, shards_of in pieces:
        steps = jnp.exp(jax.random.uniform(jax.random.fold_in(own, axis_at), (shards_of,), jnp.float32, low / len(pieces), top_value / len(pieces)))
        gain = gain * jnp.repeat(steps, dims[axis_at] // shards_of).reshape([-1 if axis == axis_at else 1 for axis in range(len(dims))])
    return gain


def scatter_about(rng, shape, width, limit, split=(), held_as=jnp.bfloat16):
    factor_of = level_of(rng, shape, split, -0.22, 0.18) if split else 1.0
    values = jax.random.normal(rng, shape, jnp.float32) * width * factor_of
    return jnp.minimum(jnp.maximum(values, -limit), limit).astype(held_as)


def setup_inputs(seed: int = 0) -> dict:
    splits = jax.random.split(jax.random.key(seed), 3)
    return {
        "sections": scatter_about(splits[0], (NSEC, 2, ROWS, WIDTH), 1.0, 6.0, ((0, 16), (3, 16)), jnp.float32),
        "prior": scatter_about(splits[1], (2, ROWS, WIDTH), 1.0, 6.0, ((2, 16),), jnp.float32),
    }


eps = 1e-06

def tables():
    index = jnp.arange(PATCH, dtype=jnp.int32)
    product = index[:, None] * index[None, :] % PATCH
    angle = product.astype(jnp.float32) * (2.0 * math.pi / PATCH)
    return (jnp.cos(angle).astype(jnp.bfloat16), jnp.sin(angle).astype(jnp.bfloat16))

def cut_patches(strip):
    padded = jnp.pad(strip, ((0, 0), (0, 0), (HALO, HALO)))
    row_index = (STRIDE * jnp.arange(PR, dtype=jnp.int32))[:, None] + jnp.arange(PATCH, dtype=jnp.int32)[None, :]
    col_index = (STRIDE * jnp.arange(NPC, dtype=jnp.int32))[:, None] + jnp.arange(PATCH, dtype=jnp.int32)[None, :]
    return padded[:, row_index[:, None, :, None], col_index[None, :, None, :]]

def spectra(patches, cosine, sine):
    centered = patches - lax.optimization_barrier(jnp.mean(patches, axis=(-2, -1), keepdims=True))
    lowered = centered.astype(jnp.bfloat16).astype(jnp.float32)
    right = jnp.concatenate([cosine, -sine], axis=1).astype(jnp.float32)
    rowed = jnp.einsum('abcmn,nk->abcmk', lowered, right).astype(jnp.bfloat16).astype(jnp.float32)
    first = jnp.einsum('km,abcmq->abckq', cosine.astype(jnp.float32), rowed)
    second = jnp.einsum('km,abcmq->abckq', sine.astype(jnp.float32), rowed)
    real = first[..., :PATCH] + second[..., PATCH:]
    imag = first[..., PATCH:] - second[..., :PATCH]
    return jnp.concatenate([real, imag], axis=-1).astype(jnp.bfloat16)

def energies(spectrum):
    values = spectrum.astype(jnp.float32)
    return lax.optimization_barrier(jnp.sum(values * values, axis=(-2, -1))) / (PATCH * PATCH)

def peaks(spec_now, spec_prev, cosine, sine):
    now = spec_now.astype(jnp.float32)
    prev = spec_prev.astype(jnp.float32)
    now_re, now_im = (now[..., :PATCH], now[..., PATCH:])
    prev_re, prev_im = (prev[..., :PATCH], prev[..., PATCH:])
    cross_re = now_re * prev_re + now_im * prev_im
    cross_im = now_im * prev_re - now_re * prev_im
    cross = jnp.concatenate([cross_re, cross_im], axis=-1).astype(jnp.bfloat16).astype(jnp.float32)
    first = jnp.einsum('km,abcmq->abckq', cosine.astype(jnp.float32), cross)
    second = jnp.einsum('km,abcmq->abckq', sine.astype(jnp.float32), cross)
    turned_re = first[..., :PATCH] - second[..., PATCH:]
    turned_im = second[..., :PATCH] + first[..., PATCH:]
    turned = jnp.concatenate([turned_re, turned_im], axis=-1).astype(jnp.bfloat16).astype(jnp.float32)
    left = jnp.concatenate([cosine, -sine], axis=0).astype(jnp.float32)
    real = jnp.einsum('abcmq,qn->abcmn', turned, left)
    scale = PATCH * jnp.sqrt(energies(spec_now) + eps) * jnp.sqrt(energies(spec_prev) + eps)
    return real / scale[..., None, None]

def reference(sections, prior):
    cosine, sine = tables()
    start = spectra(cut_patches(prior), cosine, sine)

    def advance(carry, strip):
        spec = spectra(cut_patches(strip), cosine, sine)
        return (spec, peaks(spec, carry, cosine, sine))
    _, result = lax.scan(advance, start, sections)
    return result
```

```python
import functools

import jax
import jax.numpy as jnp
import ml_dtypes
import numpy as np
from jax import lax
from jax.experimental import pallas as pl
from jax.experimental.pallas import tpu as pltpu
from jax.sharding import PartitionSpec as P

N = 256
H = 128
STRIDE = 40
PC = 4
HALO = 108
LEVELS = 2
COLS = 160
EDGE = 112
EPS = 1e-06
MESH = pl.DeviceIdType.MESH
f32, bf16 = jnp.float32, jnp.bfloat16


def tables():
    i = np.arange(N)
    product = i[:, None] * i[None, :] % N
    cos = np.cos(product * (2.0 * np.pi / N))
    sin = np.sin(product * (2.0 * np.pi / N))
    alternate = cos[:, H]
    columns = np.concatenate([cos[:, :H], -sin[:, :H]], axis=1)
    columns[:, 0] = 0.0
    columns[:, H] = alternate
    ahead = np.concatenate([cos[:H], sin[:H]], axis=0)
    ahead[H] = alternate
    back = 2.0 * np.concatenate([cos[:, :H], sin[:, :H]], axis=1)
    back[:, 0] = 1.0
    back[:, H] = alternate
    last = 2.0 * np.concatenate([cos[:, :H], -sin[:, :H]], axis=1)
    last[:, 0] = alternate
    last[:, H] = 0.0
    lowered = [a.astype(ml_dtypes.bfloat16) for a in (columns, ahead, back, cos, sin)]
    return np.stack(lowered), last.astype(ml_dtypes.bfloat16)


def dot(a, b):
    return jnp.dot(a, b, preferred_element_type=f32)


def column_stage(x, table):
    mean = jnp.sum(x, axis=1, keepdims=True) * (1.0 / N)
    low = x - mean
    energy = jnp.sum(low * low, axis=1, keepdims=True)
    return dot(low.astype(bf16), table).astype(bf16), mean, energy


def side_rows(means, energies):
    lane = lax.broadcasted_iota(jnp.int32, (COLS, H), 1)
    block = jnp.zeros((COLS, H), f32)
    for at, value in enumerate(means + energies):
        block = jnp.where(lane == at, value, block)
    block = jnp.concatenate([block, jnp.zeros((N - COLS, H), f32)], axis=0)
    return jnp.transpose(block)[:8]


def windows(own, left, right, at):
    row = lax.broadcasted_iota(jnp.int32, (8, N), 0)
    lane = lax.broadcasted_iota(jnp.int32, (8, N), 1)
    patch = row % PC
    begin = patch * STRIDE + (N - HALO)
    from_left = (patch < PC - 1) & (lane >= begin)
    from_right = (lane >= COLS) | ((patch == PC - 1) & (lane < begin - N))

    def spread(side):
        return jnp.where(row < PC, side[at : at + 1], side[at + 1 : at + 2])

    return jnp.where(from_left, spread(left), jnp.where(from_right, spread(right), spread(own)))


def centre(own, left, right, at):
    means = windows(own, left, right, at)
    means = means - jnp.sum(means, axis=1, keepdims=True) * (1.0 / N)
    energies = windows(own, left, right, at + 2) + N * means * means
    return jnp.concatenate([N * means, energies], axis=0)


def mixed(upper, lower, split):
    row = lax.broadcasted_iota(jnp.int32, upper.shape, 0)
    return jnp.where(row < split, upper.astype(f32), lower.astype(f32)).astype(bf16)


def patch_of(j, level, own, left, right):
    if j == 0:
        parts = [
            own[level, 0:144],
            mixed(own[level, 144:160], left[level, 0:16], 4),
            left[level, 16:112],
        ]
    elif j == 1:
        parts = [
            own[level, 0:160],
            right[level, 0:16],
            mixed(right[level, 16:32], left[level, 32:48], 12),
            left[level, 48:112],
        ]
    elif j == 2:
        parts = [
            own[level, 0:160],
            right[level, 0:64],
            mixed(right[level, 64:80], left[level, 80:96], 4),
            left[level, 96:112],
        ]
    else:
        parts = [
            mixed(right[level, 96:112], own[level, 0:16], 12),
            own[level, 16:160],
            right[level, 0:96],
        ]
    return jnp.concatenate(parts, axis=0)


def cross(now, prev, out):
    step = 16
    for begin in range(0, H, step):
        even, odd = pl.ds(begin, step), pl.ds(H + begin, step)
        a_er, a_ei, a_oi, a_or = now[even, :H], now[even, H:], now[odd, :H], now[odd, H:]
        b_er, b_ei, b_oi, b_or = prev[even, :H], prev[even, H:], prev[odd, :H], prev[odd, H:]
        ee_r = a_er * b_er + a_ei * b_ei
        ee_i = a_ei * b_er - a_er * b_ei
        oo_r = a_or * b_or + a_oi * b_oi
        oo_i = a_or * b_oi - a_oi * b_or
        odd_r = (a_er * b_or - a_ei * b_oi) + (a_or * b_er - a_oi * b_ei)
        minus_i = (a_oi * b_er + a_or * b_ei) - (a_ei * b_or + a_er * b_oi)
        if begin == 0:
            first = lax.broadcasted_iota(jnp.int32, (step, H), 0) == 0
            even_r = jnp.where(first, ee_r, ee_r + oo_r)
            even_i = jnp.where(first, ee_i, ee_i + oo_i)
            minus_i = jnp.where(first, oo_r, minus_i)
            odd_r = jnp.where(first, oo_i, odd_r)
        else:
            even_r, even_i = ee_r + oo_r, ee_i + oo_i
        out[even, :H] = even_r.astype(bf16)
        out[even, H:] = even_i.astype(bf16)
        out[odd, :H] = minus_i.astype(bf16)
        out[odd, H:] = odd_r.astype(bf16)


def first_kernel(
    n_sec,
    n_tile,
    x_hbm,
    prior_hbm,
    table_hbm,
    turned,
    rows_out,
    x,
    prior,
    table,
    a_own,
    a_left,
    a_right,
    b_own,
    b_left,
    b_right,
    side,
    side_out,
    side_in,
    a_rows,
    b_rows,
    spec_a,
    spec_b,
    crossed,
    load_sem,
    send_sem,
    recv_sem,
):
    s, t = lax.axis_index("sec"), lax.axis_index("tile")
    has_left, has_right = t > 0, t < n_tile - 1
    has_next, has_prev = s < n_sec - 1, s > 0
    even = s % 2 == 0
    to_left, to_right, to_next = {"tile": t - 1}, {"tile": t + 1}, {"sec": s + 1}

    def load(source, target, at):
        return pltpu.make_async_copy(source, target, load_sem.at[at])

    load_x = [load(x_hbm.at[i], x.at[i], i) for i in range(LEVELS)]
    load_first = load(table_hbm.at[0], table.at[0], 2)
    load_rest = load(table_hbm.at[1:5], table.at[1:5], 3)
    load_prior = load(prior_hbm, prior, 4)
    load_first.start()
    for copy in load_x:
        copy.start()
    load_rest.start()

    barrier = pltpu.get_barrier_semaphore()

    def greet(there, device):
        @pl.when(there)
        def _():
            pl.semaphore_signal(barrier, inc=1, device_id=device, device_id_type=MESH)

    greet(has_left, to_left)
    greet(has_right, to_right)
    greet(has_prev, {"sec": s - 1})

    @pl.when(s == 0)
    def _():
        load_prior.start()

    started = []
    count = [0]

    def remote(source, target, device, arrival):
        at = count[0]
        count[0] += 1
        return pltpu.make_async_remote_copy(
            src_ref=source,
            dst_ref=target,
            send_sem=send_sem.at[at],
            recv_sem=recv_sem.at[arrival],
            device_id=device,
            device_id_type=MESH,
        )

    def send(there, *what):
        copy = remote(*what)
        pl.when(there)(copy.start)
        started.append((there, copy))

    def arrived(there, target, arrival):
        copy = pltpu.make_async_remote_copy(
            src_ref=target,
            dst_ref=target,
            send_sem=send_sem.at[0],
            recv_sem=recv_sem.at[arrival],
            device_id=to_next,
            device_id_type=MESH,
        )
        if there is None:
            copy.wait_recv()
        else:
            pl.when(there)(copy.wait_recv)

    @pl.when(jnp.logical_not(has_left))
    def _():
        a_left[...] = jnp.zeros_like(a_left)
        b_left[...] = jnp.zeros_like(b_left)
        side_in[0] = jnp.zeros((8, N), f32)

    @pl.when(jnp.logical_not(has_right))
    def _():
        a_right[...] = jnp.zeros_like(a_right)
        b_right[...] = jnp.zeros_like(b_right)
        side_in[1] = jnp.zeros((8, N), f32)

    low, high = pl.ds(0, EDGE), pl.ds(COLS - EDGE, EDGE)
    load_first.wait()
    means, energies = [], []
    for i in range(LEVELS):
        load_x[i].wait()
        spectrum, mean, energy = column_stage(x[i], table[0])
        a_own[i] = spectrum
        means.append(mean)
        energies.append(energy)
        if i == 0:
            neighbours = [has_left, has_right, has_next]
            pl.semaphore_wait(barrier, sum(v.astype(jnp.int32) for v in neighbours))
        send(has_right, a_own.at[i, high], a_left.at[i], to_right, i)
        send(has_left, a_own.at[i, low], a_right.at[i], to_left, 2 + i)
        send(has_next, a_own.at[i], b_own.at[i], to_next, 4 + i)

    side[...] = side_rows(means, energies)

    @pl.when(s == 0)
    def _():
        load_prior.wait()
        prior_means, prior_energies = [], []
        for i in range(LEVELS):
            spectrum, mean, energy = column_stage(prior[i], table[0])
            b_own[i] = spectrum
            prior_means.append(mean)
            prior_energies.append(energy)
        rows = side_rows(prior_means, prior_energies)
        side[4:8] = rows[0:4]

    side_out[0] = pltpu.roll(side[...], N - COLS, 1)
    side_out[1] = pltpu.roll(side[...], COLS, 1)
    send(has_right, side_out.at[0], side_in.at[0], to_right, 10)
    send(has_left, side_out.at[1], side_in.at[1], to_left, 11)

    for i in range(LEVELS):
        arrived(has_left, a_left.at[i], i)
        arrived(has_right, a_right.at[i], 2 + i)
        forward = even & has_next
        send(forward & has_left, a_left.at[i], b_left.at[i], to_next, 6 + i)
        send(forward & has_right, a_right.at[i], b_right.at[i], to_next, 8 + i)
        arrived(has_prev, b_own.at[i], 4 + i)
        send(even & has_right, b_own.at[i, high], b_left.at[i], to_right, 6 + i)
        send(even & has_left, b_own.at[i, low], b_right.at[i], to_left, 8 + i)

    load_rest.wait()
    arrived(has_left, side_in.at[0], 10)
    arrived(has_right, side_in.at[1], 11)
    a_rows[...] = centre(side[...], side_in[0], side_in[1], 0)
    send(has_next, a_rows, b_rows, to_next, 12)

    @pl.when(s == 0)
    def _():
        b_rows[...] = centre(side[...], side_in[0], side_in[1], 4)

    arrived(has_prev, b_rows, 12)
    pair = jnp.concatenate([a_rows[0:8], b_rows[0:8]], axis=0).astype(bf16)
    even_part, odd_part = dot(pair, table[3]), dot(pair, table[4])
    a_e, b_e, a_o, b_o = even_part[:8], even_part[8:], odd_part[:8], odd_part[8:]
    both = jnp.concatenate([a_e * b_e + a_o * b_o, a_e * b_o - a_o * b_e], axis=0).astype(bf16)
    flat = dot(both, table[3])[:8] - dot(both, table[4])[8:]
    energy_a = jnp.sum(a_rows[8:16], axis=1, keepdims=True)
    energy_b = jnp.sum(b_rows[8:16], axis=1, keepdims=True)
    scale = 1.0 / (N * jnp.sqrt(energy_a + EPS) * jnp.sqrt(energy_b + EPS))
    rows_out[0:8] = flat * scale
    rows_out[8:16] = jnp.broadcast_to(scale, (8, N))

    @pl.loop(0, LEVELS)
    def _(i):
        for there, target, arrival in (
            (has_left, b_left, 6),
            (has_right, b_right, 8),
        ):
            arrived(there, target.at[i], arrival + i)
        for j in range(PC):
            spec_a[...] = dot(table[1], patch_of(j, i, a_own, a_left, a_right))
            spec_b[...] = dot(table[1], patch_of(j, i, b_own, b_left, b_right))
            cross(spec_a, spec_b, crossed)
            turned[i * PC + j] = dot(table[2], crossed[...]).astype(bf16)

    for there, copy in started:
        pl.when(there)(copy.wait_send)


def last_kernel(turned, rows, table, out_hbm, held, sem):
    copies = []
    for p in range(LEVELS * PC):
        product = lax.dot_general(
            table[...], turned[p], (((1,), (1,)), ((), ())), preferred_element_type=f32
        )
        held[p] = product * rows[8 + p : 9 + p] + rows[p : p + 1]
        copy = pltpu.make_async_copy(held.at[p], out_hbm.at[p], sem.at[p])
        copy.start()
        copies.append(copy)
    for copy in copies:
        copy.wait()


def local(n_sec, n_tile, sections, prior):
    x = jnp.swapaxes(sections[0], 1, 2)
    before = jnp.swapaxes(prior, 1, 2)
    table, last = tables()
    anywhere = pl.BlockSpec(memory_space=pl.ANY)
    vmem = pl.BlockSpec(memory_space=pltpu.VMEM)
    patches = LEVELS * PC
    half = lambda rows: pltpu.VMEM((LEVELS, rows, N), bf16)
    turned, rows = pl.pallas_call(
        functools.partial(first_kernel, n_sec, n_tile),
        out_shape=(
            jax.ShapeDtypeStruct((patches, N, N), bf16),
            jax.ShapeDtypeStruct((16, N), f32),
        ),
        in_specs=[anywhere] * 3,
        out_specs=(vmem, vmem),
        scratch_shapes=[
            pltpu.VMEM((LEVELS, COLS, N), f32),
            pltpu.VMEM((LEVELS, COLS, N), f32),
            pltpu.VMEM((5, N, N), bf16),
            half(COLS),
            half(EDGE),
            half(EDGE),
            half(COLS),
            half(EDGE),
            half(EDGE),
            pltpu.VMEM((8, N), f32),
            pltpu.VMEM((2, 8, N), f32),
            pltpu.VMEM((2, 8, N), f32),
            pltpu.VMEM((16, N), f32),
            pltpu.VMEM((16, N), f32),
            pltpu.VMEM((N, N), f32),
            pltpu.VMEM((N, N), f32),
            pltpu.VMEM((N, N), bf16),
            pltpu.SemaphoreType.DMA((5,)),
            pltpu.SemaphoreType.DMA((17,)),
            pltpu.SemaphoreType.DMA((13,)),
        ],
        compiler_params=pltpu.CompilerParams(
            collective_id=0, has_side_effects=True, vmem_limit_bytes=16 * 2**20
        ),
        name="spectra",
    )(x, before, jnp.asarray(table))
    maps = pl.pallas_call(
        last_kernel,
        out_shape=jax.ShapeDtypeStruct((patches, N, N), f32),
        in_specs=[vmem] * 3,
        out_specs=anywhere,
        scratch_shapes=[pltpu.VMEM((patches, N, N), f32), pltpu.SemaphoreType.DMA((patches,))],
        compiler_params=pltpu.CompilerParams(vmem_limit_bytes=16 * 2**20),
        name="maps",
    )(turned, rows, jnp.asarray(last))
    return maps.reshape(1, LEVELS, 1, PC, N, N)


def solution(mesh):
    return jax.shard_map(
        functools.partial(local, mesh.shape["sec"], mesh.shape["tile"]),
        mesh=mesh,
        in_specs=(P("sec", None, None, "tile"), P(None, None, "tile")),
        out_specs=P("sec", None, None, "tile", None, None),
        check_vma=False,
    )
```

```python
import functools

import jax
import jax.numpy as jnp
import ml_dtypes
import numpy as np
from jax import lax
from jax.experimental import pallas as pl
from jax.experimental.pallas import tpu as pltpu
from jax.sharding import PartitionSpec as P

N = 256
H = 128
STRIDE = 40
PC = 4
HALO = 108
LEVELS = 2
COLS = 160
EDGE = 112
EPS = 1e-06
MESH = pl.DeviceIdType.MESH
f32, bf16 = jnp.float32, jnp.bfloat16


def tables():
    i = np.arange(N)
    product = i[:, None] * i[None, :] % N
    cos = np.cos(product * (2.0 * np.pi / N))
    sin = np.sin(product * (2.0 * np.pi / N))
    alternate = cos[:, H]
    columns = np.concatenate([cos[:, :H], -sin[:, :H]], axis=1)
    columns[:, 0] = 0.0
    columns[:, H] = alternate
    ahead = np.concatenate([cos[:H], sin[:H]], axis=0)
    ahead[H] = alternate
    back = 2.0 * np.concatenate([cos[:, :H], sin[:, :H]], axis=1)
    back[:, 0] = 1.0
    back[:, H] = alternate
    last = 2.0 * np.concatenate([cos[:, :H], -sin[:, :H]], axis=1)
    last[:, 0] = alternate
    last[:, H] = 0.0
    lowered = [a.astype(ml_dtypes.bfloat16) for a in (columns, ahead, back, cos, sin, last)]
    return np.stack(lowered)


def dot(a, b):
    return jnp.dot(a, b, preferred_element_type=f32)


def column_stage(x, table):
    mean = jnp.sum(x, axis=1, keepdims=True) * (1.0 / N)
    low = x - mean
    energy = jnp.sum(low * low, axis=1, keepdims=True)
    return dot(low.astype(bf16), table).astype(bf16), mean, energy


def side_rows(means, energies):
    lane = lax.broadcasted_iota(jnp.int32, (COLS, H), 1)
    block = jnp.zeros((COLS, H), f32)
    for at, value in enumerate(means + energies):
        block = jnp.where(lane == at, value, block)
    block = jnp.concatenate([block, jnp.zeros((N - COLS, H), f32)], axis=0)
    return jnp.transpose(block)[:8]


def windows(own, left, right, at):
    row = lax.broadcasted_iota(jnp.int32, (8, N), 0)
    lane = lax.broadcasted_iota(jnp.int32, (8, N), 1)
    patch = row % PC
    begin = patch * STRIDE + (N - HALO)
    from_left = (patch < PC - 1) & (lane >= begin)
    from_right = (lane >= COLS) | ((patch == PC - 1) & (lane < begin - N))

    def spread(side):
        return jnp.where(row < PC, side[at : at + 1], side[at + 1 : at + 2])

    return jnp.where(from_left, spread(left), jnp.where(from_right, spread(right), spread(own)))


def centre(own, left, right):
    means = windows(own, left, right, 0)
    means = means - jnp.sum(means, axis=1, keepdims=True) * (1.0 / N)
    energies = windows(own, left, right, 2) + N * means * means
    return N * means, jnp.sum(energies, axis=1, keepdims=True)


def mixed(upper, lower, split):
    row = lax.broadcasted_iota(jnp.int32, upper.shape, 0)
    return jnp.where(row < split, upper.astype(f32), lower.astype(f32)).astype(bf16)


def patch_of(j, level, own, left, right):
    if j == 0:
        parts = [
            own[level, 0:144],
            mixed(own[level, 144:160], left[level, 0:16], 4),
            left[level, 16:112],
        ]
    elif j == 1:
        parts = [
            own[level, 0:160],
            right[level, 0:16],
            mixed(right[level, 16:32], left[level, 32:48], 12),
            left[level, 48:112],
        ]
    elif j == 2:
        parts = [
            own[level, 0:160],
            right[level, 0:64],
            mixed(right[level, 64:80], left[level, 80:96], 4),
            left[level, 96:112],
        ]
    else:
        parts = [
            mixed(right[level, 96:112], own[level, 0:16], 12),
            own[level, 16:160],
            right[level, 0:96],
        ]
    return jnp.concatenate(parts, axis=0)


def cross(now, prev, out):
    step = 16
    for begin in range(0, H, step):
        even, odd = pl.ds(begin, step), pl.ds(H + begin, step)
        a_er, a_ei, a_oi, a_or = now[even, :H], now[even, H:], now[odd, :H], now[odd, H:]
        b_er, b_ei, b_oi, b_or = prev[even, :H], prev[even, H:], prev[odd, :H], prev[odd, H:]
        ee_r = a_er * b_er + a_ei * b_ei
        ee_i = a_ei * b_er - a_er * b_ei
        oo_r = a_or * b_or + a_oi * b_oi
        oo_i = a_or * b_oi - a_oi * b_or
        odd_r = (a_er * b_or - a_ei * b_oi) + (a_or * b_er - a_oi * b_ei)
        minus_i = (a_oi * b_er + a_or * b_ei) - (a_ei * b_or + a_er * b_oi)
        if begin == 0:
            first = lax.broadcasted_iota(jnp.int32, (step, H), 0) == 0
            even_r = jnp.where(first, ee_r, ee_r + oo_r)
            even_i = jnp.where(first, ee_i, ee_i + oo_i)
            minus_i = jnp.where(first, oo_r, minus_i)
            odd_r = jnp.where(first, oo_i, odd_r)
        else:
            even_r, even_i = ee_r + oo_r, ee_i + oo_i
        out[even, :H] = even_r.astype(bf16)
        out[even, H:] = even_i.astype(bf16)
        out[odd, :H] = minus_i.astype(bf16)
        out[odd, H:] = odd_r.astype(bf16)


def first_kernel(
    n_sec,
    n_tile,
    x_hbm,
    prior_hbm,
    table_hbm,
    turned,
    rows_out,
    table,
    spec_later,
    b_own,
    b_left,
    b_right,
    x,
    prior,
    a_own,
    a_left,
    a_right,
    side,
    side_out,
    side_in,
    b_side,
    spec_a,
    spec_b,
    crossed,
    load_sem,
    send_sem,
    recv_sem,
):
    s, t = lax.axis_index("sec"), lax.axis_index("tile")
    has_left, has_right = t > 0, t < n_tile - 1
    has_next, has_prev = s < n_sec - 1, s > 0
    middle = n_tile // 2
    direct_out = (t == middle - 1) & (s % 2 == 1) & has_next & (s != n_sec // 2 - 1)
    direct_in = (t == middle) & (s % 2 == 0) & has_prev & (s != n_sec // 2)
    direct_past = (t == middle) & (s % 2 == 1) & has_next & (s != n_sec // 2 - 1)
    to_left, to_right, to_next = {"tile": t - 1}, {"tile": t + 1}, {"sec": s + 1}

    def load(source, target, at):
        return pltpu.make_async_copy(source, target, load_sem.at[at])

    load_x = [load(x_hbm.at[i], x.at[i], i) for i in range(LEVELS)]
    load_first = load(table_hbm.at[0], table.at[0], 2)
    load_rest = load(table_hbm.at[1:6], table.at[1:6], 3)
    load_prior = load(prior_hbm, prior, 4)
    load_first.start()
    for copy in load_x:
        copy.start()
    load_rest.start()

    barrier = pltpu.get_barrier_semaphore()

    def greet(there, device):
        @pl.when(there)
        def _():
            pl.semaphore_signal(barrier, inc=1, device_id=device, device_id_type=MESH)

    greet(has_left, to_left)
    greet(has_right, to_right)
    greet(has_prev, {"sec": s - 1})
    greet(direct_in, {"sec": s - 1, "tile": t - 1})

    @pl.when(s == 0)
    def _():
        load_prior.start()

    started = []
    count = [0]

    def remote(source, target, device, arrival):
        at = count[0]
        count[0] += 1
        return pltpu.make_async_remote_copy(
            src_ref=source,
            dst_ref=target,
            send_sem=send_sem.at[at],
            recv_sem=recv_sem.at[arrival],
            device_id=device,
            device_id_type=MESH,
        )

    def send(there, *what):
        copy = remote(*what)
        pl.when(there)(copy.start)
        started.append((there, copy))

    def arrived(there, target, arrival):
        copy = pltpu.make_async_remote_copy(
            src_ref=target,
            dst_ref=target,
            send_sem=send_sem.at[0],
            recv_sem=recv_sem.at[arrival],
            device_id=to_next,
            device_id_type=MESH,
        )
        if there is None:
            copy.wait_recv()
        else:
            pl.when(there)(copy.wait_recv)

    @pl.when(jnp.logical_not(has_left))
    def _():
        a_left[...] = jnp.zeros_like(a_left)
        b_left[...] = jnp.zeros_like(b_left)
        side_in[0] = jnp.zeros((8, N), f32)
        b_side[1] = jnp.zeros((8, N), f32)

    @pl.when(jnp.logical_not(has_right))
    def _():
        a_right[...] = jnp.zeros_like(a_right)
        b_right[...] = jnp.zeros_like(b_right)
        side_in[1] = jnp.zeros((8, N), f32)
        b_side[2] = jnp.zeros((8, N), f32)

    low, high = pl.ds(0, EDGE), pl.ds(COLS - EDGE, EDGE)
    to_direct = {"sec": s + 1, "tile": t + 1}

    def send_columns(i):
        send(has_right, a_own.at[i, high], a_left.at[i], to_right, i)
        send(direct_out, a_own.at[i, high], b_left.at[i], to_direct, 6 + i)
        send(has_left, a_own.at[i, low], a_right.at[i], to_left, 2 + i)
        send(has_next, a_own.at[i], b_own.at[i], to_next, 4 + i)

    load_first.wait()
    stats = []
    for i in range(LEVELS):
        load_x[i].wait()
        a_own[i], *stat = column_stage(x[i], table[0])
        stats.append(stat)
        if i == 0:
            targets = [has_left, has_right, has_next, direct_out]
            pl.semaphore_wait(barrier, sum(v.astype(jnp.int32) for v in targets))
            send_columns(i)
    side[...] = side_rows(*zip(*stats))

    @pl.when(s == 0)
    def _():
        load_prior.wait()
        prior_stats = []
        for i in range(LEVELS):
            b_own[i], *stat = column_stage(prior[i], table[0])
            prior_stats.append(stat)
        rows = side_rows(*zip(*prior_stats))
        side[4:8] = rows[0:4]

    side_out[0] = pltpu.roll(side[...], N - COLS, 1)
    side_out[1] = pltpu.roll(side[...], COLS, 1)
    send(has_right, side_out.at[0], side_in.at[0], to_right, 10)
    send(direct_out, side_out.at[0], b_side.at[1], to_direct, 13)
    send(has_left, side_out.at[1], side_in.at[1], to_left, 11)
    send(has_next, side, b_side.at[0], to_next, 12)
    send_columns(LEVELS - 1)
    for i in range(LEVELS):
        send((s == 0) & has_right, b_own.at[i, high], b_left.at[i], to_right, 6 + i)
        send((s == 0) & has_left, b_own.at[i, low], b_right.at[i], to_left, 8 + i)

    passed_on = has_next & has_left & jnp.logical_not(direct_past)
    for i in range(LEVELS):
        arrived(has_right, a_right.at[i], 2 + i)
        send(has_next & has_right, a_right.at[i], b_right.at[i], to_next, 8 + i)
        arrived(has_left, a_left.at[i], i)
        send(passed_on, a_left.at[i], b_left.at[i], to_next, 6 + i)
        if i == 0:
            arrived(has_right, side_in.at[1], 11)
            send(has_next & has_right, side_in.at[1], b_side.at[2], to_next, 14)
            arrived(has_left, side_in.at[0], 10)
            send(passed_on, side_in.at[0], b_side.at[1], to_next, 13)

    load_rest.wait()
    for j in range(PC):
        spec_a[j] = dot(table[1], patch_of(j, 0, a_own, a_left, a_right))
    for j in range(PC):
        spec_later[j] = dot(table[1], patch_of(j, 1, a_own, a_left, a_right))

    def previous_arrived(i):
        arrived(has_prev, b_own.at[i], 4 + i)
        arrived(has_right, b_right.at[i], 8 + i)
        arrived(has_left, b_left.at[i], 6 + i)

    previous_arrived(0)
    for j in range(PC):
        spec_b[j] = dot(table[1], patch_of(j, 0, b_own, b_left, b_right))
    for j in range(PC):
        cross(spec_a.at[j], spec_b.at[j], crossed.at[j])
        turned[j] = dot(table[2], crossed[j]).astype(bf16)

    arrived(has_prev, b_side.at[0], 12)
    arrived(has_prev & has_right, b_side.at[2], 14)
    arrived(has_prev & has_left, b_side.at[1], 13)

    @pl.when(s == 0)
    def _():
        b_side[0] = pltpu.roll(side[...], 4, 0)
        b_side[1] = pltpu.roll(side_in[0], 4, 0)
        b_side[2] = pltpu.roll(side_in[1], 4, 0)

    a_flat, a_energy = centre(side[...], side_in[0], side_in[1])
    b_flat, b_energy = centre(b_side[0], b_side[1], b_side[2])
    pair = jnp.concatenate([a_flat, b_flat], axis=0).astype(bf16)
    even_part, odd_part = dot(pair, table[3]), dot(pair, table[4])
    a_e, b_e, a_o, b_o = even_part[:8], even_part[8:], odd_part[:8], odd_part[8:]
    both = jnp.concatenate([a_e * b_e + a_o * b_o, a_e * b_o - a_o * b_e], axis=0).astype(bf16)
    flat = dot(both, table[3])[:8] - dot(both, table[4])[8:]
    scale = 1.0 / (N * jnp.sqrt(a_energy + EPS) * jnp.sqrt(b_energy + EPS))
    rows_out[0:8] = flat * scale
    rows_out[8:16] = jnp.broadcast_to(scale, (8, N))

    previous_arrived(1)
    for there, copy in started:
        pl.when(there)(copy.wait_send)


def last_kernel(turned, rows, table, spec_a, b_own, b_left, b_right, out_hbm, spec_b, crossed, held, sem):
    copies = []

    def finish(p, turned_p):
        product = lax.dot_general(
            table[5], turned_p, (((1,), (1,)), ((), ())), preferred_element_type=f32
        )
        held[p] = product * rows[8 + p : 9 + p] + rows[p : p + 1]
        copy = pltpu.make_async_copy(held.at[p], out_hbm.at[p], sem.at[p])
        copy.start()
        copies.append(copy)

    for j in range(PC):
        finish(j, turned[j])
    for j in range(PC):
        spec_b[j] = dot(table[1], patch_of(j, 1, b_own, b_left, b_right))
    for j in range(PC):
        cross(spec_a.at[j], spec_b.at[j], crossed.at[j])
        finish(PC + j, dot(table[2], crossed[j]).astype(bf16))
    for copy in copies:
        copy.wait()


def local(n_sec, n_tile, sections, prior):
    x = jnp.swapaxes(sections[0], 1, 2)
    before = jnp.swapaxes(prior, 1, 2)
    hbm = pl.BlockSpec(memory_space=pltpu.HBM)
    vmem = pl.BlockSpec(memory_space=pltpu.VMEM)
    patches = LEVELS * PC
    columns = lambda rows: pltpu.VMEM((LEVELS, rows, N), bf16)
    held = lambda *shape: jax.ShapeDtypeStruct(shape, bf16)
    operands = (x, before, jnp.asarray(tables()))
    results = pl.pallas_call(
        functools.partial(first_kernel, n_sec, n_tile),
        out_shape=(
            held(PC, N, N),
            jax.ShapeDtypeStruct((16, N), f32),
            held(6, N, N),
            jax.ShapeDtypeStruct((PC, N, N), f32),
            held(LEVELS, COLS, N),
            held(LEVELS, EDGE, N),
            held(LEVELS, EDGE, N),
        ),
        in_specs=[hbm] * 3,
        out_specs=(vmem,) * 7,
        scratch_shapes=[
            pltpu.VMEM((LEVELS, COLS, N), f32),
            pltpu.VMEM((LEVELS, COLS, N), f32),
            columns(COLS),
            columns(EDGE),
            columns(EDGE),
            pltpu.VMEM((8, N), f32),
            pltpu.VMEM((2, 8, N), f32),
            pltpu.VMEM((2, 8, N), f32),
            pltpu.VMEM((3, 8, N), f32),
            pltpu.VMEM((PC, N, N), f32),
            pltpu.VMEM((PC, N, N), f32),
            pltpu.VMEM((PC, N, N), bf16),
            pltpu.SemaphoreType.DMA((5,)),
            pltpu.SemaphoreType.DMA((24,)),
            pltpu.SemaphoreType.DMA((15,)),
        ],
        compiler_params=pltpu.CompilerParams(
            collective_id=0, has_side_effects=True, vmem_limit_bytes=16 * 2**20
        ),
        name="spectra",
    )(*(pltpu.with_memory_space_constraint(v, pltpu.HBM) for v in operands))
    maps = pl.pallas_call(
        last_kernel,
        out_shape=jax.ShapeDtypeStruct((patches, N, N), f32),
        in_specs=[vmem] * 7,
        out_specs=hbm,
        scratch_shapes=[
            pltpu.VMEM((PC, N, N), f32),
            pltpu.VMEM((PC, N, N), bf16),
            pltpu.VMEM((patches, N, N), f32),
            pltpu.SemaphoreType.DMA((patches,)),
        ],
        compiler_params=pltpu.CompilerParams(vmem_limit_bytes=16 * 2**20),
        name="maps",
    )(*results)
    return maps.reshape(1, LEVELS, 1, PC, N, N)


def solution(mesh):
    return jax.shard_map(
        functools.partial(local, mesh.shape["sec"], mesh.shape["tile"]),
        mesh=mesh,
        in_specs=(P("sec", None, None, "tile"), P(None, None, "tile")),
        out_specs=P("sec", None, None, "tile", None, None),
        check_vma=False,
    )
```

```python
import functools

import jax
import jax.numpy as jnp
import ml_dtypes
import numpy as np
from jax import lax
from jax.experimental import pallas as pl
from jax.experimental.pallas import tpu as pltpu
from jax.sharding import PartitionSpec as P

N = 256
H = 128
STRIDE = 40
PC = 4
HALO = 108
LEVELS = 2
COLS = 160
EDGE = 112
EPS = 1e-06
MESH = pl.DeviceIdType.MESH
f32, bf16 = jnp.float32, jnp.bfloat16


def tables():
    i = np.arange(N)
    product = i[:, None] * i[None, :] % N
    cos = np.cos(product * (2.0 * np.pi / N))
    sin = np.sin(product * (2.0 * np.pi / N))
    alternate = cos[:, H]
    columns = np.concatenate([cos[:, :H], -sin[:, :H]], axis=1)
    columns[:, 0] = 0.0
    columns[:, H] = alternate
    ahead = np.concatenate([cos[:H], sin[:H]], axis=0)
    ahead[H] = alternate
    back = 2.0 * np.concatenate([cos[:, :H], sin[:, :H]], axis=1)
    back[:, 0] = 1.0
    back[:, H] = alternate
    last = 2.0 * np.concatenate([cos[:, :H], -sin[:, :H]], axis=1)
    last[:, 0] = alternate
    last[:, H] = 0.0
    lowered = [a.astype(ml_dtypes.bfloat16) for a in (columns, ahead, back, cos, sin, last)]
    return np.stack(lowered)


def dot(a, b):
    return jnp.dot(a, b, preferred_element_type=f32)


def column_stage(x, table):
    mean = jnp.sum(x, axis=1, keepdims=True) * (1.0 / N)
    low = x - mean
    energy = jnp.sum(low * low, axis=1, keepdims=True)
    return dot(low.astype(bf16), table).astype(bf16), mean, energy


def side_rows(means, energies):
    lane = lax.broadcasted_iota(jnp.int32, (COLS, H), 1)
    block = jnp.zeros((COLS, H), f32)
    for at, value in enumerate(means + energies):
        block = jnp.where(lane == at, value, block)
    block = jnp.concatenate([block, jnp.zeros((N - COLS, H), f32)], axis=0)
    return jnp.transpose(block)[:8]


def windows(own, left, right, at):
    row = lax.broadcasted_iota(jnp.int32, (8, N), 0)
    lane = lax.broadcasted_iota(jnp.int32, (8, N), 1)
    patch = row % PC
    begin = patch * STRIDE + (N - HALO)
    from_left = (patch < PC - 1) & (lane >= begin)
    from_right = (lane >= COLS) | ((patch == PC - 1) & (lane < begin - N))

    def spread(side):
        return jnp.where(row < PC, side[at : at + 1], side[at + 1 : at + 2])

    return jnp.where(from_left, spread(left), jnp.where(from_right, spread(right), spread(own)))


def centre(own, left, right):
    means = windows(own, left, right, 0)
    means = means - jnp.sum(means, axis=1, keepdims=True) * (1.0 / N)
    energies = windows(own, left, right, 2) + N * means * means
    return N * means, jnp.sum(energies, axis=1, keepdims=True)


def mixed(upper, lower, split):
    row = lax.broadcasted_iota(jnp.int32, upper.shape, 0)
    return jnp.where(row < split, upper.astype(f32), lower.astype(f32)).astype(bf16)


def patch_of(j, level, own, left, right):
    if j == 0:
        parts = [
            own[level, 0:144],
            mixed(own[level, 144:160], left[level, 0:16], 4),
            left[level, 16:112],
        ]
    elif j == 1:
        parts = [
            own[level, 0:160],
            right[level, 0:16],
            mixed(right[level, 16:32], left[level, 32:48], 12),
            left[level, 48:112],
        ]
    elif j == 2:
        parts = [
            own[level, 0:160],
            right[level, 0:64],
            mixed(right[level, 64:80], left[level, 80:96], 4),
            left[level, 96:112],
        ]
    else:
        parts = [
            mixed(right[level, 96:112], own[level, 0:16], 12),
            own[level, 16:160],
            right[level, 0:96],
        ]
    return jnp.concatenate(parts, axis=0)


def cross(now, prev, out):
    step = 16
    for begin in range(0, H, step):
        even, odd = pl.ds(begin, step), pl.ds(H + begin, step)
        a_er, a_ei, a_oi, a_or = now[even, :H], now[even, H:], now[odd, :H], now[odd, H:]
        b_er, b_ei, b_oi, b_or = prev[even, :H], prev[even, H:], prev[odd, :H], prev[odd, H:]
        ee_r = a_er * b_er + a_ei * b_ei
        ee_i = a_ei * b_er - a_er * b_ei
        oo_r = a_or * b_or + a_oi * b_oi
        oo_i = a_or * b_oi - a_oi * b_or
        odd_r = (a_er * b_or - a_ei * b_oi) + (a_or * b_er - a_oi * b_ei)
        minus_i = (a_oi * b_er + a_or * b_ei) - (a_ei * b_or + a_er * b_oi)
        if begin == 0:
            first = lax.broadcasted_iota(jnp.int32, (step, H), 0) == 0
            even_r = jnp.where(first, ee_r, ee_r + oo_r)
            even_i = jnp.where(first, ee_i, ee_i + oo_i)
            minus_i = jnp.where(first, oo_r, minus_i)
            odd_r = jnp.where(first, oo_i, odd_r)
        else:
            even_r, even_i = ee_r + oo_r, ee_i + oo_i
        out[even, :H] = even_r.astype(bf16)
        out[even, H:] = even_i.astype(bf16)
        out[odd, :H] = minus_i.astype(bf16)
        out[odd, H:] = odd_r.astype(bf16)


def first_kernel(
    n_sec,
    n_tile,
    x_hbm,
    prior_hbm,
    table_hbm,
    held,
    rows_out,
    table,
    spec_later,
    b_own,
    b_left,
    b_right,
    x,
    prior,
    a_own,
    a_left,
    a_right,
    side,
    side_out,
    side_in,
    b_side,
    spec_a,
    spec_last,
    spec_b,
    crossed,
    turned,
    rows,
    load_sem,
    send_sem,
    recv_sem,
    ready_sem,
):
    s, t = lax.axis_index("sec"), lax.axis_index("tile")
    has_left, has_right = t > 0, t < n_tile - 1
    has_next, has_prev = s < n_sec - 1, s > 0
    middle = n_tile // 2
    at_middle, before_middle = t == middle, t == middle - 1
    elsewhere = jnp.logical_not(at_middle)
    direct_out = (t == middle - 1) & (s % 2 == 1) & has_next
    direct_in = (t == middle) & (s % 2 == 0) & has_prev
    direct_past = (t == middle) & (s % 2 == 1) & has_next
    step = t % middle
    early, late = at_middle & (s != n_sec // 2), at_middle & (s == n_sec // 2)
    far, far_next = s == n_sec // 2 - 1, s == n_sec // 2
    back_out = far & (step >= 1) & (step <= middle // 2)
    back_in = far_next & (step < middle // 2)
    back_past = far & (step < middle // 2)
    late_out, late_in = far & (t == middle - 1), far_next & (t == middle - 1)
    to_left, to_right, to_next = {"tile": t - 1}, {"tile": t + 1}, {"sec": s + 1}

    def load(source, target, at):
        return pltpu.make_async_copy(source, target, load_sem.at[at])

    load_x = [load(x_hbm.at[i], x.at[i], i) for i in range(LEVELS)]
    load_first = load(table_hbm.at[0], table.at[0], 2)
    load_rest = load(table_hbm.at[1:6], table.at[1:6], 3)
    load_prior = load(prior_hbm, prior, 4)
    load_first.start()
    for copy in load_x:
        copy.start()
    load_rest.start()

    barrier = pltpu.get_barrier_semaphore()

    def greet(there, device):
        @pl.when(there)
        def _():
            pl.semaphore_signal(barrier, inc=1, device_id=device, device_id_type=MESH)

    greet(has_left, to_left)
    greet(has_right & jnp.logical_not(before_middle), to_right)
    greet(has_prev & jnp.logical_not(late_in), {"sec": s - 1})
    greet(late_out, to_next)
    greet(back_in, {"sec": s - 1, "tile": t + 1})
    greet(direct_in, {"sec": s - 1, "tile": t - 1})

    @pl.when(s == 0)
    def _():
        load_prior.start()

    started = []
    count = [0]

    def remote(source, target, device, arrival):
        at = count[0]
        count[0] += 1
        return pltpu.make_async_remote_copy(
            src_ref=source,
            dst_ref=target,
            send_sem=send_sem.at[at],
            recv_sem=recv_sem.at[arrival],
            device_id=device,
            device_id_type=MESH,
        )

    def send(there, *what):
        copy = remote(*what)
        pl.when(there)(copy.start)
        started.append((there, copy))

    def arrived(there, target, arrival):
        copy = pltpu.make_async_remote_copy(
            src_ref=target,
            dst_ref=target,
            send_sem=send_sem.at[0],
            recv_sem=recv_sem.at[arrival],
            device_id=to_next,
            device_id_type=MESH,
        )
        if there is None:
            copy.wait_recv()
        else:
            pl.when(there)(copy.wait_recv)

    @pl.when(jnp.logical_not(has_left))
    def _():
        a_left[...] = jnp.zeros_like(a_left)
        b_left[...] = jnp.zeros_like(b_left)
        side_in[0] = jnp.zeros((8, N), f32)
        b_side[1] = jnp.zeros((8, N), f32)

    @pl.when(jnp.logical_not(has_right))
    def _():
        a_right[...] = jnp.zeros_like(a_right)
        b_right[...] = jnp.zeros_like(b_right)
        side_in[1] = jnp.zeros((8, N), f32)
        b_side[2] = jnp.zeros((8, N), f32)

    low, high = pl.ds(0, EDGE), pl.ds(COLS - EDGE, EDGE)
    to_direct, to_back = {"sec": s + 1, "tile": t + 1}, {"sec": s + 1, "tile": t - 1}

    lefts, left_copies = [], {}

    def send_left(what, when):
        source, target, arrival = what
        if arrival not in left_copies:
            left_copies[arrival] = remote(source, target, to_left, arrival)
            started.append((has_left, left_copies[arrival]))
        pl.when(when & has_left)(left_copies[arrival].start)

    def send_columns(i):
        send(has_right, a_own.at[i, high], a_left.at[i], to_right, i)
        send(direct_out, a_own.at[i, high], b_left.at[i], to_direct, 6 + i)
        lefts.append((a_own.at[i, low], a_right.at[i], 2 + i))
        send_left(lefts[-1], elsewhere)
        send(back_out, a_own.at[i, low], b_right.at[i], to_back, 8 + i)

    load_first.wait()
    stats = []
    for i in range(LEVELS):
        load_x[i].wait()
        a_own[i], *stat = column_stage(x[i], table[0])
        stats.append(stat)
        if i == 0:
            known = [has_left & elsewhere, has_right, has_next & jnp.logical_not(late_out)]
            known += [direct_out, back_out, late_in]
            pl.semaphore_wait(barrier, sum(v.astype(jnp.int32) for v in known))

            @pl.when(before_middle)
            def _():
                pl.semaphore_signal(
                    ready_sem.at[1], inc=1, device_id=to_right, device_id_type=MESH
                )

            @pl.when(late_in)
            def _():
                pl.semaphore_signal(
                    ready_sem.at[0], inc=1, device_id={"sec": s - 1}, device_id_type=MESH
                )

            send_columns(i)
    side[...] = side_rows(*zip(*stats))

    side_out[0] = pltpu.roll(side[...], N - COLS, 1)
    side_out[1] = pltpu.roll(side[...], COLS, 1)
    send(has_right, side_out.at[0], side_in.at[0], to_right, 10)
    send(direct_out, side_out.at[0], b_side.at[1], to_direct, 13)
    lefts.append((side_out.at[1], side_in.at[1], 11))
    send_left(lefts[-1], elsewhere)
    send(back_out, side_out.at[1], b_side.at[2], to_back, 14)
    send_columns(LEVELS - 1)

    @pl.when(late_out)
    def _():
        pl.semaphore_wait(ready_sem.at[0], 1)

    for i in range(LEVELS):
        send(has_next, a_own.at[i], b_own.at[i], to_next, 4 + i)
    send(has_next, side, b_side.at[0], to_next, 12)

    @pl.when(at_middle)
    def _():
        pl.semaphore_wait(ready_sem.at[1], 1)

    for what in lefts:
        send_left(what, at_middle)

    @pl.when(s == 0)
    def _():
        load_prior.wait()
        prior_stats = []
        for i in range(LEVELS):
            b_own[i], *stat = column_stage(prior[i], table[0])
            prior_stats.append(stat)
        prior_side = side_rows(*zip(*prior_stats))
        b_side[0] = prior_side
        side_out[2] = pltpu.roll(prior_side, N - COLS, 1)
        side_out[3] = pltpu.roll(prior_side, COLS, 1)

    first_right, first_left = (s == 0) & has_right, (s == 0) & has_left
    send(first_right, side_out.at[2], b_side.at[1], to_right, 13)
    send(first_left, side_out.at[3], b_side.at[2], to_left, 14)
    for i in range(LEVELS):
        send(first_right, b_own.at[i, high], b_left.at[i], to_right, 6 + i)
        send(first_left, b_own.at[i, low], b_right.at[i], to_left, 8 + i)

    left_on = has_next & has_left & jnp.logical_not(direct_past)
    right_on = has_next & has_right & jnp.logical_not(back_past)

    passed = {}

    def pass_on(when, there, on, source, arrival, target, further):
        arrived(when & there, source, arrival)
        if arrival not in passed:
            passed[arrival] = remote(source, target, to_next, further)
            started.append((on, passed[arrival]))
        pl.when(when & on)(passed[arrival].start)

    def pass_left(i):
        pass_on(True, has_left, left_on, a_left.at[i], i, b_left.at[i], 6 + i)

    def pass_right(when, i):
        pass_on(when, has_right, right_on, a_right.at[i], 2 + i, b_right.at[i], 8 + i)

    def pass_right_side(when):
        pass_on(when, has_right, right_on, side_in.at[1], 11, b_side.at[2], 14)

    def begin_spectra():
        for j in range(PC - 1):
            spec_a[j] = dot(table[1], patch_of(j, 0, a_own, a_left, a_right))

    def previous_right(i):
        arrived(has_prev, b_own.at[i], 4 + i)
        arrived(has_right, b_right.at[i], 8 + i)

    def last_patches(*levels):
        for i in levels:
            spec_last[i] = dot(table[1], patch_of(PC - 1, i, a_own, a_left, a_right))
            spec_b[PC - 1 + i] = dot(table[1], patch_of(PC - 1, i, b_own, b_left, b_right))
        for i in levels:
            cross(spec_last.at[i], spec_b.at[PC - 1 + i], crossed.at[PC - 1 + i])
        for i in levels:
            turned[PC - 1 + i] = dot(table[2], crossed[PC - 1 + i]).astype(bf16)

    upper = step >= middle // 2
    load_rest.wait()
    pass_right(at_middle, 0)
    pass_right(at_middle, 1)
    pass_right_side(at_middle)

    @pl.when(early)
    def _():
        previous_right(0)
        previous_right(1)
        last_patches(0, 1)

    pass_left(0)
    pass_right(upper, 0)
    pl.when(at_middle)(begin_spectra)
    pass_on(True, has_left, left_on, side_in.at[0], 10, b_side.at[1], 13)
    pass_right_side(upper)
    pass_left(1)
    pass_right(elsewhere & jnp.logical_not(upper), 0)
    pass_right(elsewhere, 1)
    pass_right_side(elsewhere & jnp.logical_not(upper))
    pl.when(elsewhere)(begin_spectra)

    @pl.when(late)
    def _():
        previous_right(0)
        previous_right(1)
        last_patches(0, 1)

    pl.when(elsewhere)(lambda: previous_right(0))
    arrived(has_prev, b_side.at[0], 12)
    arrived(has_right, b_side.at[2], 14)
    arrived(has_left, b_side.at[1], 13)
    arrived(has_left, b_left.at[0], 6)
    for j in range(PC - 1):
        spec_b[j] = dot(table[1], patch_of(j, 0, b_own, b_left, b_right))
    for j in range(PC - 1):
        spec_later[j] = dot(table[1], patch_of(j, 1, a_own, a_left, a_right))
    a_flat, a_energy = centre(side[...], side_in[0], side_in[1])
    b_flat, b_energy = centre(b_side[0], b_side[1], b_side[2])
    pair = jnp.concatenate([a_flat, b_flat], axis=0).astype(bf16)
    even_part, odd_part = dot(pair, table[3]), dot(pair, table[4])
    a_e, b_e, a_o, b_o = even_part[:8], even_part[8:], odd_part[:8], odd_part[8:]
    both = jnp.concatenate([a_e * b_e + a_o * b_o, a_e * b_o - a_o * b_e], axis=0).astype(bf16)
    flat = dot(both, table[3])[:8] - dot(both, table[4])[8:]
    scale = 1.0 / (N * jnp.sqrt(a_energy + EPS) * jnp.sqrt(b_energy + EPS))
    rows[0:8] = flat * scale
    rows[8:16] = jnp.broadcast_to(scale, (8, N))
    for j in range(PC - 1):
        cross(spec_a.at[j], spec_b.at[j], crossed.at[j])
    for j in range(PC - 1):
        turned[j] = dot(table[2], crossed[j]).astype(bf16)

    @pl.when(elsewhere)
    def _():
        previous_right(1)
        last_patches(0, 1)

    for p in range(PC + 1):
        held[p] = finished(turned[p], table, rows, p if p < PC else 2 * PC - 1)
    rows_out[...] = rows[...]
    for there, copy in started:
        if copy is not passed[LEVELS - 1]:
            pl.when(there)(copy.wait_send)
    arrived(has_left, b_left.at[1], 7)
    pl.when(left_on)(passed[LEVELS - 1].wait_send)


def finished(turned, table, rows, p):
    product = lax.dot_general(
        table[5], turned, (((1,), (1,)), ((), ())), preferred_element_type=f32
    )
    return product * rows[8 + p : 9 + p] + rows[p : p + 1]


def last_kernel(
    held, rows, table, spec_a, b_own, b_left, b_right, out_hbm, spec_b, crossed, turned, maps, sem
):
    copies = []

    def write(source, p):
        copy = pltpu.make_async_copy(source, out_hbm.at[p], sem.at[p])
        copy.start()
        copies.append(copy)

    for p in range(PC + 1):
        write(held.at[p], p if p < PC else 2 * PC - 1)
    for j in range(PC - 1):
        spec_b[j] = dot(table[1], patch_of(j, 1, b_own, b_left, b_right))
    for j in range(PC - 1):
        cross(spec_a.at[j], spec_b.at[j], crossed.at[j])
        turned[j] = dot(table[2], crossed[j]).astype(bf16)
    for j in range(PC - 1):
        maps[j] = finished(turned[j], table, rows, PC + j)
        write(maps.at[j], PC + j)
    for copy in copies:
        copy.wait()


def local(n_sec, n_tile, sections, prior):
    x = jnp.swapaxes(sections[0], 1, 2)
    before = jnp.swapaxes(prior, 1, 2)
    hbm = pl.BlockSpec(memory_space=pltpu.HBM)
    vmem = pl.BlockSpec(memory_space=pltpu.VMEM)
    patches = LEVELS * PC
    columns = lambda rows: pltpu.VMEM((LEVELS, rows, N), bf16)
    held = lambda *shape: jax.ShapeDtypeStruct(shape, bf16)
    operands = (x, before, jnp.asarray(tables()))
    results = pl.pallas_call(
        functools.partial(first_kernel, n_sec, n_tile),
        out_shape=(
            jax.ShapeDtypeStruct((PC + 1, N, N), f32),
            jax.ShapeDtypeStruct((16, N), f32),
            held(6, N, N),
            jax.ShapeDtypeStruct((PC - 1, N, N), f32),
            held(LEVELS, COLS, N),
            held(LEVELS, EDGE, N),
            held(LEVELS, EDGE, N),
        ),
        in_specs=[hbm] * 3,
        out_specs=(vmem,) * 7,
        scratch_shapes=[
            pltpu.VMEM((LEVELS, COLS, N), f32),
            pltpu.VMEM((LEVELS, COLS, N), f32),
            columns(COLS),
            columns(EDGE),
            columns(EDGE),
            pltpu.VMEM((8, N), f32),
            pltpu.VMEM((4, 8, N), f32),
            pltpu.VMEM((2, 8, N), f32),
            pltpu.VMEM((3, 8, N), f32),
            pltpu.VMEM((PC - 1, N, N), f32),
            pltpu.VMEM((LEVELS, N, N), f32),
            pltpu.VMEM((PC + 1, N, N), f32),
            pltpu.VMEM((PC + 1, N, N), bf16),
            pltpu.VMEM((PC + 1, N, N), bf16),
            pltpu.VMEM((16, N), f32),
            pltpu.SemaphoreType.DMA((5,)),
            pltpu.SemaphoreType.DMA((30,)),
            pltpu.SemaphoreType.DMA((15,)),
            pltpu.SemaphoreType.REGULAR((2,)),
        ],
        compiler_params=pltpu.CompilerParams(
            collective_id=0, has_side_effects=True, vmem_limit_bytes=16 * 2**20
        ),
        name="spectra",
    )(*(pltpu.with_memory_space_constraint(v, pltpu.HBM) for v in operands))
    maps = pl.pallas_call(
        last_kernel,
        out_shape=jax.ShapeDtypeStruct((patches, N, N), f32),
        in_specs=[vmem] * 7,
        out_specs=hbm,
        scratch_shapes=[
            pltpu.VMEM((PC - 1, N, N), f32),
            pltpu.VMEM((PC - 1, N, N), bf16),
            pltpu.VMEM((PC - 1, N, N), bf16),
            pltpu.VMEM((PC - 1, N, N), f32),
            pltpu.SemaphoreType.DMA((patches,)),
        ],
        compiler_params=pltpu.CompilerParams(vmem_limit_bytes=16 * 2**20),
        name="maps",
    )(*results)
    return maps.reshape(1, LEVELS, 1, PC, N, N)


def solution(mesh):
    return jax.shard_map(
        functools.partial(local, mesh.shape["sec"], mesh.shape["tile"]),
        mesh=mesh,
        in_specs=(P("sec", None, None, "tile"), P(None, None, "tile")),
        out_specs=P("sec", None, None, "tile", None, None),
        check_vma=False,
    )
```

```python
import functools

import jax
import jax.numpy as jnp
import ml_dtypes
import numpy as np
from jax import lax
from jax.experimental import pallas as pl
from jax.experimental.pallas import tpu as pltpu
from jax.sharding import PartitionSpec as P

N = 256
H = 128
STRIDE = 40
PC = 4
HALO = 108
LEVELS = 2
COLS = 160
EDGE = 112
EPS = 1e-06
MESH = pl.DeviceIdType.MESH
f32, bf16 = jnp.float32, jnp.bfloat16


def tables():
    i = np.arange(N)
    product = i[:, None] * i[None, :] % N
    cos = np.cos(product * (2.0 * np.pi / N))
    sin = np.sin(product * (2.0 * np.pi / N))
    alternate = cos[:, H]
    columns = np.concatenate([cos[:, :H], -sin[:, :H]], axis=1)
    columns[:, 0] = 0.0
    columns[:, H] = alternate
    ahead = np.concatenate([cos[:H], sin[:H]], axis=0)
    ahead[H] = alternate
    back = 2.0 * np.concatenate([cos[:, :H], sin[:, :H]], axis=1)
    back[:, 0] = 1.0
    back[:, H] = alternate
    last = 2.0 * np.concatenate([cos[:, :H], -sin[:, :H]], axis=1)
    last[:, 0] = alternate
    last[:, H] = 0.0
    lowered = [a.astype(ml_dtypes.bfloat16) for a in (columns, ahead, back, cos, sin, last)]
    return np.stack(lowered)


def dot(a, b):
    return jnp.dot(a, b, preferred_element_type=f32)


def column_stats(x):
    mean = jnp.sum(x, axis=1, keepdims=True) * (1.0 / N)
    low = x - mean
    return low.astype(bf16), mean, jnp.sum(low * low, axis=1, keepdims=True)


def side_rows(means, energies):
    lane = lax.broadcasted_iota(jnp.int32, (COLS, H), 1)
    block = jnp.zeros((COLS, H), f32)
    for at, value in enumerate(means + energies):
        block = jnp.where(lane == at, value, block)
    block = jnp.concatenate([block, jnp.zeros((N - COLS, H), f32)], axis=0)
    return jnp.transpose(block)[:8]


def windows(own, left, right, at):
    row = lax.broadcasted_iota(jnp.int32, (8, N), 0)
    lane = lax.broadcasted_iota(jnp.int32, (8, N), 1)
    patch = row % PC
    begin = patch * STRIDE + (N - HALO)
    from_left = (patch < PC - 1) & (lane >= begin)
    from_right = (lane >= COLS) | ((patch == PC - 1) & (lane < begin - N))

    def spread(side):
        return jnp.where(row < PC, side[at : at + 1], side[at + 1 : at + 2])

    return jnp.where(from_left, spread(left), jnp.where(from_right, spread(right), spread(own)))


def centre(own, left, right):
    means = windows(own, left, right, 0)
    means = means - jnp.sum(means, axis=1, keepdims=True) * (1.0 / N)
    energies = windows(own, left, right, 2) + N * means * means
    return N * means, jnp.sum(energies, axis=1, keepdims=True)


def mixed(upper, lower, split):
    row = lax.broadcasted_iota(jnp.int32, upper.shape, 0)
    return jnp.where(row < split, upper.astype(f32), lower.astype(f32)).astype(bf16)


def patch_of(j, level, own, left, right):
    if j == 0:
        parts = [
            own[level, 0:144],
            mixed(own[level, 144:160], left[level, 0:16], 4),
            left[level, 16:112],
        ]
    elif j == 1:
        parts = [
            own[level, 0:160],
            right[level, 0:16],
            mixed(right[level, 16:32], left[level, 32:48], 12),
            left[level, 48:112],
        ]
    elif j == 2:
        parts = [
            own[level, 0:160],
            right[level, 0:64],
            mixed(right[level, 64:80], left[level, 80:96], 4),
            left[level, 96:112],
        ]
    else:
        parts = [
            mixed(right[level, 96:112], own[level, 0:16], 12),
            own[level, 16:160],
            right[level, 0:96],
        ]
    return jnp.concatenate(parts, axis=0)


def cross(now, prev, out):
    step = 16
    for begin in range(0, H, step):
        even, odd = pl.ds(begin, step), pl.ds(H + begin, step)
        a_er, a_ei, a_oi, a_or = now[even, :H], now[even, H:], now[odd, :H], now[odd, H:]
        b_er, b_ei, b_oi, b_or = prev[even, :H], prev[even, H:], prev[odd, :H], prev[odd, H:]
        ee_r = a_er * b_er + a_ei * b_ei
        ee_i = a_ei * b_er - a_er * b_ei
        oo_r = a_or * b_or + a_oi * b_oi
        oo_i = a_or * b_oi - a_oi * b_or
        odd_r = (a_er * b_or - a_ei * b_oi) + (a_or * b_er - a_oi * b_ei)
        minus_i = (a_oi * b_er + a_or * b_ei) - (a_ei * b_or + a_er * b_oi)
        if begin == 0:
            first = lax.broadcasted_iota(jnp.int32, (step, H), 0) == 0
            even_r = jnp.where(first, ee_r, ee_r + oo_r)
            even_i = jnp.where(first, ee_i, ee_i + oo_i)
            minus_i = jnp.where(first, oo_r, minus_i)
            odd_r = jnp.where(first, oo_i, odd_r)
        else:
            even_r, even_i = ee_r + oo_r, ee_i + oo_i
        out[even, :H] = even_r.astype(bf16)
        out[even, H:] = even_i.astype(bf16)
        out[odd, :H] = minus_i.astype(bf16)
        out[odd, H:] = odd_r.astype(bf16)


def first_kernel(
    n_sec,
    n_tile,
    x_hbm,
    prior_hbm,
    table_hbm,
    held,
    turned_out,
    rows_out,
    table,
    spec_later,
    b_own,
    b_left,
    b_right,
    x,
    prior,
    a_own,
    a_left,
    a_right,
    side,
    side_out,
    side_in,
    b_side,
    r_own,
    r_side,
    spec_a,
    spec_last,
    spec_b,
    crossed,
    turned,
    rows,
    load_sem,
    send_sem,
    recv_sem,
    ready_sem,
):
    s, t = lax.axis_index("sec"), lax.axis_index("tile")
    has_left, has_right = t > 0, t < n_tile - 1
    has_next, has_prev = s < n_sec - 1, s > 0
    middle = n_tile // 2
    at_middle, before_middle = t == middle, t == middle - 1
    elsewhere = jnp.logical_not(at_middle)
    crossing = (s % 2 == 1) & has_next
    left_past = at_middle & crossing
    step = t % middle
    early = at_middle & (s != n_sec // 2)
    not_early = jnp.logical_not(early)
    far, far_next = s == n_sec // 2 - 1, s == n_sec // 2
    back_out = far & (step >= 1) & (step <= middle // 2)
    back_in = far_next & (step < middle // 2)
    back_past = far & (step < middle // 2)
    late_out, late_in = far & before_middle, far_next & before_middle
    relay_out, relay_in = crossing & before_middle, crossing & (t == n_tile - 1)
    edge_out, edge_in = relay_out & jnp.logical_not(far), relay_in & jnp.logical_not(far)
    tile_out, tile_in = relay_out & far, relay_in & far
    not_tile_out = jnp.logical_not(tile_out)
    first_patches = at_middle & (s % 2 == 0) & has_prev
    to_left, to_right, to_next = {"tile": t - 1}, {"tile": t + 1}, {"sec": s + 1}

    def load(source, target, at):
        return pltpu.make_async_copy(source, target, load_sem.at[at])

    load_x = [load(x_hbm.at[i], x.at[i], i) for i in range(LEVELS)]
    load_first = load(table_hbm.at[0], table.at[0], 2)
    load_rest = load(table_hbm.at[1:6], table.at[1:6], 3)
    load_prior = load(prior_hbm, prior, 4)
    load_x[0].start()
    load_x[1].start()
    load_first.start()
    load_rest.start()

    barrier = pltpu.get_barrier_semaphore()

    def greet(there, device):
        @pl.when(there)
        def _():
            pl.semaphore_signal(barrier, inc=1, device_id=device, device_id_type=MESH)

    greet(has_left, to_left)
    greet(has_right & jnp.logical_not(before_middle), to_right)
    greet(has_prev & jnp.logical_not(late_in), {"sec": s - 1})
    greet(late_out, to_next)
    greet(back_in, {"sec": s - 1, "tile": t + 1})
    greet(first_patches & far_next, {"sec": s - 1, "tile": t - 1})
    greet(relay_in, {"tile": middle - 1})
    relayed = (first_patches & jnp.logical_not(far_next)) | late_in
    greet(relayed, {"sec": s - 1, "tile": n_tile - 1})

    @pl.when(s == 0)
    def _():
        load_prior.start()

    started = {}
    count = [0]

    def note(there, copy):
        started.setdefault(id(there), (there, []))[1].append(copy)

    def settle(groups):
        for there, copies in list(groups.values()):

            @pl.when(there)
            def _(copies=copies):
                for copy in copies:
                    copy.wait_send()

        groups.clear()

    def remote(source, target, device, arrival):
        at = count[0]
        count[0] += 1
        return pltpu.make_async_remote_copy(
            src_ref=source,
            dst_ref=target,
            send_sem=send_sem.at[at],
            recv_sem=recv_sem.at[arrival],
            device_id=device,
            device_id_type=MESH,
        )

    def send(there, *what):
        copy = remote(*what)
        pl.when(there)(copy.start)
        note(there, copy)

    def arrived(there, target, arrival):
        copy = pltpu.make_async_remote_copy(
            src_ref=target,
            dst_ref=target,
            send_sem=send_sem.at[0],
            recv_sem=recv_sem.at[arrival],
            device_id=to_next,
            device_id_type=MESH,
        )
        if there is None:
            copy.wait_recv()
        else:
            pl.when(there)(copy.wait_recv)

    @pl.when(jnp.logical_not(has_left))
    def _():
        a_left[...] = jnp.zeros_like(a_left)
        b_left[...] = jnp.zeros_like(b_left)
        side_in[0] = jnp.zeros((8, N), f32)
        b_side[1] = jnp.zeros((8, N), f32)

    @pl.when(jnp.logical_not(has_right))
    def _():
        a_right[...] = jnp.zeros_like(a_right)
        b_right[...] = jnp.zeros_like(b_right)
        side_in[1] = jnp.zeros((8, N), f32)
        b_side[2] = jnp.zeros((8, N), f32)

    low, high = pl.ds(0, EDGE), pl.ds(COLS - EDGE, EDGE)
    to_direct, to_back = {"sec": s + 1, "tile": t + 1}, {"sec": s + 1, "tile": t - 1}
    to_last, to_middle = {"tile": n_tile - 1}, {"sec": s + 1, "tile": middle}
    to_before = {"sec": s + 1, "tile": middle - 1}

    def prepare(there, *what):
        copy = remote(*what)
        note(there, copy)
        return lambda when: pl.when(when & there)(copy.start)

    def columns_to(i):
        right = prepare(has_right, a_own.at[i, high], a_left.at[i], to_right, i)
        left = prepare(has_left, a_own.at[i, low], a_right.at[i], to_left, 2 + i)
        return right, left

    def send_columns(i):
        send(tile_out, a_own.at[i, high], b_left.at[i], to_direct, 6 + i)
        right, left = to_sides[i]
        right(not_tile_out)
        send(edge_out, a_own.at[i, high], r_own.at[i, high], to_last, 15 + i)
        left(elsewhere)
        send(back_out, a_own.at[i, low], b_right.at[i], to_back, 8 + i)

    to_sides = [columns_to(i) for i in range(LEVELS)]
    lowered, stats = [], []
    for i in range(LEVELS):
        load_x[i].wait()
        low_i, *stat = column_stats(x[i])
        lowered.append(low_i)
        stats.append(stat)
    own_side = side_rows(*zip(*stats))
    side[...] = own_side
    side_out[0] = pltpu.roll(own_side, N - COLS, 1)
    side_out[1] = pltpu.roll(own_side, COLS, 1)
    load_first.wait()
    a_own[0] = dot(lowered[0], table[0]).astype(bf16)

    known = [has_left & elsewhere, has_right, has_next & jnp.logical_not(late_out)]
    known += [relay_out, tile_out, relay_in, back_out, late_in]
    pl.semaphore_wait(barrier, sum(v.astype(jnp.int32) for v in known))

    @pl.when(before_middle)
    def _():
        pl.semaphore_signal(ready_sem.at[1], inc=1, device_id=to_right, device_id_type=MESH)

    @pl.when(late_in)
    def _():
        pl.semaphore_signal(
            ready_sem.at[0], inc=1, device_id={"sec": s - 1}, device_id_type=MESH
        )

    send(has_right, side_out.at[0], side_in.at[0], to_right, 10)
    send(tile_out, side_out.at[0], b_side.at[1], to_direct, 13)
    send(edge_out, side_out.at[0], r_side, to_last, 17)
    side_left = prepare(has_left, side_out.at[1], side_in.at[1], to_left, 11)
    side_left(elsewhere)
    send(back_out, side_out.at[1], b_side.at[2], to_back, 14)
    send_columns(0)
    a_own[1] = dot(lowered[1], table[0]).astype(bf16)
    send_columns(1)
    for right, _ in to_sides:
        right(tile_out)

    for i in range(LEVELS):
        send(tile_out, a_own.at[i], r_own.at[i], to_last, 15 + i)
    send(tile_out, side, r_side, to_last, 17)
    own_on = has_next & not_tile_out

    for i in range(LEVELS):
        send(own_on, a_own.at[i], b_own.at[i], to_next, 4 + i)
    send(own_on, side, b_side.at[0], to_next, 12)

    arrived(relay_in, r_side, 17)
    send(edge_in, r_side, b_side.at[1], to_middle, 13)
    send(tile_in, r_side, b_side.at[0], to_before, 12)
    for i in range(LEVELS):
        arrived(edge_in, r_own.at[i, high], 15 + i)
        send(edge_in, r_own.at[i, high], b_left.at[i], to_middle, 6 + i)
        arrived(tile_in, r_own.at[i], 15 + i)
        send(tile_in, r_own.at[i], b_own.at[i], to_before, 4 + i)

    @pl.when(at_middle)
    def _():
        pl.semaphore_wait(ready_sem.at[1], 1)

    side_left(at_middle)
    for _, left in to_sides:
        left(at_middle)

    @pl.when(s == 0)
    def _():
        load_prior.wait()
        prior_stats = []
        for i in range(LEVELS):
            low_i, *stat = column_stats(prior[i])
            b_own[i] = dot(low_i, table[0]).astype(bf16)
            prior_stats.append(stat)
        prior_side = side_rows(*zip(*prior_stats))
        b_side[0] = prior_side
        side_out[2] = pltpu.roll(prior_side, N - COLS, 1)
        side_out[3] = pltpu.roll(prior_side, COLS, 1)

    first_right, first_left = (s == 0) & has_right, (s == 0) & has_left
    send(first_right, side_out.at[2], b_side.at[1], to_right, 13)
    send(first_left, side_out.at[3], b_side.at[2], to_left, 14)
    for i in range(LEVELS):
        send(first_right, b_own.at[i, high], b_left.at[i], to_right, 6 + i)
        send(first_left, b_own.at[i, low], b_right.at[i], to_left, 8 + i)

    @pl.when(late_out)
    def _():
        pl.semaphore_wait(ready_sem.at[0], 1)

    left_on = has_next & has_left & jnp.logical_not(left_past)
    right_on = has_next & has_right & jnp.logical_not(back_past)

    passed = {}
    last_waits = dict(started)
    started.clear()

    def pass_on(when, there, on, source, arrival, target, further):
        arrived(when & there, source, arrival)
        if arrival not in passed:
            passed[arrival] = remote(source, target, to_next, further)
            if arrival != 1:
                note(on, passed[arrival])
        pl.when(when & on)(passed[arrival].start)

    def pass_left(i):
        pass_on(True, has_left, left_on, a_left.at[i], i, b_left.at[i], 6 + i)

    def pass_right(when, i):
        pass_on(when, has_right, right_on, a_right.at[i], 2 + i, b_right.at[i], 8 + i)

    def pass_right_side(when):
        pass_on(when, has_right, right_on, side_in.at[1], 11, b_side.at[2], 14)

    def begin_spectra():
        for j in range(PC - 1):
            spec_a[j] = dot(table[1], patch_of(j, 0, a_own, a_left, a_right))

    def previous_right(i):
        arrived(has_prev, b_own.at[i], 4 + i)
        arrived(has_right, b_right.at[i], 8 + i)

    def last_patches(*levels):
        for i in levels:
            spec_last[i] = dot(table[1], patch_of(PC - 1, i, a_own, a_left, a_right))
            spec_b[PC - 1 + i] = dot(table[1], patch_of(PC - 1, i, b_own, b_left, b_right))
        for i in levels:
            cross(spec_last.at[i], spec_b.at[PC - 1 + i], crossed.at[PC - 1 + i])
        for i in levels:
            turned[PC - 1 + i] = dot(table[2], crossed[PC - 1 + i]).astype(bf16)

    upper = step >= middle // 2
    load_rest.wait()
    pass_right(at_middle, 0)
    pass_right(at_middle, 1)
    pass_right_side(at_middle)

    @pl.when(early)
    def _():
        previous_right(0)
        previous_right(1)
        last_patches(0, 1)

    pass_on(True, has_left, left_on, side_in.at[0], 10, b_side.at[1], 13)
    pass_right_side(upper)
    pass_left(0)
    pass_right(upper, 0)
    pl.when(at_middle)(begin_spectra)
    pass_left(1)
    pass_right(elsewhere & jnp.logical_not(upper), 0)
    pass_right(elsewhere, 1)
    pass_right_side(elsewhere & jnp.logical_not(upper))
    pl.when(elsewhere)(begin_spectra)

    settle(last_waits)
    arrived(has_prev, b_side.at[0], 12)
    arrived(has_right, b_side.at[2], 14)
    arrived(has_left, b_side.at[1], 13)
    for j in range(PC - 1):
        spec_later[j] = dot(table[1], patch_of(j, 1, a_own, a_left, a_right))
    a_flat, a_energy = centre(side[...], side_in[0], side_in[1])
    b_flat, b_energy = centre(b_side[0], b_side[1], b_side[2])
    pair = jnp.concatenate([a_flat, b_flat], axis=0).astype(bf16)
    even_part, odd_part = dot(pair, table[3]), dot(pair, table[4])
    a_e, b_e, a_o, b_o = even_part[:8], even_part[8:], odd_part[:8], odd_part[8:]
    both = jnp.concatenate([a_e * b_e + a_o * b_o, a_e * b_o - a_o * b_e], axis=0).astype(bf16)
    flat = dot(both, table[3])[:8] - dot(both, table[4])[8:]
    scale = 1.0 / (N * jnp.sqrt(a_energy + EPS) * jnp.sqrt(b_energy + EPS))
    rows[0:8] = flat * scale
    rows[8:16] = jnp.broadcast_to(scale, (8, N))
    rows_out[...] = rows[...]

    pl.when(not_early)(lambda: previous_right(0))
    arrived(has_left, b_left.at[0], 6)
    for j in range(PC - 1):
        spec_b[j] = dot(table[1], patch_of(j, 0, b_own, b_left, b_right))
    for j in range(PC - 1):
        cross(spec_a.at[j], spec_b.at[j], crossed.at[j])
    for j in range(PC - 1):
        turned[j] = dot(table[2], crossed[j]).astype(bf16)
    for j in range(PC - 1):
        held[j] = finished(turned[j], table, rows, j)

    @pl.when(not_early)
    def _():
        previous_right(1)
        last_patches(0, 1)

    for j in range(LEVELS):
        turned_out[j] = turned[PC - 1 + j]
    settle(started)
    arrived(has_left, b_left.at[1], 7)
    pl.when(left_on)(passed[1].wait_send)


def finished(turned, table, rows, p):
    product = lax.dot_general(
        table[5], turned, (((1,), (1,)), ((), ())), preferred_element_type=f32
    )
    return product * rows[8 + p : 9 + p] + rows[p : p + 1]


def last_kernel(
    held, lasts, rows, table, spec_a, b_own, b_left, b_right, out_hbm, spec_b, crossed, turned, maps, sem
):
    copies = []

    def write(source, p):
        copy = pltpu.make_async_copy(source, out_hbm.at[p], sem.at[p])
        copy.start()
        copies.append(copy)

    for j in range(PC - 1):
        write(held.at[j], j)
    for j in range(PC - 1):
        spec_b[j] = dot(table[1], patch_of(j, 1, b_own, b_left, b_right))
    for i in range(LEVELS):
        maps[PC - 1 + i] = finished(lasts[i], table, rows, (i + 1) * PC - 1)
        write(maps.at[PC - 1 + i], (i + 1) * PC - 1)
    for j in range(PC - 1):
        cross(spec_a.at[j], spec_b.at[j], crossed.at[j])
        turned[j] = dot(table[2], crossed[j]).astype(bf16)
    for j in range(PC - 1):
        maps[j] = finished(turned[j], table, rows, PC + j)
        write(maps.at[j], PC + j)
    for copy in copies:
        copy.wait()


def local(n_sec, n_tile, sections, prior):
    x = jnp.swapaxes(sections[0], 1, 2)
    before = jnp.swapaxes(prior, 1, 2)
    hbm = pl.BlockSpec(memory_space=pltpu.HBM)
    vmem = pl.BlockSpec(memory_space=pltpu.VMEM)
    patches = LEVELS * PC
    columns = lambda rows: pltpu.VMEM((LEVELS, rows, N), bf16)
    held = lambda *shape: jax.ShapeDtypeStruct(shape, bf16)
    operands = (x, before, jnp.asarray(tables()))
    results = pl.pallas_call(
        functools.partial(first_kernel, n_sec, n_tile),
        out_shape=(
            jax.ShapeDtypeStruct((PC - 1, N, N), f32),
            held(LEVELS, N, N),
            jax.ShapeDtypeStruct((16, N), f32),
            held(6, N, N),
            jax.ShapeDtypeStruct((PC - 1, N, N), f32),
            held(LEVELS, COLS, N),
            held(LEVELS, EDGE, N),
            held(LEVELS, EDGE, N),
        ),
        in_specs=[hbm] * 3,
        out_specs=(vmem,) * 8,
        scratch_shapes=[
            pltpu.VMEM((LEVELS, COLS, N), f32),
            pltpu.VMEM((LEVELS, COLS, N), f32),
            columns(COLS),
            columns(EDGE),
            columns(EDGE),
            pltpu.VMEM((8, N), f32),
            pltpu.VMEM((4, 8, N), f32),
            pltpu.VMEM((2, 8, N), f32),
            pltpu.VMEM((3, 8, N), f32),
            columns(COLS),
            pltpu.VMEM((8, N), f32),
            pltpu.VMEM((PC - 1, N, N), f32),
            pltpu.VMEM((LEVELS, N, N), f32),
            pltpu.VMEM((PC + 1, N, N), f32),
            pltpu.VMEM((PC + 1, N, N), bf16),
            pltpu.VMEM((PC + 1, N, N), bf16),
            pltpu.VMEM((16, N), f32),
            pltpu.SemaphoreType.DMA((5,)),
            pltpu.SemaphoreType.DMA((44,)),
            pltpu.SemaphoreType.DMA((18,)),
            pltpu.SemaphoreType.REGULAR((2,)),
        ],
        compiler_params=pltpu.CompilerParams(
            collective_id=0, has_side_effects=True, vmem_limit_bytes=16 * 2**20
        ),
        name="spectra",
    )(*(pltpu.with_memory_space_constraint(v, pltpu.HBM) for v in operands))
    maps = pl.pallas_call(
        last_kernel,
        out_shape=jax.ShapeDtypeStruct((patches, N, N), f32),
        in_specs=[vmem] * 8,
        out_specs=hbm,
        scratch_shapes=[
            pltpu.VMEM((PC - 1, N, N), f32),
            pltpu.VMEM((PC - 1, N, N), bf16),
            pltpu.VMEM((PC - 1, N, N), bf16),
            pltpu.VMEM((PC + 1, N, N), f32),
            pltpu.SemaphoreType.DMA((patches,)),
        ],
        compiler_params=pltpu.CompilerParams(vmem_limit_bytes=16 * 2**20),
        name="maps",
    )(*results)
    return maps.reshape(1, LEVELS, 1, PC, N, N)


def solution(mesh):
    return jax.shard_map(
        functools.partial(local, mesh.shape["sec"], mesh.shape["tile"]),
        mesh=mesh,
        in_specs=(P("sec", None, None, "tile"), P(None, None, "tile")),
        out_specs=P("sec", None, None, "tile", None, None),
        check_vma=False,
    )
```

```python
import functools

import jax
import jax.numpy as jnp
import ml_dtypes
import numpy as np
from jax import lax
from jax.experimental import pallas as pl
from jax.experimental.pallas import tpu as pltpu
from jax.sharding import PartitionSpec as P

N = 256
H = 128
STRIDE = 40
PC = 4
HALO = 108
LEVELS = 2
COLS = 160
EDGE = 112
EPS = 1e-06
MESH = pl.DeviceIdType.MESH
f32, bf16 = jnp.float32, jnp.bfloat16


def tables():
    i = np.arange(N)
    product = i[:, None] * i[None, :] % N
    cos = np.cos(product * (2.0 * np.pi / N))
    sin = np.sin(product * (2.0 * np.pi / N))
    alternate = cos[:, H]
    columns = np.concatenate([cos[:, :H], -sin[:, :H]], axis=1)
    columns[:, 0] = 0.0
    columns[:, H] = alternate
    ahead = np.concatenate([cos[:H], sin[:H]], axis=0)
    ahead[H] = alternate
    back = 2.0 * np.concatenate([cos[:, :H], sin[:, :H]], axis=1)
    back[:, 0] = 1.0
    back[:, H] = alternate
    last = 2.0 * np.concatenate([cos[:, :H], -sin[:, :H]], axis=1)
    last[:, 0] = alternate
    last[:, H] = 0.0
    lowered = [a.astype(ml_dtypes.bfloat16) for a in (columns, ahead, back, cos, sin, last)]
    return np.stack(lowered)


def dot(a, b):
    return jnp.dot(a, b, preferred_element_type=f32)


def column_stats(x):
    mean = jnp.sum(x, axis=1, keepdims=True) * (1.0 / N)
    low = x - mean
    return low.astype(bf16), mean, jnp.sum(low * low, axis=1, keepdims=True)


def side_rows(means, energies):
    lane = lax.broadcasted_iota(jnp.int32, (COLS, H), 1)
    block = jnp.zeros((COLS, H), f32)
    for at, value in enumerate(means + energies):
        block = jnp.where(lane == at, value, block)
    block = jnp.concatenate([block, jnp.zeros((N - COLS, H), f32)], axis=0)
    return jnp.transpose(block)[:8]


def windows(own, left, right, at):
    row = lax.broadcasted_iota(jnp.int32, (8, N), 0)
    lane = lax.broadcasted_iota(jnp.int32, (8, N), 1)
    patch = row % PC
    begin = patch * STRIDE + (N - HALO)
    from_left = (patch < PC - 1) & (lane >= begin)
    from_right = (lane >= COLS) | ((patch == PC - 1) & (lane < begin - N))

    def spread(side):
        return jnp.where(row < PC, side[at : at + 1], side[at + 1 : at + 2])

    return jnp.where(from_left, spread(left), jnp.where(from_right, spread(right), spread(own)))


def centre(own, left, right):
    means = windows(own, left, right, 0)
    means = means - jnp.sum(means, axis=1, keepdims=True) * (1.0 / N)
    energies = windows(own, left, right, 2) + N * means * means
    return N * means, jnp.sum(energies, axis=1, keepdims=True)


def mixed(upper, lower, split):
    row = lax.broadcasted_iota(jnp.int32, upper.shape, 0)
    return jnp.where(row < split, upper.astype(f32), lower.astype(f32)).astype(bf16)


def patch_of(j, level, own, left, right):
    if j == 0:
        parts = [
            own[level, 0:144],
            mixed(own[level, 144:160], left[level, 0:16], 4),
            left[level, 16:112],
        ]
    elif j == 1:
        parts = [
            own[level, 0:160],
            right[level, 0:16],
            mixed(right[level, 16:32], left[level, 32:48], 12),
            left[level, 48:112],
        ]
    elif j == 2:
        parts = [
            own[level, 0:160],
            right[level, 0:64],
            mixed(right[level, 64:80], left[level, 80:96], 4),
            left[level, 96:112],
        ]
    else:
        parts = [
            mixed(right[level, 96:112], own[level, 0:16], 12),
            own[level, 16:160],
            right[level, 0:96],
        ]
    return jnp.concatenate(parts, axis=0)


def cross(now, prev, out):
    step = 16
    for begin in range(0, H, step):
        even, odd = pl.ds(begin, step), pl.ds(H + begin, step)
        a_er, a_ei, a_oi, a_or = now[even, :H], now[even, H:], now[odd, :H], now[odd, H:]
        b_er, b_ei, b_oi, b_or = prev[even, :H], prev[even, H:], prev[odd, :H], prev[odd, H:]
        ee_r = a_er * b_er + a_ei * b_ei
        ee_i = a_ei * b_er - a_er * b_ei
        oo_r = a_or * b_or + a_oi * b_oi
        oo_i = a_or * b_oi - a_oi * b_or
        odd_r = (a_er * b_or - a_ei * b_oi) + (a_or * b_er - a_oi * b_ei)
        minus_i = (a_oi * b_er + a_or * b_ei) - (a_ei * b_or + a_er * b_oi)
        if begin == 0:
            first = lax.broadcasted_iota(jnp.int32, (step, H), 0) == 0
            even_r = jnp.where(first, ee_r, ee_r + oo_r)
            even_i = jnp.where(first, ee_i, ee_i + oo_i)
            minus_i = jnp.where(first, oo_r, minus_i)
            odd_r = jnp.where(first, oo_i, odd_r)
        else:
            even_r, even_i = ee_r + oo_r, ee_i + oo_i
        out[even, :H] = even_r.astype(bf16)
        out[even, H:] = even_i.astype(bf16)
        out[odd, :H] = minus_i.astype(bf16)
        out[odd, H:] = odd_r.astype(bf16)


def first_kernel(
    n_sec,
    n_tile,
    x_hbm,
    prior_hbm,
    table_hbm,
    held,
    turned_out,
    rows_out,
    table,
    spec_later,
    b_own,
    b_left,
    b_right,
    x,
    prior,
    a_own,
    a_left,
    a_right,
    side,
    side_out,
    side_in,
    b_side,
    r_own,
    r_side,
    spec_a,
    spec_last,
    spec_b,
    crossed,
    turned,
    rows,
    load_sem,
    send_sem,
    recv_sem,
    ready_sem,
):
    s, t = lax.axis_index("sec"), lax.axis_index("tile")
    has_left, has_right = t > 0, t < n_tile - 1
    has_next, has_prev = s < n_sec - 1, s > 0
    middle = n_tile // 2
    at_middle, before_middle = t == middle, t == middle - 1
    elsewhere = jnp.logical_not(at_middle)
    crossing = (s % 2 == 1) & has_next
    left_past = at_middle & crossing
    step = t % middle
    split, before_split = at_middle & (s != n_sec // 2), before_middle & (s != n_sec // 2)
    joined = jnp.logical_not(split)
    early = at_middle & (s != n_sec // 2)
    not_early = jnp.logical_not(early)
    far, far_next = s == n_sec // 2 - 1, s == n_sec // 2
    back_out = far & (step >= 1) & (step <= middle // 2)
    back_in = far_next & (step < middle // 2)
    back_past = far & ((step < middle // 2) | before_middle)
    late_out, late_in = far & before_middle, far_next & before_middle
    over_out, over_in = far & at_middle, late_in
    relay_out, relay_in = crossing & before_middle, crossing & (t == n_tile - 1)
    edge_out, edge_in = relay_out & jnp.logical_not(far), relay_in & jnp.logical_not(far)
    tile_out, tile_in = relay_out & far, relay_in & far
    not_tile_out = jnp.logical_not(tile_out)
    first_patches = at_middle & (s % 2 == 0) & has_prev
    to_left, to_right, to_next = {"tile": t - 1}, {"tile": t + 1}, {"sec": s + 1}

    def load(source, target, at):
        return pltpu.make_async_copy(source, target, load_sem.at[at])

    load_x = [load(x_hbm.at[i], x.at[i], i) for i in range(LEVELS)]
    load_first = load(table_hbm.at[0], table.at[0], 2)
    load_rest = load(table_hbm.at[1:6], table.at[1:6], 3)
    load_prior = load(prior_hbm, prior, 4)
    load_x[0].start()
    load_x[1].start()
    load_first.start()
    load_rest.start()

    barrier = pltpu.get_barrier_semaphore()

    def greet(there, device):
        @pl.when(there)
        def _():
            pl.semaphore_signal(barrier, inc=1, device_id=device, device_id_type=MESH)

    greet(has_left, to_left)
    greet(has_right & jnp.logical_not(before_split), to_right)
    greet(has_prev & jnp.logical_not(late_in), {"sec": s - 1})
    greet(late_out, to_next)
    greet(back_in, {"sec": s - 1, "tile": t + 1})
    greet(first_patches & far_next, {"sec": s - 1, "tile": t - 1})
    greet(relay_in, {"tile": middle - 1})
    relayed = (first_patches & jnp.logical_not(far_next)) | late_in
    greet(relayed, {"sec": s - 1, "tile": n_tile - 1})
    greet(over_out, {"sec": s + 1, "tile": t - 1})

    @pl.when(s == 0)
    def _():
        load_prior.start()

    started = {}
    count = [0]

    def note(there, copy):
        started.setdefault(id(there), (there, []))[1].append(copy)

    def settle(groups):
        for there, copies in list(groups.values()):

            @pl.when(there)
            def _(copies=copies):
                for copy in copies:
                    copy.wait_send()

        groups.clear()

    def remote(source, target, device, arrival):
        at = count[0]
        count[0] += 1
        return pltpu.make_async_remote_copy(
            src_ref=source,
            dst_ref=target,
            send_sem=send_sem.at[at],
            recv_sem=recv_sem.at[arrival],
            device_id=device,
            device_id_type=MESH,
        )

    def send(there, *what):
        copy = remote(*what)
        pl.when(there)(copy.start)
        note(there, copy)

    def arrived(there, target, arrival):
        copy = pltpu.make_async_remote_copy(
            src_ref=target,
            dst_ref=target,
            send_sem=send_sem.at[0],
            recv_sem=recv_sem.at[arrival],
            device_id=to_next,
            device_id_type=MESH,
        )
        if there is None:
            copy.wait_recv()
        else:
            pl.when(there)(copy.wait_recv)

    @pl.when(jnp.logical_not(has_left))
    def _():
        a_left[...] = jnp.zeros_like(a_left)
        b_left[...] = jnp.zeros_like(b_left)
        side_in[0] = jnp.zeros((8, N), f32)
        b_side[1] = jnp.zeros((8, N), f32)

    @pl.when(jnp.logical_not(has_right))
    def _():
        a_right[...] = jnp.zeros_like(a_right)
        b_right[...] = jnp.zeros_like(b_right)
        side_in[1] = jnp.zeros((8, N), f32)
        b_side[2] = jnp.zeros((8, N), f32)

    low, high = pl.ds(0, EDGE), pl.ds(COLS - EDGE, EDGE)
    to_direct, to_back = {"sec": s + 1, "tile": t + 1}, {"sec": s + 1, "tile": t - 1}
    to_last, to_middle = {"tile": n_tile - 1}, {"sec": s + 1, "tile": middle}
    to_before = {"sec": s + 1, "tile": middle - 1}

    def prepare(there, *what):
        copy = remote(*what)
        note(there, copy)
        return lambda when: pl.when(when & there)(copy.start)

    def columns_to(i):
        right = prepare(has_right, a_own.at[i, high], a_left.at[i], to_right, i)
        left = prepare(has_left, a_own.at[i, low], a_right.at[i], to_left, 2 + i)
        return right, left

    def send_columns(i):
        send(tile_out, a_own.at[i, high], b_left.at[i], to_direct, 6 + i)
        send(tile_out, a_own.at[i], r_own.at[i], to_last, 15 + i)
        right, left = to_sides[i]
        right(not_tile_out)
        send(edge_out, a_own.at[i, high], r_own.at[i, high], to_last, 15 + i)
        left(joined)
        send(back_out, a_own.at[i, low], b_right.at[i], to_back, 8 + i)

    to_sides = [columns_to(i) for i in range(LEVELS)]
    lowered, stats = [], []
    for i in range(LEVELS):
        load_x[i].wait()
        low_i, *stat = column_stats(x[i])
        lowered.append(low_i)
        stats.append(stat)
    own_side = side_rows(*zip(*stats))
    side[...] = own_side
    side_out[0] = pltpu.roll(own_side, N - COLS, 1)
    side_out[1] = pltpu.roll(own_side, COLS, 1)
    load_first.wait()
    a_own[0] = dot(lowered[0], table[0]).astype(bf16)

    known = [has_left & joined, has_right, has_next & jnp.logical_not(late_out)]
    known += [relay_out, tile_out, relay_in, back_out, late_in, over_in]
    pl.semaphore_wait(barrier, sum(v.astype(jnp.int32) for v in known))

    @pl.when(before_split)
    def _():
        pl.semaphore_signal(ready_sem.at[1], inc=1, device_id=to_right, device_id_type=MESH)

    @pl.when(over_in)
    def _():
        pl.semaphore_signal(
            ready_sem.at[2],
            inc=1,
            device_id={"sec": s - 1, "tile": t + 1},
            device_id_type=MESH,
        )

    @pl.when(late_in)
    def _():
        pl.semaphore_signal(
            ready_sem.at[0], inc=1, device_id={"sec": s - 1}, device_id_type=MESH
        )

    send(has_right, side_out.at[0], side_in.at[0], to_right, 10)
    send(tile_out, side_out.at[0], b_side.at[1], to_direct, 13)
    send(edge_out, side_out.at[0], r_side, to_last, 17)
    side_left = prepare(has_left, side_out.at[1], side_in.at[1], to_left, 11)
    side_left(joined)
    send(back_out, side_out.at[1], b_side.at[2], to_back, 14)
    send_columns(0)
    a_own[1] = dot(lowered[1], table[0]).astype(bf16)
    send_columns(1)
    for right, _ in to_sides:
        right(tile_out)

    send(tile_out, side, r_side, to_last, 17)
    own_on = has_next & not_tile_out

    for i in range(LEVELS):
        send(own_on, a_own.at[i], b_own.at[i], to_next, 4 + i)
    send(own_on, side, b_side.at[0], to_next, 12)

    for i in range(LEVELS):
        arrived(edge_in, r_own.at[i, high], 15 + i)
        send(edge_in, r_own.at[i, high], b_left.at[i], to_middle, 6 + i)
        arrived(tile_in, r_own.at[i], 15 + i)
        send(tile_in, r_own.at[i], b_own.at[i], to_before, 4 + i)
        if i == 0:
            arrived(edge_in, r_side, 17)
            send(edge_in, r_side, b_side.at[1], to_middle, 13)
    arrived(tile_in, r_side, 17)
    send(tile_in, r_side, b_side.at[0], to_before, 12)

    @pl.when(split)
    def _():
        pl.semaphore_wait(ready_sem.at[1], 1)

    side_left(split)
    for _, left in to_sides:
        left(split)

    @pl.when(over_out)
    def _():
        pl.semaphore_wait(ready_sem.at[2], 1)

    send(over_out, side_out.at[1], b_side.at[2], to_back, 14)
    for i in range(LEVELS):
        send(over_out, a_own.at[i, low], b_right.at[i], to_back, 8 + i)

    @pl.when(s == 0)
    def _():
        load_prior.wait()
        prior_stats = []
        for i in range(LEVELS):
            low_i, *stat = column_stats(prior[i])
            b_own[i] = dot(low_i, table[0]).astype(bf16)
            prior_stats.append(stat)
        prior_side = side_rows(*zip(*prior_stats))
        b_side[0] = prior_side
        side_out[2] = pltpu.roll(prior_side, N - COLS, 1)
        side_out[3] = pltpu.roll(prior_side, COLS, 1)

    first_right, first_left = (s == 0) & has_right, (s == 0) & has_left
    send(first_right, side_out.at[2], b_side.at[1], to_right, 13)
    send(first_left, side_out.at[3], b_side.at[2], to_left, 14)
    for i in range(LEVELS):
        send(first_right, b_own.at[i, high], b_left.at[i], to_right, 6 + i)
        send(first_left, b_own.at[i, low], b_right.at[i], to_left, 8 + i)

    @pl.when(late_out)
    def _():
        pl.semaphore_wait(ready_sem.at[0], 1)

    left_on = has_next & has_left & jnp.logical_not(left_past)
    right_on = has_next & has_right & jnp.logical_not(back_past)

    passed = {}
    last_waits = dict(started)
    started.clear()

    def pass_on(when, there, on, source, arrival, target, further):
        arrived(when & there, source, arrival)
        if arrival not in passed:
            passed[arrival] = remote(source, target, to_next, further)
            if arrival != 1:
                note(on, passed[arrival])
        pl.when(when & on)(passed[arrival].start)

    def pass_left(i):
        pass_on(True, has_left, left_on, a_left.at[i], i, b_left.at[i], 6 + i)

    def pass_right(when, i):
        pass_on(when, has_right, right_on, a_right.at[i], 2 + i, b_right.at[i], 8 + i)

    def pass_right_side(when):
        pass_on(when, has_right, right_on, side_in.at[1], 11, b_side.at[2], 14)

    def begin_spectra():
        for j in range(PC - 1):
            spec_a[j] = dot(table[1], patch_of(j, 0, a_own, a_left, a_right))

    def previous_right(i):
        arrived(has_prev, b_own.at[i], 4 + i)
        arrived(has_right, b_right.at[i], 8 + i)

    def last_patches(*levels):
        for i in levels:
            spec_last[i] = dot(table[1], patch_of(PC - 1, i, a_own, a_left, a_right))
            spec_b[PC - 1 + i] = dot(table[1], patch_of(PC - 1, i, b_own, b_left, b_right))
        for i in levels:
            cross(spec_last.at[i], spec_b.at[PC - 1 + i], crossed.at[PC - 1 + i])
        for i in levels:
            turned[PC - 1 + i] = dot(table[2], crossed[PC - 1 + i]).astype(bf16)

    upper = (step >= middle // 2) & jnp.logical_not(before_middle)
    load_rest.wait()
    pass_right(at_middle, 0)
    pass_right(at_middle, 1)
    pass_right_side(at_middle)

    @pl.when(early)
    def _():
        previous_right(0)
        previous_right(1)
        last_patches(0, 1)

    pass_on(True, has_left, left_on, side_in.at[0], 10, b_side.at[1], 13)
    pass_right_side(upper)
    pass_left(0)
    pass_right(upper, 0)
    pl.when(at_middle)(begin_spectra)
    pass_left(1)
    pass_right(elsewhere & jnp.logical_not(upper), 0)
    pass_right(elsewhere, 1)
    pass_right_side(elsewhere & jnp.logical_not(upper))
    pl.when(elsewhere)(begin_spectra)

    settle(last_waits)
    arrived(has_prev, b_side.at[0], 12)
    arrived(has_right, b_side.at[2], 14)
    arrived(has_left, b_side.at[1], 13)
    for j in range(PC - 1):
        spec_later[j] = dot(table[1], patch_of(j, 1, a_own, a_left, a_right))
    a_flat, a_energy = centre(side[...], side_in[0], side_in[1])
    b_flat, b_energy = centre(b_side[0], b_side[1], b_side[2])
    pair = jnp.concatenate([a_flat, b_flat], axis=0).astype(bf16)
    even_part, odd_part = dot(pair, table[3]), dot(pair, table[4])
    a_e, b_e, a_o, b_o = even_part[:8], even_part[8:], odd_part[:8], odd_part[8:]
    both = jnp.concatenate([a_e * b_e + a_o * b_o, a_e * b_o - a_o * b_e], axis=0).astype(bf16)
    flat = dot(both, table[3])[:8] - dot(both, table[4])[8:]
    scale = 1.0 / (N * jnp.sqrt(a_energy + EPS) * jnp.sqrt(b_energy + EPS))
    rows[0:8] = flat * scale
    rows[8:16] = jnp.broadcast_to(scale, (8, N))
    rows_out[...] = rows[...]

    pl.when(not_early)(lambda: previous_right(0))
    arrived(has_left, b_left.at[0], 6)
    for j in range(PC - 1):
        spec_b[j] = dot(table[1], patch_of(j, 0, b_own, b_left, b_right))
    for j in range(PC - 1):
        cross(spec_a.at[j], spec_b.at[j], crossed.at[j])
    for j in range(PC - 1):
        turned[j] = dot(table[2], crossed[j]).astype(bf16)
    for j in range(PC - 1):
        held[j] = finished(turned[j], table, rows, j)

    @pl.when(not_early)
    def _():
        previous_right(1)
        last_patches(0, 1)

    for j in range(LEVELS):
        turned_out[j] = turned[PC - 1 + j]
    settle(started)
    arrived(has_left, b_left.at[1], 7)
    pl.when(left_on)(passed[1].wait_send)


def finished(turned, table, rows, p):
    product = lax.dot_general(
        table[5], turned, (((1,), (1,)), ((), ())), preferred_element_type=f32
    )
    return product * rows[8 + p : 9 + p] + rows[p : p + 1]


def last_kernel(
    held, lasts, rows, table, spec_a, b_own, b_left, b_right, out_hbm, spec_b, crossed, turned, maps, sem
):
    copies = []

    def write(source, p):
        copy = pltpu.make_async_copy(source, out_hbm.at[p], sem.at[p])
        copy.start()
        copies.append(copy)

    for j in range(PC - 1):
        write(held.at[j], j)
    for j in range(PC - 1):
        spec_b[j] = dot(table[1], patch_of(j, 1, b_own, b_left, b_right))
    for i in range(LEVELS):
        maps[PC - 1 + i] = finished(lasts[i], table, rows, (i + 1) * PC - 1)
        write(maps.at[PC - 1 + i], (i + 1) * PC - 1)
    for j in range(PC - 1):
        cross(spec_a.at[j], spec_b.at[j], crossed.at[j])
        turned[j] = dot(table[2], crossed[j]).astype(bf16)
    for j in range(PC - 1):
        maps[j] = finished(turned[j], table, rows, PC + j)
        write(maps.at[j], PC + j)
    for copy in copies:
        copy.wait()


def local(n_sec, n_tile, sections, prior):
    x = jnp.swapaxes(sections[0], 1, 2)
    before = jnp.swapaxes(prior, 1, 2)
    hbm = pl.BlockSpec(memory_space=pltpu.HBM)
    vmem = pl.BlockSpec(memory_space=pltpu.VMEM)
    patches = LEVELS * PC
    columns = lambda rows: pltpu.VMEM((LEVELS, rows, N), bf16)
    held = lambda *shape: jax.ShapeDtypeStruct(shape, bf16)
    operands = (x, before, jnp.asarray(tables()))
    results = pl.pallas_call(
        functools.partial(first_kernel, n_sec, n_tile),
        out_shape=(
            jax.ShapeDtypeStruct((PC - 1, N, N), f32),
            held(LEVELS, N, N),
            jax.ShapeDtypeStruct((16, N), f32),
            held(6, N, N),
            jax.ShapeDtypeStruct((PC - 1, N, N), f32),
            held(LEVELS, COLS, N),
            held(LEVELS, EDGE, N),
            held(LEVELS, EDGE, N),
        ),
        in_specs=[hbm] * 3,
        out_specs=(vmem,) * 8,
        scratch_shapes=[
            pltpu.VMEM((LEVELS, COLS, N), f32),
            pltpu.VMEM((LEVELS, COLS, N), f32),
            columns(COLS),
            columns(EDGE),
            columns(EDGE),
            pltpu.VMEM((8, N), f32),
            pltpu.VMEM((4, 8, N), f32),
            pltpu.VMEM((2, 8, N), f32),
            pltpu.VMEM((3, 8, N), f32),
            columns(COLS),
            pltpu.VMEM((8, N), f32),
            pltpu.VMEM((PC - 1, N, N), f32),
            pltpu.VMEM((LEVELS, N, N), f32),
            pltpu.VMEM((PC + 1, N, N), f32),
            pltpu.VMEM((PC + 1, N, N), bf16),
            pltpu.VMEM((PC + 1, N, N), bf16),
            pltpu.VMEM((16, N), f32),
            pltpu.SemaphoreType.DMA((5,)),
            pltpu.SemaphoreType.DMA((47,)),
            pltpu.SemaphoreType.DMA((18,)),
            pltpu.SemaphoreType.REGULAR((3,)),
        ],
        compiler_params=pltpu.CompilerParams(
            collective_id=0, has_side_effects=True, vmem_limit_bytes=16 * 2**20
        ),
        name="spectra",
    )(*(pltpu.with_memory_space_constraint(v, pltpu.HBM) for v in operands))
    maps = pl.pallas_call(
        last_kernel,
        out_shape=jax.ShapeDtypeStruct((patches, N, N), f32),
        in_specs=[vmem] * 8,
        out_specs=hbm,
        scratch_shapes=[
            pltpu.VMEM((PC - 1, N, N), f32),
            pltpu.VMEM((PC - 1, N, N), bf16),
            pltpu.VMEM((PC - 1, N, N), bf16),
            pltpu.VMEM((PC + 1, N, N), f32),
            pltpu.SemaphoreType.DMA((patches,)),
        ],
        compiler_params=pltpu.CompilerParams(vmem_limit_bytes=16 * 2**20),
        name="maps",
    )(*results)
    return maps.reshape(1, LEVELS, 1, PC, N, N)


def solution(mesh):
    return jax.shard_map(
        functools.partial(local, mesh.shape["sec"], mesh.shape["tile"]),
        mesh=mesh,
        in_specs=(P("sec", None, None, "tile"), P(None, None, "tile")),
        out_specs=P("sec", None, None, "tile", None, None),
        check_vma=False,
    )
```

```python
import functools

import jax
import jax.numpy as jnp
import ml_dtypes
import numpy as np
from jax import lax
from jax.experimental import pallas as pl
from jax.experimental.pallas import tpu as pltpu
from jax.sharding import PartitionSpec as P

N = 256
H = 128
STRIDE = 40
PC = 4
HALO = 108
LEVELS = 2
COLS = 160
EDGE = 112
EPS = 1e-06
MESH = pl.DeviceIdType.MESH
f32, bf16 = jnp.float32, jnp.bfloat16


def tables():
    i = np.arange(N)
    product = i[:, None] * i[None, :] % N
    cos = np.cos(product * (2.0 * np.pi / N))
    sin = np.sin(product * (2.0 * np.pi / N))
    alternate = cos[:, H]
    columns = np.concatenate([cos[:, :H], -sin[:, :H]], axis=1)
    columns[:, 0] = 0.0
    columns[:, H] = alternate
    ahead = np.concatenate([cos[:H], sin[:H]], axis=0)
    ahead[H] = alternate
    back = 2.0 * np.concatenate([cos[:, :H], sin[:, :H]], axis=1)
    back[:, 0] = 1.0
    back[:, H] = alternate
    last = 2.0 * np.concatenate([cos[:, :H], -sin[:, :H]], axis=1)
    last[:, 0] = alternate
    last[:, H] = 0.0
    lowered = [a.astype(ml_dtypes.bfloat16) for a in (columns, ahead, back, cos, sin, last)]
    return np.stack(lowered)


def dot(a, b):
    return jnp.dot(a, b, preferred_element_type=f32)


def column_stats(x):
    mean = jnp.sum(x, axis=1, keepdims=True) * (1.0 / N)
    low = x - mean
    return low.astype(bf16), mean, jnp.sum(low * low, axis=1, keepdims=True)


def side_rows(means, energies):
    lane = lax.broadcasted_iota(jnp.int32, (COLS, H), 1)
    block = jnp.zeros((COLS, H), f32)
    for at, value in enumerate(means + energies):
        block = jnp.where(lane == at, value, block)
    block = jnp.concatenate([block, jnp.zeros((N - COLS, H), f32)], axis=0)
    return jnp.transpose(block)[:8]


def windows(own, left, right, at):
    row = lax.broadcasted_iota(jnp.int32, (8, N), 0)
    lane = lax.broadcasted_iota(jnp.int32, (8, N), 1)
    patch = row % PC
    begin = patch * STRIDE + (N - HALO)
    from_left = (patch < PC - 1) & (lane >= begin)
    from_right = (lane >= COLS) | ((patch == PC - 1) & (lane < begin - N))

    def spread(side):
        return jnp.where(row < PC, side[at : at + 1], side[at + 1 : at + 2])

    return jnp.where(from_left, spread(left), jnp.where(from_right, spread(right), spread(own)))


def centre(own, left, right):
    means = windows(own, left, right, 0)
    means = means - jnp.sum(means, axis=1, keepdims=True) * (1.0 / N)
    energies = windows(own, left, right, 2) + N * means * means
    return N * means, jnp.sum(energies, axis=1, keepdims=True)


def mixed(upper, lower, split):
    row = lax.broadcasted_iota(jnp.int32, upper.shape, 0)
    return jnp.where(row < split, upper.astype(f32), lower.astype(f32)).astype(bf16)


def patch_of(j, level, own, left, right):
    if j == 0:
        parts = [
            own[level, 0:144],
            mixed(own[level, 144:160], left[level, 0:16], 4),
            left[level, 16:112],
        ]
    elif j == 1:
        parts = [
            own[level, 0:160],
            right[level, 0:16],
            mixed(right[level, 16:32], left[level, 32:48], 12),
            left[level, 48:112],
        ]
    elif j == 2:
        parts = [
            own[level, 0:160],
            right[level, 0:64],
            mixed(right[level, 64:80], left[level, 80:96], 4),
            left[level, 96:112],
        ]
    else:
        parts = [
            mixed(right[level, 96:112], own[level, 0:16], 12),
            own[level, 16:160],
            right[level, 0:96],
        ]
    return jnp.concatenate(parts, axis=0)


def cross(now, prev, out):
    step = 16
    for begin in range(0, H, step):
        even, odd = pl.ds(begin, step), pl.ds(H + begin, step)
        a_er, a_ei, a_oi, a_or = now[even, :H], now[even, H:], now[odd, :H], now[odd, H:]
        b_er, b_ei, b_oi, b_or = prev[even, :H], prev[even, H:], prev[odd, :H], prev[odd, H:]
        ee_r = a_er * b_er + a_ei * b_ei
        ee_i = a_ei * b_er - a_er * b_ei
        oo_r = a_or * b_or + a_oi * b_oi
        oo_i = a_or * b_oi - a_oi * b_or
        odd_r = (a_er * b_or - a_ei * b_oi) + (a_or * b_er - a_oi * b_ei)
        minus_i = (a_oi * b_er + a_or * b_ei) - (a_ei * b_or + a_er * b_oi)
        if begin == 0:
            first = lax.broadcasted_iota(jnp.int32, (step, H), 0) == 0
            even_r = jnp.where(first, ee_r, ee_r + oo_r)
            even_i = jnp.where(first, ee_i, ee_i + oo_i)
            minus_i = jnp.where(first, oo_r, minus_i)
            odd_r = jnp.where(first, oo_i, odd_r)
        else:
            even_r, even_i = ee_r + oo_r, ee_i + oo_i
        out[even, :H] = even_r.astype(bf16)
        out[even, H:] = even_i.astype(bf16)
        out[odd, :H] = minus_i.astype(bf16)
        out[odd, H:] = odd_r.astype(bf16)


def first_kernel(
    n_sec,
    n_tile,
    x_hbm,
    prior_hbm,
    table_hbm,
    held,
    turned_out,
    rows_out,
    table,
    spec_later,
    b_own,
    b_left,
    b_right,
    x,
    prior,
    a_own,
    a_left,
    a_right,
    side,
    side_out,
    side_in,
    b_side,
    r_own,
    r_side,
    spec_a,
    spec_last,
    spec_b,
    crossed,
    turned,
    rows,
    load_sem,
    send_sem,
    recv_sem,
    ready_sem,
):
    s, t = lax.axis_index("sec"), lax.axis_index("tile")
    has_left, has_right = t > 0, t < n_tile - 1
    has_next, has_prev = s < n_sec - 1, s > 0
    middle = n_tile // 2
    at_middle, before_middle = t == middle, t == middle - 1
    elsewhere = jnp.logical_not(at_middle)
    crossing = (s % 2 == 1) & has_next
    left_past = at_middle & crossing
    step = t % middle
    split, before_split = at_middle & (s != n_sec // 2), before_middle & (s != n_sec // 2)
    joined = jnp.logical_not(split)
    early = at_middle & (s != n_sec // 2)
    not_early = jnp.logical_not(early)
    far, far_next = s == n_sec // 2 - 1, s == n_sec // 2
    back_out = far & (step >= 1) & (step <= middle // 2)
    back_in = far_next & (step < middle // 2)
    back_past = far & ((step < middle // 2) | before_middle)
    late_out, late_in = far & before_middle, far_next & before_middle
    over_out, over_in = far & at_middle, late_in
    relay_out, relay_in = crossing & before_middle, crossing & (t == n_tile - 1)
    edge_out, edge_in = relay_out & jnp.logical_not(far), relay_in & jnp.logical_not(far)
    tile_out, tile_in = relay_out & far, relay_in & far
    not_tile_out = jnp.logical_not(tile_out)
    first_patches = at_middle & (s % 2 == 0) & has_prev
    to_left, to_right, to_next = {"tile": t - 1}, {"tile": t + 1}, {"sec": s + 1}

    def load(source, target, at):
        return pltpu.make_async_copy(source, target, load_sem.at[at])

    load_x = [load(x_hbm.at[i], x.at[i], i) for i in range(LEVELS)]
    load_first = load(table_hbm.at[0], table.at[0], 2)
    load_rest = load(table_hbm.at[1:6], table.at[1:6], 3)
    load_prior = load(prior_hbm, prior, 4)
    load_x[0].start()
    load_x[1].start()
    load_first.start()
    load_rest.start()

    barrier = pltpu.get_barrier_semaphore()

    def greet(there, device):
        @pl.when(there)
        def _():
            pl.semaphore_signal(barrier, inc=1, device_id=device, device_id_type=MESH)

    greet(has_left, to_left)
    greet(has_right & jnp.logical_not(before_split), to_right)
    greet(has_prev & jnp.logical_not(late_in), {"sec": s - 1})
    greet(late_out, to_next)
    greet(back_in, {"sec": s - 1, "tile": t + 1})
    greet(first_patches & far_next, {"sec": s - 1, "tile": t - 1})
    greet(relay_in, {"tile": middle - 1})
    relayed = (first_patches & jnp.logical_not(far_next)) | late_in
    greet(relayed, {"sec": s - 1, "tile": n_tile - 1})
    greet(over_out, {"sec": s + 1, "tile": t - 1})

    @pl.when(s == 0)
    def _():
        load_prior.start()

    started = {}
    count = [0]

    def note(there, copy):
        started.setdefault(id(there), (there, []))[1].append(copy)

    def settle(groups):
        for there, copies in list(groups.values()):

            @pl.when(there)
            def _(copies=copies):
                for copy in copies:
                    copy.wait_send()

        groups.clear()

    def remote(source, target, device, arrival):
        at = count[0]
        count[0] += 1
        return pltpu.make_async_remote_copy(
            src_ref=source,
            dst_ref=target,
            send_sem=send_sem.at[at],
            recv_sem=recv_sem.at[arrival],
            device_id=device,
            device_id_type=MESH,
        )

    def send(there, *what):
        copy = remote(*what)
        pl.when(there)(copy.start)
        note(there, copy)

    def arrived(there, target, arrival):
        copy = pltpu.make_async_remote_copy(
            src_ref=target,
            dst_ref=target,
            send_sem=send_sem.at[0],
            recv_sem=recv_sem.at[arrival],
            device_id=to_next,
            device_id_type=MESH,
        )
        if there is None:
            copy.wait_recv()
        else:
            pl.when(there)(copy.wait_recv)

    @pl.when(jnp.logical_not(has_left))
    def _():
        a_left[...] = jnp.zeros_like(a_left)
        b_left[...] = jnp.zeros_like(b_left)
        side_in[0] = jnp.zeros((8, N), f32)
        b_side[1] = jnp.zeros((8, N), f32)

    @pl.when(jnp.logical_not(has_right))
    def _():
        a_right[...] = jnp.zeros_like(a_right)
        b_right[...] = jnp.zeros_like(b_right)
        side_in[1] = jnp.zeros((8, N), f32)
        b_side[2] = jnp.zeros((8, N), f32)

    low, high = pl.ds(0, EDGE), pl.ds(COLS - EDGE, EDGE)
    to_direct, to_back = {"sec": s + 1, "tile": t + 1}, {"sec": s + 1, "tile": t - 1}
    to_last, to_middle = {"tile": n_tile - 1}, {"sec": s + 1, "tile": middle}
    to_before = {"sec": s + 1, "tile": middle - 1}

    def prepare(there, *what):
        copy = remote(*what)
        note(there, copy)
        return lambda when: pl.when(when & there)(copy.start)

    def columns_to(i):
        right = prepare(has_right, a_own.at[i, high], a_left.at[i], to_right, i)
        left = prepare(has_left, a_own.at[i, low], a_right.at[i], to_left, 2 + i)
        return right, left

    def send_columns(i):
        send(back_out, a_own.at[i, low], b_right.at[i], to_back, 8 + i)
        send(tile_out, a_own.at[i, high], b_left.at[i], to_direct, 6 + i)
        send(tile_out, a_own.at[i], r_own.at[i], to_last, 15 + i)
        right, left = to_sides[i]
        right(not_tile_out)
        send(edge_out, a_own.at[i, high], r_own.at[i, high], to_last, 15 + i)
        left(joined)
    to_sides = [columns_to(i) for i in range(LEVELS)]
    lowered, stats = [], []
    for i in range(LEVELS):
        load_x[i].wait()
        low_i, *stat = column_stats(x[i])
        lowered.append(low_i)
        stats.append(stat)
    own_side = side_rows(*zip(*stats))
    side[...] = own_side
    side_out[0] = pltpu.roll(own_side, N - COLS, 1)
    side_out[1] = pltpu.roll(own_side, COLS, 1)
    load_first.wait()
    a_own[0] = dot(lowered[0], table[0]).astype(bf16)

    known = [has_left & joined, has_right, has_next & jnp.logical_not(late_out)]
    known += [relay_out, tile_out, relay_in, back_out, late_in, over_in]
    pl.semaphore_wait(barrier, sum(v.astype(jnp.int32) for v in known))

    @pl.when(before_split)
    def _():
        pl.semaphore_signal(ready_sem.at[1], inc=1, device_id=to_right, device_id_type=MESH)

    @pl.when(over_in)
    def _():
        pl.semaphore_signal(
            ready_sem.at[2],
            inc=1,
            device_id={"sec": s - 1, "tile": t + 1},
            device_id_type=MESH,
        )

    @pl.when(late_in)
    def _():
        pl.semaphore_signal(
            ready_sem.at[0], inc=1, device_id={"sec": s - 1}, device_id_type=MESH
        )

    send(back_out, side_out.at[1], b_side.at[2], to_back, 14)
    send(has_right, side_out.at[0], side_in.at[0], to_right, 10)
    send(tile_out, side_out.at[0], b_side.at[1], to_direct, 13)
    send(edge_out, side_out.at[0], r_side, to_last, 17)
    side_left = prepare(has_left, side_out.at[1], side_in.at[1], to_left, 11)
    side_left(joined)
    send_columns(0)
    a_own[1] = dot(lowered[1], table[0]).astype(bf16)
    send_columns(1)
    for right, _ in to_sides:
        right(tile_out)

    send(tile_out, side, r_side, to_last, 17)
    own_on = has_next & not_tile_out

    for i in range(LEVELS):
        send(own_on, a_own.at[i], b_own.at[i], to_next, 4 + i)
    send(own_on, side, b_side.at[0], to_next, 12)

    for i in range(LEVELS):
        arrived(edge_in, r_own.at[i, high], 15 + i)
        send(edge_in, r_own.at[i, high], b_left.at[i], to_middle, 6 + i)
        arrived(tile_in, r_own.at[i], 15 + i)
        send(tile_in, r_own.at[i], b_own.at[i], to_before, 4 + i)
        if i == 0:
            arrived(edge_in, r_side, 17)
            send(edge_in, r_side, b_side.at[1], to_middle, 13)
    arrived(tile_in, r_side, 17)
    send(tile_in, r_side, b_side.at[0], to_before, 12)

    @pl.when(split)
    def _():
        pl.semaphore_wait(ready_sem.at[1], 1)

    side_left(split)
    for _, left in to_sides:
        left(split)

    @pl.when(over_out)
    def _():
        pl.semaphore_wait(ready_sem.at[2], 1)

    send(over_out, side_out.at[1], b_side.at[2], to_back, 14)
    for i in range(LEVELS):
        send(over_out, a_own.at[i, low], b_right.at[i], to_back, 8 + i)

    @pl.when(s == 0)
    def _():
        load_prior.wait()
        prior_stats = []
        for i in range(LEVELS):
            low_i, *stat = column_stats(prior[i])
            b_own[i] = dot(low_i, table[0]).astype(bf16)
            prior_stats.append(stat)
        prior_side = side_rows(*zip(*prior_stats))
        b_side[0] = prior_side
        side_out[2] = pltpu.roll(prior_side, N - COLS, 1)
        side_out[3] = pltpu.roll(prior_side, COLS, 1)

    first_right, first_left = (s == 0) & has_right, (s == 0) & has_left
    send(first_right, side_out.at[2], b_side.at[1], to_right, 13)
    send(first_left, side_out.at[3], b_side.at[2], to_left, 14)
    for i in range(LEVELS):
        send(first_right, b_own.at[i, high], b_left.at[i], to_right, 6 + i)
        send(first_left, b_own.at[i, low], b_right.at[i], to_left, 8 + i)

    @pl.when(late_out)
    def _():
        pl.semaphore_wait(ready_sem.at[0], 1)

    left_on = has_next & has_left & jnp.logical_not(left_past)
    right_on = has_next & has_right & jnp.logical_not(back_past)

    passed = {}
    last_waits = dict(started)
    started.clear()

    def pass_on(when, there, on, source, arrival, target, further):
        arrived(when & there, source, arrival)
        if arrival not in passed:
            passed[arrival] = remote(source, target, to_next, further)
            if arrival != 1:
                note(on, passed[arrival])
        pl.when(when & on)(passed[arrival].start)

    def pass_left(i):
        pass_on(True, has_left, left_on, a_left.at[i], i, b_left.at[i], 6 + i)

    def pass_right(when, i):
        pass_on(when, has_right, right_on, a_right.at[i], 2 + i, b_right.at[i], 8 + i)

    def pass_right_side(when):
        pass_on(when, has_right, right_on, side_in.at[1], 11, b_side.at[2], 14)

    def begin_spectra():
        for j in range(PC - 1):
            spec_a[j] = dot(table[1], patch_of(j, 0, a_own, a_left, a_right))

    def previous_right(i):
        arrived(has_prev, b_own.at[i], 4 + i)
        arrived(has_right, b_right.at[i], 8 + i)

    def last_patches(*levels):
        for i in levels:
            spec_last[i] = dot(table[1], patch_of(PC - 1, i, a_own, a_left, a_right))
            spec_b[PC - 1 + i] = dot(table[1], patch_of(PC - 1, i, b_own, b_left, b_right))
        for i in levels:
            cross(spec_last.at[i], spec_b.at[PC - 1 + i], crossed.at[PC - 1 + i])
        for i in levels:
            turned[PC - 1 + i] = dot(table[2], crossed[PC - 1 + i]).astype(bf16)

    upper = (step >= middle // 2) & jnp.logical_not(before_middle)
    load_rest.wait()
    pass_right(at_middle, 0)
    pass_right(at_middle, 1)
    pass_right_side(at_middle)

    @pl.when(early)
    def _():
        previous_right(0)
        previous_right(1)
        last_patches(0, 1)

    pass_on(True, has_left, left_on, side_in.at[0], 10, b_side.at[1], 13)
    pass_right_side(upper)
    pass_left(0)
    pass_right(upper, 0)
    pl.when(at_middle)(begin_spectra)
    pass_left(1)
    pass_right(elsewhere & jnp.logical_not(upper), 0)
    pass_right(elsewhere, 1)
    pass_right_side(elsewhere & jnp.logical_not(upper))
    pl.when(elsewhere)(begin_spectra)

    settle(last_waits)
    arrived(has_prev, b_side.at[0], 12)
    arrived(has_right, b_side.at[2], 14)
    arrived(has_left, b_side.at[1], 13)
    for j in range(PC - 1):
        spec_later[j] = dot(table[1], patch_of(j, 1, a_own, a_left, a_right))
    a_flat, a_energy = centre(side[...], side_in[0], side_in[1])
    b_flat, b_energy = centre(b_side[0], b_side[1], b_side[2])
    pair = jnp.concatenate([a_flat, b_flat], axis=0).astype(bf16)
    even_part, odd_part = dot(pair, table[3]), dot(pair, table[4])
    a_e, b_e, a_o, b_o = even_part[:8], even_part[8:], odd_part[:8], odd_part[8:]
    both = jnp.concatenate([a_e * b_e + a_o * b_o, a_e * b_o - a_o * b_e], axis=0).astype(bf16)
    flat = dot(both, table[3])[:8] - dot(both, table[4])[8:]
    scale = 1.0 / (N * jnp.sqrt(a_energy + EPS) * jnp.sqrt(b_energy + EPS))
    rows[0:8] = flat * scale
    rows[8:16] = jnp.broadcast_to(scale, (8, N))
    rows_out[...] = rows[...]

    pl.when(not_early)(lambda: previous_right(0))
    arrived(has_left, b_left.at[0], 6)
    for j in range(PC - 1):
        spec_b[j] = dot(table[1], patch_of(j, 0, b_own, b_left, b_right))
    for j in range(PC - 1):
        cross(spec_a.at[j], spec_b.at[j], crossed.at[j])
    for j in range(PC - 1):
        turned[j] = dot(table[2], crossed[j]).astype(bf16)
    for j in range(PC - 1):
        held[j] = finished(turned[j], table, rows, j)

    @pl.when(not_early)
    def _():
        previous_right(1)
        last_patches(0, 1)

    for j in range(LEVELS):
        turned_out[j] = turned[PC - 1 + j]
    settle(started)
    arrived(has_left, b_left.at[1], 7)
    pl.when(left_on)(passed[1].wait_send)


def finished(turned, table, rows, p):
    product = lax.dot_general(
        table[5], turned, (((1,), (1,)), ((), ())), preferred_element_type=f32
    )
    return product * rows[8 + p : 9 + p] + rows[p : p + 1]


def last_kernel(
    held, lasts, rows, table, spec_a, b_own, b_left, b_right, out_hbm, spec_b, crossed, turned, maps, sem
):
    copies = []

    def write(source, p):
        copy = pltpu.make_async_copy(source, out_hbm.at[p], sem.at[p])
        copy.start()
        copies.append(copy)

    for j in range(PC - 1):
        write(held.at[j], j)
    for j in range(PC - 1):
        spec_b[j] = dot(table[1], patch_of(j, 1, b_own, b_left, b_right))
    for i in range(LEVELS):
        maps[PC - 1 + i] = finished(lasts[i], table, rows, (i + 1) * PC - 1)
        write(maps.at[PC - 1 + i], (i + 1) * PC - 1)
    for j in range(PC - 1):
        cross(spec_a.at[j], spec_b.at[j], crossed.at[j])
        turned[j] = dot(table[2], crossed[j]).astype(bf16)
    for j in range(PC - 1):
        maps[j] = finished(turned[j], table, rows, PC + j)
        write(maps.at[j], PC + j)
    for copy in copies:
        copy.wait()


def local(n_sec, n_tile, sections, prior):
    x = jnp.swapaxes(sections[0], 1, 2)
    before = jnp.swapaxes(prior, 1, 2)
    hbm = pl.BlockSpec(memory_space=pltpu.HBM)
    vmem = pl.BlockSpec(memory_space=pltpu.VMEM)
    patches = LEVELS * PC
    columns = lambda rows: pltpu.VMEM((LEVELS, rows, N), bf16)
    held = lambda *shape: jax.ShapeDtypeStruct(shape, bf16)
    operands = (x, before, jnp.asarray(tables()))
    results = pl.pallas_call(
        functools.partial(first_kernel, n_sec, n_tile),
        out_shape=(
            jax.ShapeDtypeStruct((PC - 1, N, N), f32),
            held(LEVELS, N, N),
            jax.ShapeDtypeStruct((16, N), f32),
            held(6, N, N),
            jax.ShapeDtypeStruct((PC - 1, N, N), f32),
            held(LEVELS, COLS, N),
            held(LEVELS, EDGE, N),
            held(LEVELS, EDGE, N),
        ),
        in_specs=[hbm] * 3,
        out_specs=(vmem,) * 8,
        scratch_shapes=[
            pltpu.VMEM((LEVELS, COLS, N), f32),
            pltpu.VMEM((LEVELS, COLS, N), f32),
            columns(COLS),
            columns(EDGE),
            columns(EDGE),
            pltpu.VMEM((8, N), f32),
            pltpu.VMEM((4, 8, N), f32),
            pltpu.VMEM((2, 8, N), f32),
            pltpu.VMEM((3, 8, N), f32),
            columns(COLS),
            pltpu.VMEM((8, N), f32),
            pltpu.VMEM((PC - 1, N, N), f32),
            pltpu.VMEM((LEVELS, N, N), f32),
            pltpu.VMEM((PC + 1, N, N), f32),
            pltpu.VMEM((PC + 1, N, N), bf16),
            pltpu.VMEM((PC + 1, N, N), bf16),
            pltpu.VMEM((16, N), f32),
            pltpu.SemaphoreType.DMA((5,)),
            pltpu.SemaphoreType.DMA((47,)),
            pltpu.SemaphoreType.DMA((18,)),
            pltpu.SemaphoreType.REGULAR((3,)),
        ],
        compiler_params=pltpu.CompilerParams(
            collective_id=0, has_side_effects=True, vmem_limit_bytes=16 * 2**20
        ),
        name="spectra",
    )(*(pltpu.with_memory_space_constraint(v, pltpu.HBM) for v in operands))
    maps = pl.pallas_call(
        last_kernel,
        out_shape=jax.ShapeDtypeStruct((patches, N, N), f32),
        in_specs=[vmem] * 8,
        out_specs=hbm,
        scratch_shapes=[
            pltpu.VMEM((PC - 1, N, N), f32),
            pltpu.VMEM((PC - 1, N, N), bf16),
            pltpu.VMEM((PC - 1, N, N), bf16),
            pltpu.VMEM((PC + 1, N, N), f32),
            pltpu.SemaphoreType.DMA((patches,)),
        ],
        compiler_params=pltpu.CompilerParams(vmem_limit_bytes=16 * 2**20),
        name="maps",
    )(*results)
    return maps.reshape(1, LEVELS, 1, PC, N, N)


def solution(mesh):
    return jax.shard_map(
        functools.partial(local, mesh.shape["sec"], mesh.shape["tile"]),
        mesh=mesh,
        in_specs=(P("sec", None, None, "tile"), P(None, None, "tile")),
        out_specs=P("sec", None, None, "tile", None, None),
        check_vma=False,
    )
```

```python
import functools

import jax
import jax.numpy as jnp
import ml_dtypes
import numpy as np
from jax import lax
from jax.experimental import pallas as pl
from jax.experimental.pallas import tpu as pltpu
from jax.sharding import PartitionSpec as P

N = 256
H = 128
STRIDE = 40
PC = 4
HALO = 108
LEVELS = 2
COLS = 160
EDGE = 112
EPS = 1e-06
MESH = pl.DeviceIdType.MESH
f32, bf16 = jnp.float32, jnp.bfloat16


def tables():
    i = np.arange(N)
    product = i[:, None] * i[None, :] % N
    cos = np.cos(product * (2.0 * np.pi / N))
    sin = np.sin(product * (2.0 * np.pi / N))
    alternate = cos[:, H]
    columns = np.concatenate([cos[:, :H], -sin[:, :H]], axis=1)
    columns[:, 0] = 0.0
    columns[:, H] = alternate
    ahead = np.concatenate([cos[:H], sin[:H]], axis=0)
    ahead[H] = alternate
    back = 2.0 * np.concatenate([cos[:, :H], sin[:, :H]], axis=1)
    back[:, 0] = 1.0
    back[:, H] = alternate
    last = 2.0 * np.concatenate([cos[:, :H], -sin[:, :H]], axis=1)
    last[:, 0] = alternate
    last[:, H] = 0.0
    lowered = [a.astype(ml_dtypes.bfloat16) for a in (columns, ahead, back, cos, sin, last)]
    return np.stack(lowered)


def dot(a, b):
    return jnp.dot(a, b, preferred_element_type=f32)


def column_stats(x):
    mean = jnp.sum(x, axis=1, keepdims=True) * (1.0 / N)
    low = x - mean
    return low.astype(bf16), mean, jnp.sum(low * low, axis=1, keepdims=True)


def side_rows(means, energies):
    lane = lax.broadcasted_iota(jnp.int32, (COLS, H), 1)
    block = jnp.zeros((COLS, H), f32)
    for at, value in enumerate(means + energies):
        block = jnp.where(lane == at, value, block)
    block = jnp.concatenate([block, jnp.zeros((N - COLS, H), f32)], axis=0)
    return jnp.transpose(block)[:8]


def windows(own, left, right, at):
    row = lax.broadcasted_iota(jnp.int32, (8, N), 0)
    lane = lax.broadcasted_iota(jnp.int32, (8, N), 1)
    patch = row % PC
    begin = patch * STRIDE + (N - HALO)
    from_left = (patch < PC - 1) & (lane >= begin)
    from_right = (lane >= COLS) | ((patch == PC - 1) & (lane < begin - N))

    def spread(side):
        return jnp.where(row < PC, side[at : at + 1], side[at + 1 : at + 2])

    return jnp.where(from_left, spread(left), jnp.where(from_right, spread(right), spread(own)))


def centre(own, left, right):
    means = windows(own, left, right, 0)
    means = means - jnp.sum(means, axis=1, keepdims=True) * (1.0 / N)
    energies = windows(own, left, right, 2) + N * means * means
    return N * means, jnp.sum(energies, axis=1, keepdims=True)


def mixed(upper, lower, split):
    row = lax.broadcasted_iota(jnp.int32, upper.shape, 0)
    return jnp.where(row < split, upper.astype(f32), lower.astype(f32)).astype(bf16)


def patch_of(j, level, own, left, right):
    if j == 0:
        parts = [
            own[level, 0:144],
            mixed(own[level, 144:160], left[level, 0:16], 4),
            left[level, 16:112],
        ]
    elif j == 1:
        parts = [
            own[level, 0:160],
            right[level, 0:16],
            mixed(right[level, 16:32], left[level, 32:48], 12),
            left[level, 48:112],
        ]
    elif j == 2:
        parts = [
            own[level, 0:160],
            right[level, 0:64],
            mixed(right[level, 64:80], left[level, 80:96], 4),
            left[level, 96:112],
        ]
    else:
        parts = [
            mixed(right[level, 96:112], own[level, 0:16], 12),
            own[level, 16:160],
            right[level, 0:96],
        ]
    return jnp.concatenate(parts, axis=0)


def cross(now, prev, out):
    step = 16
    for begin in range(0, H, step):
        even, odd = pl.ds(begin, step), pl.ds(H + begin, step)
        a_er, a_ei, a_oi, a_or = now[even, :H], now[even, H:], now[odd, :H], now[odd, H:]
        b_er, b_ei, b_oi, b_or = prev[even, :H], prev[even, H:], prev[odd, :H], prev[odd, H:]
        ee_r = a_er * b_er + a_ei * b_ei
        ee_i = a_ei * b_er - a_er * b_ei
        oo_r = a_or * b_or + a_oi * b_oi
        oo_i = a_or * b_oi - a_oi * b_or
        odd_r = (a_er * b_or - a_ei * b_oi) + (a_or * b_er - a_oi * b_ei)
        minus_i = (a_oi * b_er + a_or * b_ei) - (a_ei * b_or + a_er * b_oi)
        if begin == 0:
            first = lax.broadcasted_iota(jnp.int32, (step, H), 0) == 0
            even_r = jnp.where(first, ee_r, ee_r + oo_r)
            even_i = jnp.where(first, ee_i, ee_i + oo_i)
            minus_i = jnp.where(first, oo_r, minus_i)
            odd_r = jnp.where(first, oo_i, odd_r)
        else:
            even_r, even_i = ee_r + oo_r, ee_i + oo_i
        out[even, :H] = even_r.astype(bf16)
        out[even, H:] = even_i.astype(bf16)
        out[odd, :H] = minus_i.astype(bf16)
        out[odd, H:] = odd_r.astype(bf16)


def first_kernel(
    n_sec,
    n_tile,
    x_hbm,
    prior_hbm,
    table_hbm,
    turned_out,
    rows_out,
    table,
    spec_later,
    b_own,
    b_left,
    b_right,
    x,
    prior,
    a_own,
    a_left,
    a_right,
    side,
    side_out,
    side_in,
    b_side,
    r_own,
    r_side,
    spec_a,
    spec_last,
    spec_b,
    crossed,
    rows,
    load_sem,
    send_sem,
    recv_sem,
    ready_sem,
):
    s, t = lax.axis_index("sec"), lax.axis_index("tile")
    has_left, has_right = t > 0, t < n_tile - 1
    has_next, has_prev = s < n_sec - 1, s > 0
    middle = n_tile // 2
    at_middle, before_middle = t == middle, t == middle - 1
    elsewhere = jnp.logical_not(at_middle)
    crossing = (s % 2 == 1) & has_next
    left_past = at_middle & crossing
    step = t % middle
    split, before_split = at_middle & (s != n_sec // 2), before_middle & (s != n_sec // 2)
    joined = jnp.logical_not(split)
    early = at_middle & (s != n_sec // 2)
    not_early = jnp.logical_not(early)
    far, far_next = s == n_sec // 2 - 1, s == n_sec // 2
    back_out = far & (step >= 1) & (step <= middle // 2)
    back_in = far_next & (step < middle // 2)
    back_past = far & ((step < middle // 2) | before_middle)
    late_out, late_in = far & before_middle, far_next & before_middle
    over_out, over_in = far & at_middle, late_in
    relay_out, relay_in = crossing & before_middle, crossing & (t == n_tile - 1)
    edge_out, edge_in = relay_out & jnp.logical_not(far), relay_in & jnp.logical_not(far)
    tile_out, tile_in = relay_out & far, relay_in & far
    not_tile_out = jnp.logical_not(tile_out)
    first_patches = at_middle & (s % 2 == 0) & has_prev
    to_left, to_right, to_next = {"tile": t - 1}, {"tile": t + 1}, {"sec": s + 1}

    def load(source, target, at):
        return pltpu.make_async_copy(source, target, load_sem.at[at])

    load_x = [load(x_hbm.at[i], x.at[i], i) for i in range(LEVELS)]
    load_first = load(table_hbm.at[0], table.at[0], 2)
    load_rest = load(table_hbm.at[1:6], table.at[1:6], 3)
    load_prior = load(prior_hbm, prior, 4)
    load_x[0].start()
    load_x[1].start()
    load_first.start()
    load_rest.start()

    barrier = pltpu.get_barrier_semaphore()

    def greet(there, device):
        @pl.when(there)
        def _():
            pl.semaphore_signal(barrier, inc=1, device_id=device, device_id_type=MESH)

    greet(has_left, to_left)
    greet(has_right & jnp.logical_not(before_split), to_right)
    greet(has_prev & jnp.logical_not(late_in), {"sec": s - 1})
    greet(late_out, to_next)
    greet(back_in, {"sec": s - 1, "tile": t + 1})
    greet(first_patches & far_next, {"sec": s - 1, "tile": t - 1})
    greet(relay_in, {"tile": middle - 1})
    relayed = (first_patches & jnp.logical_not(far_next)) | late_in
    greet(relayed, {"sec": s - 1, "tile": n_tile - 1})
    greet(over_out, {"sec": s + 1, "tile": t - 1})

    @pl.when(s == 0)
    def _():
        load_prior.start()

    started = {}
    count = [0]

    def note(there, copy):
        started.setdefault(id(there), (there, []))[1].append(copy)

    def settle(groups):
        for there, copies in list(groups.values()):

            @pl.when(there)
            def _(copies=copies):
                for copy in copies:
                    copy.wait_send()

        groups.clear()

    def remote(source, target, device, arrival):
        at = count[0]
        count[0] += 1
        return pltpu.make_async_remote_copy(
            src_ref=source,
            dst_ref=target,
            send_sem=send_sem.at[at],
            recv_sem=recv_sem.at[arrival],
            device_id=device,
            device_id_type=MESH,
        )

    def send(there, *what):
        copy = remote(*what)
        pl.when(there)(copy.start)
        note(there, copy)

    def arrived(there, target, arrival):
        copy = pltpu.make_async_remote_copy(
            src_ref=target,
            dst_ref=target,
            send_sem=send_sem.at[0],
            recv_sem=recv_sem.at[arrival],
            device_id=to_next,
            device_id_type=MESH,
        )
        if there is None:
            copy.wait_recv()
        else:
            pl.when(there)(copy.wait_recv)

    @pl.when(jnp.logical_not(has_left))
    def _():
        a_left[...] = jnp.zeros_like(a_left)
        b_left[...] = jnp.zeros_like(b_left)
        side_in[0] = jnp.zeros((8, N), f32)
        b_side[1] = jnp.zeros((8, N), f32)

    @pl.when(jnp.logical_not(has_right))
    def _():
        a_right[...] = jnp.zeros_like(a_right)
        b_right[...] = jnp.zeros_like(b_right)
        side_in[1] = jnp.zeros((8, N), f32)
        b_side[2] = jnp.zeros((8, N), f32)

    low, high = pl.ds(0, EDGE), pl.ds(COLS - EDGE, EDGE)
    to_direct, to_back = {"sec": s + 1, "tile": t + 1}, {"sec": s + 1, "tile": t - 1}
    to_last, to_middle = {"tile": n_tile - 1}, {"sec": s + 1, "tile": middle}
    to_before = {"sec": s + 1, "tile": middle - 1}

    def prepare(there, *what):
        copy = remote(*what)
        note(there, copy)
        return lambda when: pl.when(when & there)(copy.start)

    def columns_to(i):
        right = prepare(has_right, a_own.at[i, high], a_left.at[i], to_right, i)
        left = prepare(has_left, a_own.at[i, low], a_right.at[i], to_left, 2 + i)
        return right, left

    def send_columns(i):
        send(back_out, a_own.at[i, low], b_right.at[i], to_back, 8 + i)
        send(tile_out, a_own.at[i, high], b_left.at[i], to_direct, 6 + i)
        send(tile_out, a_own.at[i], r_own.at[i], to_last, 15 + i)
        right, left = to_sides[i]
        right(not_tile_out)
        send(edge_out, a_own.at[i, high], r_own.at[i, high], to_last, 15 + i)
        left(joined)
    to_sides = [columns_to(i) for i in range(LEVELS)]
    lowered, stats = [], []
    for i in range(LEVELS):
        load_x[i].wait()
        low_i, *stat = column_stats(x[i])
        lowered.append(low_i)
        stats.append(stat)
    own_side = side_rows(*zip(*stats))
    side[...] = own_side
    side_out[0] = pltpu.roll(own_side, N - COLS, 1)
    side_out[1] = pltpu.roll(own_side, COLS, 1)
    load_first.wait()
    a_own[0] = dot(lowered[0], table[0]).astype(bf16)

    known = [has_left & joined, has_right, has_next & jnp.logical_not(late_out)]
    known += [relay_out, tile_out, relay_in, back_out, late_in, over_in]
    pl.semaphore_wait(barrier, sum(v.astype(jnp.int32) for v in known))

    @pl.when(before_split)
    def _():
        pl.semaphore_signal(ready_sem.at[1], inc=1, device_id=to_right, device_id_type=MESH)

    @pl.when(over_in)
    def _():
        pl.semaphore_signal(
            ready_sem.at[2],
            inc=1,
            device_id={"sec": s - 1, "tile": t + 1},
            device_id_type=MESH,
        )

    @pl.when(late_in)
    def _():
        pl.semaphore_signal(
            ready_sem.at[0], inc=1, device_id={"sec": s - 1}, device_id_type=MESH
        )

    send(back_out, side_out.at[1], b_side.at[2], to_back, 14)
    send(has_right, side_out.at[0], side_in.at[0], to_right, 10)
    send(tile_out, side_out.at[0], b_side.at[1], to_direct, 13)
    send(edge_out, side_out.at[0], r_side, to_last, 17)
    side_left = prepare(has_left, side_out.at[1], side_in.at[1], to_left, 11)
    side_left(joined)
    send_columns(0)
    a_own[1] = dot(lowered[1], table[0]).astype(bf16)
    send_columns(1)
    for right, _ in to_sides:
        right(tile_out)

    send(tile_out, side, r_side, to_last, 17)
    own_on = has_next & not_tile_out

    for i in range(LEVELS):
        send(own_on, a_own.at[i], b_own.at[i], to_next, 4 + i)
    send(own_on, side, b_side.at[0], to_next, 12)

    for i in range(LEVELS):
        arrived(edge_in, r_own.at[i, high], 15 + i)
        send(edge_in, r_own.at[i, high], b_left.at[i], to_middle, 6 + i)
        arrived(tile_in, r_own.at[i], 15 + i)
        send(tile_in, r_own.at[i], b_own.at[i], to_before, 4 + i)
        if i == 0:
            arrived(edge_in, r_side, 17)
            send(edge_in, r_side, b_side.at[1], to_middle, 13)
    arrived(tile_in, r_side, 17)
    send(tile_in, r_side, b_side.at[0], to_before, 12)

    @pl.when(split)
    def _():
        pl.semaphore_wait(ready_sem.at[1], 1)

    side_left(split)
    for _, left in to_sides:
        left(split)

    @pl.when(over_out)
    def _():
        pl.semaphore_wait(ready_sem.at[2], 1)

    send(over_out, side_out.at[1], b_side.at[2], to_back, 14)
    for i in range(LEVELS):
        send(over_out, a_own.at[i, low], b_right.at[i], to_back, 8 + i)

    @pl.when(s == 0)
    def _():
        load_prior.wait()
        prior_stats = []
        for i in range(LEVELS):
            low_i, *stat = column_stats(prior[i])
            b_own[i] = dot(low_i, table[0]).astype(bf16)
            prior_stats.append(stat)
        prior_side = side_rows(*zip(*prior_stats))
        b_side[0] = prior_side
        side_out[2] = pltpu.roll(prior_side, N - COLS, 1)
        side_out[3] = pltpu.roll(prior_side, COLS, 1)

    first_right, first_left = (s == 0) & has_right, (s == 0) & has_left
    send(first_right, side_out.at[2], b_side.at[1], to_right, 13)
    send(first_left, side_out.at[3], b_side.at[2], to_left, 14)
    for i in range(LEVELS):
        send(first_right, b_own.at[i, high], b_left.at[i], to_right, 6 + i)
        send(first_left, b_own.at[i, low], b_right.at[i], to_left, 8 + i)

    @pl.when(late_out)
    def _():
        pl.semaphore_wait(ready_sem.at[0], 1)

    left_on = has_next & has_left & jnp.logical_not(left_past)
    right_on = has_next & has_right & jnp.logical_not(back_past)

    passed = {}
    last_waits = dict(started)
    started.clear()

    def pass_on(when, there, on, source, arrival, target, further):
        arrived(when & there, source, arrival)
        if arrival not in passed:
            passed[arrival] = remote(source, target, to_next, further)
            if arrival != 1:
                note(on, passed[arrival])
        pl.when(when & on)(passed[arrival].start)

    def pass_left(i):
        pass_on(True, has_left, left_on, a_left.at[i], i, b_left.at[i], 6 + i)

    def pass_right(when, i):
        pass_on(when, has_right, right_on, a_right.at[i], 2 + i, b_right.at[i], 8 + i)

    def pass_right_side(when):
        pass_on(when, has_right, right_on, side_in.at[1], 11, b_side.at[2], 14)

    def begin_spectra():
        for j in range(PC - 1):
            spec_a[j] = dot(table[1], patch_of(j, 0, a_own, a_left, a_right))

    def previous_right(i):
        arrived(has_prev, b_own.at[i], 4 + i)
        arrived(has_right, b_right.at[i], 8 + i)

    def last_patches(*levels):
        for i in levels:
            spec_last[i] = dot(table[1], patch_of(PC - 1, i, a_own, a_left, a_right))
            spec_b[PC - 1 + i] = dot(table[1], patch_of(PC - 1, i, b_own, b_left, b_right))
        for i in levels:
            cross(spec_last.at[i], spec_b.at[PC - 1 + i], crossed.at[PC - 1 + i])
        for i in levels:
            turned_out[PC - 1 + i] = dot(table[2], crossed[PC - 1 + i]).astype(bf16)

    upper = (step >= middle // 2) & jnp.logical_not(before_middle)
    load_rest.wait()
    pass_right(at_middle, 0)
    pass_right(at_middle, 1)
    pass_right_side(at_middle)

    @pl.when(early)
    def _():
        previous_right(0)
        previous_right(1)
        last_patches(0, 1)

    pass_on(True, has_left, left_on, side_in.at[0], 10, b_side.at[1], 13)
    pass_right_side(upper)
    pass_left(0)
    pass_right(upper, 0)
    pl.when(at_middle)(begin_spectra)
    pass_left(1)
    pass_right(elsewhere & jnp.logical_not(upper), 0)
    pass_right(elsewhere, 1)
    pass_right_side(elsewhere & jnp.logical_not(upper))
    pl.when(elsewhere)(begin_spectra)

    settle(last_waits)
    arrived(has_prev, b_side.at[0], 12)
    arrived(has_right, b_side.at[2], 14)
    arrived(has_left, b_side.at[1], 13)
    for j in range(PC - 1):
        spec_later[j] = dot(table[1], patch_of(j, 1, a_own, a_left, a_right))
    a_flat, a_energy = centre(side[...], side_in[0], side_in[1])
    b_flat, b_energy = centre(b_side[0], b_side[1], b_side[2])
    pair = jnp.concatenate([a_flat, b_flat], axis=0).astype(bf16)
    even_part, odd_part = dot(pair, table[3]), dot(pair, table[4])
    a_e, b_e, a_o, b_o = even_part[:8], even_part[8:], odd_part[:8], odd_part[8:]
    both = jnp.concatenate([a_e * b_e + a_o * b_o, a_e * b_o - a_o * b_e], axis=0).astype(bf16)
    flat = dot(both, table[3])[:8] - dot(both, table[4])[8:]
    scale = 1.0 / (N * jnp.sqrt(a_energy + EPS) * jnp.sqrt(b_energy + EPS))
    rows[0:8] = flat * scale
    rows[8:16] = jnp.broadcast_to(scale, (8, N))
    rows_out[...] = rows[...]

    pl.when(not_early)(lambda: previous_right(0))
    arrived(has_left, b_left.at[0], 6)
    for j in range(PC - 1):
        spec_b[j] = dot(table[1], patch_of(j, 0, b_own, b_left, b_right))
    for j in range(PC - 1):
        cross(spec_a.at[j], spec_b.at[j], crossed.at[j])
    for j in range(PC - 1):
        turned_out[j] = dot(table[2], crossed[j]).astype(bf16)

    @pl.when(not_early)
    def _():
        previous_right(1)
        last_patches(0, 1)

    settle(started)
    arrived(has_left, b_left.at[1], 7)
    pl.when(left_on)(passed[1].wait_send)


def finished(turned, table, rows, p):
    product = lax.dot_general(
        table[5], turned, (((1,), (1,)), ((), ())), preferred_element_type=f32
    )
    return product * rows[8 + p : 9 + p] + rows[p : p + 1]


def last_kernel(
    before, rows, table, spec_a, b_own, b_left, b_right, out_hbm, spec_b, crossed, turned, maps, sem
):
    copies = []

    def write(source, p):
        copy = pltpu.make_async_copy(source, out_hbm.at[p], sem.at[p])
        copy.start()
        copies.append(copy)

    for j in range(PC - 1):
        spec_b[j] = dot(table[1], patch_of(j, 1, b_own, b_left, b_right))
    for j in range(PC + 1):
        p = j if j < PC else 2 * PC - 1
        maps[p] = finished(before[j], table, rows, p)
        write(maps.at[p], p)
    for j in range(PC - 1):
        cross(spec_a.at[j], spec_b.at[j], crossed.at[j])
        turned[j] = dot(table[2], crossed[j]).astype(bf16)
    for j in range(PC - 1):
        maps[PC + j] = finished(turned[j], table, rows, PC + j)
        write(maps.at[PC + j], PC + j)
    for copy in copies:
        copy.wait()


def local(n_sec, n_tile, sections, prior):
    x = jnp.swapaxes(sections[0], 1, 2)
    before = jnp.swapaxes(prior, 1, 2)
    hbm = pl.BlockSpec(memory_space=pltpu.HBM)
    vmem = pl.BlockSpec(memory_space=pltpu.VMEM)
    patches = LEVELS * PC
    columns = lambda rows: pltpu.VMEM((LEVELS, rows, N), bf16)
    held = lambda *shape: jax.ShapeDtypeStruct(shape, bf16)
    operands = (x, before, jnp.asarray(tables()))
    results = pl.pallas_call(
        functools.partial(first_kernel, n_sec, n_tile),
        out_shape=(
            held(PC + 1, N, N),
            jax.ShapeDtypeStruct((16, N), f32),
            held(6, N, N),
            jax.ShapeDtypeStruct((PC - 1, N, N), f32),
            held(LEVELS, COLS, N),
            held(LEVELS, EDGE, N),
            held(LEVELS, EDGE, N),
        ),
        in_specs=[hbm] * 3,
        out_specs=(vmem,) * 7,
        scratch_shapes=[
            pltpu.VMEM((LEVELS, COLS, N), f32),
            pltpu.VMEM((LEVELS, COLS, N), f32),
            columns(COLS),
            columns(EDGE),
            columns(EDGE),
            pltpu.VMEM((8, N), f32),
            pltpu.VMEM((4, 8, N), f32),
            pltpu.VMEM((2, 8, N), f32),
            pltpu.VMEM((3, 8, N), f32),
            columns(COLS),
            pltpu.VMEM((8, N), f32),
            pltpu.VMEM((PC - 1, N, N), f32),
            pltpu.VMEM((LEVELS, N, N), f32),
            pltpu.VMEM((PC + 1, N, N), f32),
            pltpu.VMEM((PC + 1, N, N), bf16),
            pltpu.VMEM((16, N), f32),
            pltpu.SemaphoreType.DMA((5,)),
            pltpu.SemaphoreType.DMA((47,)),
            pltpu.SemaphoreType.DMA((18,)),
            pltpu.SemaphoreType.REGULAR((3,)),
        ],
        compiler_params=pltpu.CompilerParams(
            collective_id=0, has_side_effects=True, vmem_limit_bytes=16 * 2**20
        ),
        name="spectra",
    )(*(pltpu.with_memory_space_constraint(v, pltpu.HBM) for v in operands))
    maps = pl.pallas_call(
        last_kernel,
        out_shape=jax.ShapeDtypeStruct((patches, N, N), f32),
        in_specs=[vmem] * 7,
        out_specs=hbm,
        scratch_shapes=[
            pltpu.VMEM((PC - 1, N, N), f32),
            pltpu.VMEM((PC - 1, N, N), bf16),
            pltpu.VMEM((PC - 1, N, N), bf16),
            pltpu.VMEM((patches, N, N), f32),
            pltpu.SemaphoreType.DMA((patches,)),
        ],
        compiler_params=pltpu.CompilerParams(vmem_limit_bytes=16 * 2**20),
        name="maps",
    )(*results)
    return maps.reshape(1, LEVELS, 1, PC, N, N)


def solution(mesh):
    return jax.shard_map(
        functools.partial(local, mesh.shape["sec"], mesh.shape["tile"]),
        mesh=mesh,
        in_specs=(P("sec", None, None, "tile"), P(None, None, "tile")),
        out_specs=P("sec", None, None, "tile", None, None),
        check_vma=False,
    )
```

```python
import functools

import jax
import jax.numpy as jnp
import ml_dtypes
import numpy as np
from jax import lax
from jax.experimental import pallas as pl
from jax.experimental.pallas import tpu as pltpu
from jax.sharding import PartitionSpec as P

N = 256
H = 128
STRIDE = 40
PC = 4
HALO = 108
LEVELS = 2
COLS = 160
EDGE = 112
EPS = 1e-06
MESH = pl.DeviceIdType.MESH
f32, bf16 = jnp.float32, jnp.bfloat16


def tables():
    i = np.arange(N)
    product = i[:, None] * i[None, :] % N
    cos = np.cos(product * (2.0 * np.pi / N))
    sin = np.sin(product * (2.0 * np.pi / N))
    alternate = cos[:, H]
    columns = np.concatenate([cos[:, :H], -sin[:, :H]], axis=1)
    columns[:, 0] = 0.0
    columns[:, H] = alternate
    ahead = np.concatenate([cos[:H], sin[:H]], axis=0)
    ahead[H] = alternate
    back = 2.0 * np.concatenate([cos[:, :H], sin[:, :H]], axis=1)
    back[:, 0] = 1.0
    back[:, H] = alternate
    last = 2.0 * np.concatenate([cos[:, :H], -sin[:, :H]], axis=1)
    last[:, 0] = alternate
    last[:, H] = 0.0
    lowered = [a.astype(ml_dtypes.bfloat16) for a in (columns, ahead, back, cos, sin, last)]
    return np.stack(lowered)


def dot(a, b):
    return jnp.dot(a, b, preferred_element_type=f32)


def column_stats(x):
    mean = jnp.sum(x, axis=1, keepdims=True) * (1.0 / N)
    low = x - mean
    return low.astype(bf16), mean, jnp.sum(low * low, axis=1, keepdims=True)


def side_rows(means, energies):
    lane = lax.broadcasted_iota(jnp.int32, (COLS, H), 1)
    block = jnp.zeros((COLS, H), f32)
    for at, value in enumerate(means + energies):
        block = jnp.where(lane == at, value, block)
    block = jnp.concatenate([block, jnp.zeros((N - COLS, H), f32)], axis=0)
    return jnp.transpose(block)[:8]


def windows(own, left, right, at):
    row = lax.broadcasted_iota(jnp.int32, (8, N), 0)
    lane = lax.broadcasted_iota(jnp.int32, (8, N), 1)
    patch = row % PC
    begin = patch * STRIDE + (N - HALO)
    from_left = (patch < PC - 1) & (lane >= begin)
    from_right = (lane >= COLS) | ((patch == PC - 1) & (lane < begin - N))

    def spread(side):
        return jnp.where(row < PC, side[at : at + 1], side[at + 1 : at + 2])

    return jnp.where(from_left, spread(left), jnp.where(from_right, spread(right), spread(own)))


def centre(own, left, right):
    means = windows(own, left, right, 0)
    means = means - jnp.sum(means, axis=1, keepdims=True) * (1.0 / N)
    energies = windows(own, left, right, 2) + N * means * means
    return N * means, jnp.sum(energies, axis=1, keepdims=True)


def mixed(upper, lower, split):
    row = lax.broadcasted_iota(jnp.int32, upper.shape, 0)
    return jnp.where(row < split, upper.astype(f32), lower.astype(f32)).astype(bf16)


def patch_of(j, level, own, left, right):
    if j == 0:
        parts = [
            own[level, 0:144],
            mixed(own[level, 144:160], left[level, 0:16], 4),
            left[level, 16:112],
        ]
    elif j == 1:
        parts = [
            own[level, 0:160],
            right[level, 0:16],
            mixed(right[level, 16:32], left[level, 32:48], 12),
            left[level, 48:112],
        ]
    elif j == 2:
        parts = [
            own[level, 0:160],
            right[level, 0:64],
            mixed(right[level, 64:80], left[level, 80:96], 4),
            left[level, 96:112],
        ]
    else:
        parts = [
            mixed(right[level, 96:112], own[level, 0:16], 12),
            own[level, 16:160],
            right[level, 0:96],
        ]
    return jnp.concatenate(parts, axis=0)


def cross(now, prev, out):
    step = 16
    for begin in range(0, H, step):
        even, odd = pl.ds(begin, step), pl.ds(H + begin, step)
        a_er, a_ei, a_oi, a_or = now[even, :H], now[even, H:], now[odd, :H], now[odd, H:]
        b_er, b_ei, b_oi, b_or = prev[even, :H], prev[even, H:], prev[odd, :H], prev[odd, H:]
        ee_r = a_er * b_er + a_ei * b_ei
        ee_i = a_ei * b_er - a_er * b_ei
        oo_r = a_or * b_or + a_oi * b_oi
        oo_i = a_or * b_oi - a_oi * b_or
        odd_r = (a_er * b_or - a_ei * b_oi) + (a_or * b_er - a_oi * b_ei)
        minus_i = (a_oi * b_er + a_or * b_ei) - (a_ei * b_or + a_er * b_oi)
        if begin == 0:
            first = lax.broadcasted_iota(jnp.int32, (step, H), 0) == 0
            even_r = jnp.where(first, ee_r, ee_r + oo_r)
            even_i = jnp.where(first, ee_i, ee_i + oo_i)
            minus_i = jnp.where(first, oo_r, minus_i)
            odd_r = jnp.where(first, oo_i, odd_r)
        else:
            even_r, even_i = ee_r + oo_r, ee_i + oo_i
        out[even, :H] = even_r.astype(bf16)
        out[even, H:] = even_i.astype(bf16)
        out[odd, :H] = minus_i.astype(bf16)
        out[odd, H:] = odd_r.astype(bf16)


def first_kernel(
    n_sec,
    n_tile,
    x_hbm,
    prior_hbm,
    table_hbm,
    turned_out,
    rows_out,
    table,
    spec_later,
    b_own,
    b_left,
    b_right,
    x,
    prior,
    a_own,
    a_left,
    a_right,
    side,
    side_out,
    side_in,
    b_side,
    r_own,
    r_side,
    spec_a,
    spec_last,
    spec_b,
    crossed,
    rows,
    load_sem,
    send_sem,
    recv_sem,
    ready_sem,
):
    s, t = lax.axis_index("sec"), lax.axis_index("tile")
    has_left, has_right = t > 0, t < n_tile - 1
    has_next, has_prev = s < n_sec - 1, s > 0
    middle = n_tile // 2
    at_middle, before_middle = t == middle, t == middle - 1
    elsewhere = jnp.logical_not(at_middle)
    crossing = (s % 2 == 1) & has_next
    left_past = at_middle & crossing
    step = t % middle
    split, before_split = at_middle & (s != n_sec // 2), before_middle & (s != n_sec // 2)
    joined = jnp.logical_not(split)
    early = at_middle & (s != n_sec // 2)
    not_early = jnp.logical_not(early)
    far, far_next = s == n_sec // 2 - 1, s == n_sec // 2
    back_out = far & (step >= 1) & (step <= middle // 2)
    back_in = far_next & (step < middle // 2)
    back_past = far & ((step < middle // 2) | before_middle)
    late_out, late_in = far & before_middle, far_next & before_middle
    over_out, over_in = far & at_middle, late_in
    relay_out, relay_in = crossing & before_middle, crossing & (t == n_tile - 1)
    edge_out, edge_in = relay_out & jnp.logical_not(far), relay_in & jnp.logical_not(far)
    tile_out, tile_in = relay_out & far, relay_in & far
    not_tile_out = jnp.logical_not(tile_out)
    first_patches = at_middle & (s % 2 == 0) & has_prev
    to_left, to_right, to_next = {"tile": t - 1}, {"tile": t + 1}, {"sec": s + 1}

    def load(source, target, at):
        return pltpu.make_async_copy(source, target, load_sem.at[at])

    load_x = [load(x_hbm.at[i], x.at[i], i) for i in range(LEVELS)]
    load_first = load(table_hbm.at[0], table.at[0], 2)
    load_rest = load(table_hbm.at[1:6], table.at[1:6], 3)
    load_prior = load(prior_hbm, prior, 4)
    load_x[0].start()
    load_x[1].start()
    load_first.start()
    load_rest.start()

    barrier = pltpu.get_barrier_semaphore()

    def greet(there, device):
        @pl.when(there)
        def _():
            pl.semaphore_signal(barrier, inc=1, device_id=device, device_id_type=MESH)

    greet(has_left, to_left)
    greet(has_right & jnp.logical_not(before_split), to_right)
    greet(has_prev & jnp.logical_not(late_in), {"sec": s - 1})
    greet(late_out, to_next)
    greet(back_in, {"sec": s - 1, "tile": t + 1})
    greet(first_patches & far_next, {"sec": s - 1, "tile": t - 1})
    greet(relay_in, {"tile": middle - 1})
    relayed = (first_patches & jnp.logical_not(far_next)) | late_in
    greet(relayed, {"sec": s - 1, "tile": n_tile - 1})
    greet(over_out, {"sec": s + 1, "tile": t - 1})

    @pl.when(s == 0)
    def _():
        load_prior.start()

    started = {}
    count = [0]

    def note(there, copy):
        started.setdefault(id(there), (there, []))[1].append(copy)

    def settle(groups):
        for there, copies in list(groups.values()):

            @pl.when(there)
            def _(copies=copies):
                for copy in copies:
                    copy.wait_send()

        groups.clear()

    def remote(source, target, device, arrival):
        at = count[0]
        count[0] += 1
        return pltpu.make_async_remote_copy(
            src_ref=source,
            dst_ref=target,
            send_sem=send_sem.at[at],
            recv_sem=recv_sem.at[arrival],
            device_id=device,
            device_id_type=MESH,
        )

    def send(there, *what):
        copy = remote(*what)
        pl.when(there)(copy.start)
        note(there, copy)

    def arrived(there, target, arrival):
        copy = pltpu.make_async_remote_copy(
            src_ref=target,
            dst_ref=target,
            send_sem=send_sem.at[0],
            recv_sem=recv_sem.at[arrival],
            device_id=to_next,
            device_id_type=MESH,
        )
        if there is None:
            copy.wait_recv()
        else:
            pl.when(there)(copy.wait_recv)

    @pl.when(jnp.logical_not(has_left))
    def _():
        a_left[...] = jnp.zeros_like(a_left)
        b_left[...] = jnp.zeros_like(b_left)
        side_in[0] = jnp.zeros((8, N), f32)
        b_side[1] = jnp.zeros((8, N), f32)

    @pl.when(jnp.logical_not(has_right))
    def _():
        a_right[...] = jnp.zeros_like(a_right)
        b_right[...] = jnp.zeros_like(b_right)
        side_in[1] = jnp.zeros((8, N), f32)
        b_side[2] = jnp.zeros((8, N), f32)

    low, high = pl.ds(0, EDGE), pl.ds(COLS - EDGE, EDGE)
    to_direct, to_back = {"sec": s + 1, "tile": t + 1}, {"sec": s + 1, "tile": t - 1}
    to_last, to_middle = {"tile": n_tile - 1}, {"sec": s + 1, "tile": middle}
    to_before = {"sec": s + 1, "tile": middle - 1}

    def prepare(there, *what):
        copy = remote(*what)
        note(there, copy)
        return lambda when: pl.when(when & there)(copy.start)

    def columns_to(i):
        right = prepare(has_right, a_own.at[i, high], a_left.at[i], to_right, i)
        left = prepare(has_left, a_own.at[i, low], a_right.at[i], to_left, 2 + i)
        return right, left

    def send_columns(i):
        send(back_out, a_own.at[i, low], b_right.at[i], to_back, 8 + i)
        send(tile_out, a_own.at[i, high], b_left.at[i], to_direct, 6 + i)
        send(tile_out, a_own.at[i], r_own.at[i], to_last, 15 + i)
        right, left = to_sides[i]
        right(not_tile_out)
        send(edge_out, a_own.at[i, high], r_own.at[i, high], to_last, 15 + i)
        left(joined)
    to_sides = [columns_to(i) for i in range(LEVELS)]
    lowered, stats = [], []
    for i in range(LEVELS):
        load_x[i].wait()
        low_i, *stat = column_stats(x[i])
        lowered.append(low_i)
        stats.append(stat)
    own_side = side_rows(*zip(*stats))
    side[...] = own_side
    side_out[0] = pltpu.roll(own_side, N - COLS, 1)
    side_out[1] = pltpu.roll(own_side, COLS, 1)
    load_first.wait()
    a_own[0] = dot(lowered[0], table[0]).astype(bf16)

    known = [has_left & joined, has_right, has_next & jnp.logical_not(late_out)]
    known += [relay_out, tile_out, relay_in, back_out, late_in, over_in]
    pl.semaphore_wait(barrier, sum(v.astype(jnp.int32) for v in known))

    @pl.when(before_split)
    def _():
        pl.semaphore_signal(ready_sem.at[1], inc=1, device_id=to_right, device_id_type=MESH)

    @pl.when(over_in)
    def _():
        pl.semaphore_signal(
            ready_sem.at[2],
            inc=1,
            device_id={"sec": s - 1, "tile": t + 1},
            device_id_type=MESH,
        )

    @pl.when(late_in)
    def _():
        pl.semaphore_signal(
            ready_sem.at[0], inc=1, device_id={"sec": s - 1}, device_id_type=MESH
        )

    send(back_out, side_out.at[1], b_side.at[2], to_back, 14)
    send(has_right, side_out.at[0], side_in.at[0], to_right, 10)
    send(tile_out, side_out.at[0], b_side.at[1], to_direct, 13)
    send(edge_out, side_out.at[0], r_side, to_last, 17)
    side_left = prepare(has_left, side_out.at[1], side_in.at[1], to_left, 11)
    side_left(joined)
    send_columns(0)
    a_own[1] = dot(lowered[1], table[0]).astype(bf16)
    send_columns(1)
    for right, _ in to_sides:
        right(tile_out)

    send(tile_out, side, r_side, to_last, 17)
    own_on = has_next & not_tile_out

    for i in range(LEVELS):
        send(own_on, a_own.at[i], b_own.at[i], to_next, 4 + i)
    send(own_on, side, b_side.at[0], to_next, 12)

    for i in range(LEVELS):
        arrived(edge_in, r_own.at[i, high], 15 + i)
        send(edge_in, r_own.at[i, high], b_left.at[i], to_middle, 6 + i)
        arrived(tile_in, r_own.at[i], 15 + i)
        send(tile_in, r_own.at[i], b_own.at[i], to_before, 4 + i)
        if i == 0:
            arrived(edge_in, r_side, 17)
            send(edge_in, r_side, b_side.at[1], to_middle, 13)
    arrived(tile_in, r_side, 17)
    send(tile_in, r_side, b_side.at[0], to_before, 12)

    @pl.when(split)
    def _():
        pl.semaphore_wait(ready_sem.at[1], 1)

    side_left(split)
    for _, left in to_sides:
        left(split)

    @pl.when(s == 0)
    def _():
        load_prior.wait()
        prior_stats = []
        for i in range(LEVELS):
            low_i, *stat = column_stats(prior[i])
            b_own[i] = dot(low_i, table[0]).astype(bf16)
            prior_stats.append(stat)
        prior_side = side_rows(*zip(*prior_stats))
        b_side[0] = prior_side
        side_out[2] = pltpu.roll(prior_side, N - COLS, 1)
        side_out[3] = pltpu.roll(prior_side, COLS, 1)

    first_right, first_left = (s == 0) & has_right, (s == 0) & has_left
    send(first_right, side_out.at[2], b_side.at[1], to_right, 13)
    send(first_left, side_out.at[3], b_side.at[2], to_left, 14)
    for i in range(LEVELS):
        send(first_right, b_own.at[i, high], b_left.at[i], to_right, 6 + i)
        send(first_left, b_own.at[i, low], b_right.at[i], to_left, 8 + i)

    @pl.when(late_out)
    def _():
        pl.semaphore_wait(ready_sem.at[0], 1)

    left_on = has_next & has_left & jnp.logical_not(left_past)
    right_on = has_next & has_right & jnp.logical_not(back_past)

    passed = {}
    last_waits = dict(started)
    started.clear()

    def pass_on(when, there, on, source, arrival, target, further):
        arrived(when & there, source, arrival)
        if arrival not in passed:
            passed[arrival] = remote(source, target, to_next, further)
            if arrival != 1:
                note(on, passed[arrival])
        pl.when(when & on)(passed[arrival].start)

    def pass_left(i):
        pass_on(True, has_left, left_on, a_left.at[i], i, b_left.at[i], 6 + i)

    def pass_right(when, i):
        pass_on(when, has_right, right_on, a_right.at[i], 2 + i, b_right.at[i], 8 + i)

    def pass_right_side(when):
        pass_on(when, has_right, right_on, side_in.at[1], 11, b_side.at[2], 14)

    def begin_spectra():
        for j in range(PC - 1):
            spec_a[j] = dot(table[1], patch_of(j, 0, a_own, a_left, a_right))

    def previous_right(i):
        arrived(has_prev, b_own.at[i], 4 + i)
        arrived(has_right, b_right.at[i], 8 + i)

    def last_patches(*levels):
        for i in levels:
            spec_last[i] = dot(table[1], patch_of(PC - 1, i, a_own, a_left, a_right))
            spec_b[PC - 1 + i] = dot(table[1], patch_of(PC - 1, i, b_own, b_left, b_right))
        for i in levels:
            cross(spec_last.at[i], spec_b.at[PC - 1 + i], crossed.at[PC - 1 + i])
        for i in levels:
            turned_out[PC - 1 + i] = dot(table[2], crossed[PC - 1 + i]).astype(bf16)

    upper = (step >= middle // 2) & jnp.logical_not(before_middle)
    load_rest.wait()
    pass_right(at_middle, 0)
    pass_right(at_middle, 1)
    pass_right_side(at_middle)

    @pl.when(early)
    def _():
        previous_right(0)
        previous_right(1)
        last_patches(0, 1)

    @pl.when(over_out)
    def _():
        pl.semaphore_wait(ready_sem.at[2], 1)

    send(over_out, side_out.at[1], b_side.at[2], to_back, 14)
    for i in range(LEVELS):
        send(over_out, a_own.at[i, low], b_right.at[i], to_back, 8 + i)

    pass_on(True, has_left, left_on, side_in.at[0], 10, b_side.at[1], 13)
    pass_right_side(upper)
    pass_left(0)
    pass_right(upper, 0)
    pl.when(at_middle)(begin_spectra)
    pass_left(1)
    pass_right(elsewhere & jnp.logical_not(upper), 0)
    pass_right(elsewhere, 1)
    pass_right_side(elsewhere & jnp.logical_not(upper))
    pl.when(elsewhere)(begin_spectra)

    settle(last_waits)
    arrived(has_prev, b_side.at[0], 12)
    arrived(has_right, b_side.at[2], 14)
    arrived(has_left, b_side.at[1], 13)
    for j in range(PC - 1):
        spec_later[j] = dot(table[1], patch_of(j, 1, a_own, a_left, a_right))
    a_flat, a_energy = centre(side[...], side_in[0], side_in[1])
    b_flat, b_energy = centre(b_side[0], b_side[1], b_side[2])
    pair = jnp.concatenate([a_flat, b_flat], axis=0).astype(bf16)
    even_part, odd_part = dot(pair, table[3]), dot(pair, table[4])
    a_e, b_e, a_o, b_o = even_part[:8], even_part[8:], odd_part[:8], odd_part[8:]
    both = jnp.concatenate([a_e * b_e + a_o * b_o, a_e * b_o - a_o * b_e], axis=0).astype(bf16)
    flat = dot(both, table[3])[:8] - dot(both, table[4])[8:]
    scale = 1.0 / (N * jnp.sqrt(a_energy + EPS) * jnp.sqrt(b_energy + EPS))
    rows[0:8] = flat * scale
    rows[8:16] = jnp.broadcast_to(scale, (8, N))
    rows_out[...] = rows[...]

    pl.when(not_early)(lambda: previous_right(0))
    arrived(has_left, b_left.at[0], 6)
    for j in range(PC - 1):
        spec_b[j] = dot(table[1], patch_of(j, 0, b_own, b_left, b_right))
    for j in range(PC - 1):
        cross(spec_a.at[j], spec_b.at[j], crossed.at[j])
    for j in range(PC - 1):
        turned_out[j] = dot(table[2], crossed[j]).astype(bf16)

    @pl.when(not_early)
    def _():
        previous_right(1)
        last_patches(0, 1)

    settle(started)
    arrived(has_left, b_left.at[1], 7)
    pl.when(left_on)(passed[1].wait_send)


def finished(turned, table, rows, p):
    product = lax.dot_general(
        table[5], turned, (((1,), (1,)), ((), ())), preferred_element_type=f32
    )
    return product * rows[8 + p : 9 + p] + rows[p : p + 1]


def last_kernel(
    before, rows, table, spec_a, b_own, b_left, b_right, out_hbm, spec_b, crossed, turned, maps, sem
):
    copies = []

    def write(source, p):
        copy = pltpu.make_async_copy(source, out_hbm.at[p], sem.at[p])
        copy.start()
        copies.append(copy)

    for j in range(PC - 1):
        spec_b[j] = dot(table[1], patch_of(j, 1, b_own, b_left, b_right))
    for j in range(PC + 1):
        p = j if j < PC else 2 * PC - 1
        maps[p] = finished(before[j], table, rows, p)
        write(maps.at[p], p)
    for j in range(PC - 1):
        cross(spec_a.at[j], spec_b.at[j], crossed.at[j])
        turned[j] = dot(table[2], crossed[j]).astype(bf16)
    for j in range(PC - 1):
        maps[PC + j] = finished(turned[j], table, rows, PC + j)
        write(maps.at[PC + j], PC + j)
    for copy in copies:
        copy.wait()


def local(n_sec, n_tile, sections, prior):
    x = jnp.swapaxes(sections[0], 1, 2)
    before = jnp.swapaxes(prior, 1, 2)
    hbm = pl.BlockSpec(memory_space=pltpu.HBM)
    vmem = pl.BlockSpec(memory_space=pltpu.VMEM)
    patches = LEVELS * PC
    columns = lambda rows: pltpu.VMEM((LEVELS, rows, N), bf16)
    held = lambda *shape: jax.ShapeDtypeStruct(shape, bf16)
    operands = (x, before, jnp.asarray(tables()))
    results = pl.pallas_call(
        functools.partial(first_kernel, n_sec, n_tile),
        out_shape=(
            held(PC + 1, N, N),
            jax.ShapeDtypeStruct((16, N), f32),
            held(6, N, N),
            jax.ShapeDtypeStruct((PC - 1, N, N), f32),
            held(LEVELS, COLS, N),
            held(LEVELS, EDGE, N),
            held(LEVELS, EDGE, N),
        ),
        in_specs=[hbm] * 3,
        out_specs=(vmem,) * 7,
        scratch_shapes=[
            pltpu.VMEM((LEVELS, COLS, N), f32),
            pltpu.VMEM((LEVELS, COLS, N), f32),
            columns(COLS),
            columns(EDGE),
            columns(EDGE),
            pltpu.VMEM((8, N), f32),
            pltpu.VMEM((4, 8, N), f32),
            pltpu.VMEM((2, 8, N), f32),
            pltpu.VMEM((3, 8, N), f32),
            columns(COLS),
            pltpu.VMEM((8, N), f32),
            pltpu.VMEM((PC - 1, N, N), f32),
            pltpu.VMEM((LEVELS, N, N), f32),
            pltpu.VMEM((PC + 1, N, N), f32),
            pltpu.VMEM((PC + 1, N, N), bf16),
            pltpu.VMEM((16, N), f32),
            pltpu.SemaphoreType.DMA((5,)),
            pltpu.SemaphoreType.DMA((47,)),
            pltpu.SemaphoreType.DMA((18,)),
            pltpu.SemaphoreType.REGULAR((3,)),
        ],
        compiler_params=pltpu.CompilerParams(
            collective_id=0, has_side_effects=True, vmem_limit_bytes=16 * 2**20
        ),
        name="spectra",
    )(*(pltpu.with_memory_space_constraint(v, pltpu.HBM) for v in operands))
    maps = pl.pallas_call(
        last_kernel,
        out_shape=jax.ShapeDtypeStruct((patches, N, N), f32),
        in_specs=[vmem] * 7,
        out_specs=hbm,
        scratch_shapes=[
            pltpu.VMEM((PC - 1, N, N), f32),
            pltpu.VMEM((PC - 1, N, N), bf16),
            pltpu.VMEM((PC - 1, N, N), bf16),
            pltpu.VMEM((patches, N, N), f32),
            pltpu.SemaphoreType.DMA((patches,)),
        ],
        compiler_params=pltpu.CompilerParams(vmem_limit_bytes=16 * 2**20),
        name="maps",
    )(*results)
    return maps.reshape(1, LEVELS, 1, PC, N, N)


def solution(mesh):
    return jax.shard_map(
        functools.partial(local, mesh.shape["sec"], mesh.shape["tile"]),
        mesh=mesh,
        in_specs=(P("sec", None, None, "tile"), P(None, None, "tile")),
        out_specs=P("sec", None, None, "tile", None, None),
        check_vma=False,
    )
```

```python
import functools

import jax
import jax.numpy as jnp
import ml_dtypes
import numpy as np
from jax import lax
from jax.experimental import pallas as pl
from jax.experimental.pallas import tpu as pltpu
from jax.sharding import PartitionSpec as P

N = 256
H = 128
STRIDE = 40
PC = 4
HALO = 108
LEVELS = 2
COLS = 160
EDGE = 112
EPS = 1e-06
MESH = pl.DeviceIdType.MESH
f32, bf16 = jnp.float32, jnp.bfloat16


def tables():
    i = np.arange(N)
    product = i[:, None] * i[None, :] % N
    cos = np.cos(product * (2.0 * np.pi / N))
    sin = np.sin(product * (2.0 * np.pi / N))
    alternate = cos[:, H]
    columns = np.concatenate([cos[:, :H], -sin[:, :H]], axis=1)
    columns[:, 0] = 0.0
    columns[:, H] = alternate
    ahead = np.concatenate([cos[:H], sin[:H]], axis=0)
    ahead[H] = alternate
    back = 2.0 * np.concatenate([cos[:, :H], sin[:, :H]], axis=1)
    back[:, 0] = 1.0
    back[:, H] = alternate
    last = 2.0 * np.concatenate([cos[:, :H], -sin[:, :H]], axis=1)
    last[:, 0] = alternate
    last[:, H] = 0.0
    lowered = [a.astype(ml_dtypes.bfloat16) for a in (columns, ahead, back, cos, sin, last)]
    return np.stack(lowered)


def dot(a, b):
    return jnp.dot(a, b, preferred_element_type=f32)


def column_stats(x):
    mean = jnp.sum(x, axis=1, keepdims=True) * (1.0 / N)
    low = x - mean
    return low.astype(bf16), mean, jnp.sum(low * low, axis=1, keepdims=True)


def side_rows(means, energies):
    lane = lax.broadcasted_iota(jnp.int32, (COLS, H), 1)
    block = jnp.zeros((COLS, H), f32)
    for at, value in enumerate(means + energies):
        block = jnp.where(lane == at, value, block)
    block = jnp.concatenate([block, jnp.zeros((N - COLS, H), f32)], axis=0)
    return jnp.transpose(block)[:8]


def windows(own, left, right, at):
    row = lax.broadcasted_iota(jnp.int32, (8, N), 0)
    lane = lax.broadcasted_iota(jnp.int32, (8, N), 1)
    patch = row % PC
    begin = patch * STRIDE + (N - HALO)
    from_left = (patch < PC - 1) & (lane >= begin)
    from_right = (lane >= COLS) | ((patch == PC - 1) & (lane < begin - N))

    def spread(side):
        return jnp.where(row < PC, side[at : at + 1], side[at + 1 : at + 2])

    return jnp.where(from_left, spread(left), jnp.where(from_right, spread(right), spread(own)))


def centre(own, left, right):
    means = windows(own, left, right, 0)
    means = means - jnp.sum(means, axis=1, keepdims=True) * (1.0 / N)
    energies = windows(own, left, right, 2) + N * means * means
    return N * means, jnp.sum(energies, axis=1, keepdims=True)


def mixed(upper, lower, split):
    row = lax.broadcasted_iota(jnp.int32, upper.shape, 0)
    return jnp.where(row < split, upper.astype(f32), lower.astype(f32)).astype(bf16)


def patch_of(j, level, own, left, right):
    if j == 0:
        parts = [
            own[level, 0:144],
            mixed(own[level, 144:160], left[level, 0:16], 4),
            left[level, 16:112],
        ]
    elif j == 1:
        parts = [
            own[level, 0:160],
            right[level, 0:16],
            mixed(right[level, 16:32], left[level, 32:48], 12),
            left[level, 48:112],
        ]
    elif j == 2:
        parts = [
            own[level, 0:160],
            right[level, 0:64],
            mixed(right[level, 64:80], left[level, 80:96], 4),
            left[level, 96:112],
        ]
    else:
        parts = [
            mixed(right[level, 96:112], own[level, 0:16], 12),
            own[level, 16:160],
            right[level, 0:96],
        ]
    return jnp.concatenate(parts, axis=0)


def cross(now, prev, out):
    step = 16
    for begin in range(0, H, step):
        even, odd = pl.ds(begin, step), pl.ds(H + begin, step)
        a_er, a_ei, a_oi, a_or = now[even, :H], now[even, H:], now[odd, :H], now[odd, H:]
        b_er, b_ei, b_oi, b_or = prev[even, :H], prev[even, H:], prev[odd, :H], prev[odd, H:]
        ee_r = a_er * b_er + a_ei * b_ei
        ee_i = a_ei * b_er - a_er * b_ei
        oo_r = a_or * b_or + a_oi * b_oi
        oo_i = a_or * b_oi - a_oi * b_or
        odd_r = (a_er * b_or - a_ei * b_oi) + (a_or * b_er - a_oi * b_ei)
        minus_i = (a_oi * b_er + a_or * b_ei) - (a_ei * b_or + a_er * b_oi)
        if begin == 0:
            first = lax.broadcasted_iota(jnp.int32, (step, H), 0) == 0
            even_r = jnp.where(first, ee_r, ee_r + oo_r)
            even_i = jnp.where(first, ee_i, ee_i + oo_i)
            minus_i = jnp.where(first, oo_r, minus_i)
            odd_r = jnp.where(first, oo_i, odd_r)
        else:
            even_r, even_i = ee_r + oo_r, ee_i + oo_i
        out[even, :H] = even_r.astype(bf16)
        out[even, H:] = even_i.astype(bf16)
        out[odd, :H] = minus_i.astype(bf16)
        out[odd, H:] = odd_r.astype(bf16)


def first_kernel(
    n_sec,
    n_tile,
    x_hbm,
    prior_hbm,
    table_hbm,
    turned_out,
    rows_out,
    table,
    spec_later,
    b_own,
    b_left,
    b_right,
    x,
    prior,
    a_own,
    a_left,
    a_right,
    side,
    side_out,
    side_in,
    b_side,
    r_own,
    r_side,
    spec_a,
    spec_last,
    spec_b,
    crossed,
    rows,
    load_sem,
    send_sem,
    recv_sem,
    ready_sem,
):
    s, t = lax.axis_index("sec"), lax.axis_index("tile")
    has_left, has_right = t > 0, t < n_tile - 1
    has_next, has_prev = s < n_sec - 1, s > 0
    middle = n_tile // 2
    at_middle, before_middle = t == middle, t == middle - 1
    elsewhere = jnp.logical_not(at_middle)
    crossing = (s % 2 == 1) & has_next
    left_past = at_middle & crossing
    step = t % middle
    split, before_split = at_middle & (s != n_sec // 2), before_middle & (s != n_sec // 2)
    joined = jnp.logical_not(split)
    early = at_middle & (s != n_sec // 2)
    not_early = jnp.logical_not(early)
    far, far_next = s == n_sec // 2 - 1, s == n_sec // 2
    back_out = far & (step >= 1) & (step <= middle // 2)
    back_in = far_next & (step < middle // 2)
    back_past = far & ((step < middle // 2) | before_middle)
    late_out, late_in = far & before_middle, far_next & before_middle
    over_out, over_in = far & at_middle, late_in
    relay_out, relay_in = crossing & before_middle, crossing & (t == n_tile - 1)
    edge_out, edge_in = relay_out & jnp.logical_not(far), relay_in & jnp.logical_not(far)
    tile_out, tile_in = relay_out & far, relay_in & far
    not_tile_out = jnp.logical_not(tile_out)
    first_patches = at_middle & (s % 2 == 0) & has_prev
    to_left, to_right, to_next = {"tile": t - 1}, {"tile": t + 1}, {"sec": s + 1}

    def load(source, target, at):
        return pltpu.make_async_copy(source, target, load_sem.at[at])

    load_x = [load(x_hbm.at[i], x.at[i], i) for i in range(LEVELS)]
    load_first = load(table_hbm.at[0], table.at[0], 2)
    load_rest = load(table_hbm.at[1:6], table.at[1:6], 3)
    load_prior = load(prior_hbm, prior, 4)
    load_x[0].start()
    load_x[1].start()
    load_first.start()
    load_rest.start()

    barrier = pltpu.get_barrier_semaphore()

    def greet(there, device):
        @pl.when(there)
        def _():
            pl.semaphore_signal(barrier, inc=1, device_id=device, device_id_type=MESH)

    greet(has_left, to_left)
    greet(has_right & jnp.logical_not(before_split), to_right)
    greet(has_prev & jnp.logical_not(late_in), {"sec": s - 1})
    greet(late_out, to_next)
    greet(back_in, {"sec": s - 1, "tile": t + 1})
    greet(first_patches & far_next, {"sec": s - 1, "tile": t - 1})
    greet(relay_in, {"tile": middle - 1})
    relayed = (first_patches & jnp.logical_not(far_next)) | late_in
    greet(relayed, {"sec": s - 1, "tile": n_tile - 1})
    greet(over_out, {"sec": s + 1, "tile": t - 1})

    @pl.when(s == 0)
    def _():
        load_prior.start()

    started = {}
    count = [0]

    def note(there, copy):
        started.setdefault(id(there), (there, []))[1].append(copy)

    def settle(groups):
        for there, copies in list(groups.values()):

            @pl.when(there)
            def _(copies=copies):
                for copy in copies:
                    copy.wait_send()

        groups.clear()

    def remote(source, target, device, arrival):
        at = count[0]
        count[0] += 1
        return pltpu.make_async_remote_copy(
            src_ref=source,
            dst_ref=target,
            send_sem=send_sem.at[at],
            recv_sem=recv_sem.at[arrival],
            device_id=device,
            device_id_type=MESH,
        )

    def send(there, *what):
        copy = remote(*what)
        pl.when(there)(copy.start)
        note(there, copy)

    def arrived(there, target, arrival):
        copy = pltpu.make_async_remote_copy(
            src_ref=target,
            dst_ref=target,
            send_sem=send_sem.at[0],
            recv_sem=recv_sem.at[arrival],
            device_id=to_next,
            device_id_type=MESH,
        )
        if there is None:
            copy.wait_recv()
        else:
            pl.when(there)(copy.wait_recv)

    @pl.when(jnp.logical_not(has_left))
    def _():
        a_left[...] = jnp.zeros_like(a_left)
        b_left[...] = jnp.zeros_like(b_left)
        side_in[0] = jnp.zeros((8, N), f32)
        b_side[1] = jnp.zeros((8, N), f32)

    @pl.when(jnp.logical_not(has_right))
    def _():
        a_right[...] = jnp.zeros_like(a_right)
        b_right[...] = jnp.zeros_like(b_right)
        side_in[1] = jnp.zeros((8, N), f32)
        b_side[2] = jnp.zeros((8, N), f32)

    low, high = pl.ds(0, EDGE), pl.ds(COLS - EDGE, EDGE)
    to_direct, to_back = {"sec": s + 1, "tile": t + 1}, {"sec": s + 1, "tile": t - 1}
    to_last, to_middle = {"tile": n_tile - 1}, {"sec": s + 1, "tile": middle}
    to_before = {"sec": s + 1, "tile": middle - 1}

    def prepare(there, *what):
        copy = remote(*what)
        note(there, copy)
        return lambda when: pl.when(when & there)(copy.start)

    def columns_to(i):
        right = prepare(has_right, a_own.at[i, high], a_left.at[i], to_right, i)
        left = prepare(has_left, a_own.at[i, low], a_right.at[i], to_left, 2 + i)
        return right, left

    def send_columns(i):
        send(back_out, a_own.at[i, low], b_right.at[i], to_back, 8 + i)
        send(tile_out, a_own.at[i, high], b_left.at[i], to_direct, 6 + i)
        send(tile_out, a_own.at[i], r_own.at[i], to_last, 15 + i)
        right, left = to_sides[i]
        right(not_tile_out)
        send(edge_out, a_own.at[i, high], r_own.at[i, high], to_last, 15 + i)
        left(joined & jnp.logical_not(before_middle))
    to_sides = [columns_to(i) for i in range(LEVELS)]
    lowered, stats = [], []
    for i in range(LEVELS):
        load_x[i].wait()
        low_i, *stat = column_stats(x[i])
        lowered.append(low_i)
        stats.append(stat)
    own_side = side_rows(*zip(*stats))
    side[...] = own_side
    side_out[0] = pltpu.roll(own_side, N - COLS, 1)
    side_out[1] = pltpu.roll(own_side, COLS, 1)
    load_first.wait()
    a_own[0] = dot(lowered[0], table[0]).astype(bf16)

    known = [has_left & joined, has_right, has_next & jnp.logical_not(late_out)]
    known += [relay_out, tile_out, relay_in, back_out, late_in, over_in]
    pl.semaphore_wait(barrier, sum(v.astype(jnp.int32) for v in known))

    @pl.when(before_split)
    def _():
        pl.semaphore_signal(ready_sem.at[1], inc=1, device_id=to_right, device_id_type=MESH)

    @pl.when(over_in)
    def _():
        pl.semaphore_signal(
            ready_sem.at[2],
            inc=1,
            device_id={"sec": s - 1, "tile": t + 1},
            device_id_type=MESH,
        )

    @pl.when(late_in)
    def _():
        pl.semaphore_signal(
            ready_sem.at[0], inc=1, device_id={"sec": s - 1}, device_id_type=MESH
        )

    send(back_out, side_out.at[1], b_side.at[2], to_back, 14)
    send(has_right, side_out.at[0], side_in.at[0], to_right, 10)
    send(tile_out, side_out.at[0], b_side.at[1], to_direct, 13)
    send(edge_out, side_out.at[0], r_side, to_last, 17)
    side_left = prepare(has_left, side_out.at[1], side_in.at[1], to_left, 11)
    side_left(joined)
    send_columns(0)
    a_own[1] = dot(lowered[1], table[0]).astype(bf16)
    send_columns(1)
    for right, _ in to_sides:
        right(tile_out)
    for _, left in to_sides:
        left(before_middle)

    send(tile_out, side, r_side, to_last, 17)
    own_on = has_next & not_tile_out

    for i in range(LEVELS):
        send(own_on, a_own.at[i], b_own.at[i], to_next, 4 + i)
    send(own_on, side, b_side.at[0], to_next, 12)

    for i in range(LEVELS):
        arrived(edge_in, r_own.at[i, high], 15 + i)
        send(edge_in, r_own.at[i, high], b_left.at[i], to_middle, 6 + i)
        arrived(tile_in, r_own.at[i], 15 + i)
        send(tile_in, r_own.at[i], b_own.at[i], to_before, 4 + i)
        if i == 0:
            arrived(edge_in, r_side, 17)
            send(edge_in, r_side, b_side.at[1], to_middle, 13)
    arrived(tile_in, r_side, 17)
    send(tile_in, r_side, b_side.at[0], to_before, 12)

    @pl.when(split)
    def _():
        pl.semaphore_wait(ready_sem.at[1], 1)

    side_left(split)
    for _, left in to_sides:
        left(split)

    @pl.when(s == 0)
    def _():
        load_prior.wait()
        prior_stats = []
        for i in range(LEVELS):
            low_i, *stat = column_stats(prior[i])
            b_own[i] = dot(low_i, table[0]).astype(bf16)
            prior_stats.append(stat)
        prior_side = side_rows(*zip(*prior_stats))
        b_side[0] = prior_side
        side_out[2] = pltpu.roll(prior_side, N - COLS, 1)
        side_out[3] = pltpu.roll(prior_side, COLS, 1)

    first_right, first_left = (s == 0) & has_right, (s == 0) & has_left
    send(first_right, side_out.at[2], b_side.at[1], to_right, 13)
    send(first_left, side_out.at[3], b_side.at[2], to_left, 14)
    for i in range(LEVELS):
        send(first_right, b_own.at[i, high], b_left.at[i], to_right, 6 + i)
        send(first_left, b_own.at[i, low], b_right.at[i], to_left, 8 + i)

    @pl.when(late_out)
    def _():
        pl.semaphore_wait(ready_sem.at[0], 1)

    left_on = has_next & has_left & jnp.logical_not(left_past)
    right_on = has_next & has_right & jnp.logical_not(back_past)

    passed = {}
    last_waits = dict(started)
    started.clear()

    def pass_on(when, there, on, source, arrival, target, further):
        arrived(when & there, source, arrival)
        if arrival not in passed:
            passed[arrival] = remote(source, target, to_next, further)
            if arrival != 1:
                note(on, passed[arrival])
        pl.when(when & on)(passed[arrival].start)

    def pass_left(i):
        pass_on(True, has_left, left_on, a_left.at[i], i, b_left.at[i], 6 + i)

    def pass_right(when, i):
        pass_on(when, has_right, right_on, a_right.at[i], 2 + i, b_right.at[i], 8 + i)

    def pass_right_side(when):
        pass_on(when, has_right, right_on, side_in.at[1], 11, b_side.at[2], 14)

    def begin_spectra():
        for j in range(PC - 1):
            spec_a[j] = dot(table[1], patch_of(j, 0, a_own, a_left, a_right))

    def previous_right(i):
        arrived(has_prev, b_own.at[i], 4 + i)
        arrived(has_right, b_right.at[i], 8 + i)

    def last_patches(*levels):
        for i in levels:
            spec_last[i] = dot(table[1], patch_of(PC - 1, i, a_own, a_left, a_right))
            spec_b[PC - 1 + i] = dot(table[1], patch_of(PC - 1, i, b_own, b_left, b_right))
        for i in levels:
            cross(spec_last.at[i], spec_b.at[PC - 1 + i], crossed.at[PC - 1 + i])
        for i in levels:
            turned_out[PC - 1 + i] = dot(table[2], crossed[PC - 1 + i]).astype(bf16)

    upper = (step >= middle // 2) & jnp.logical_not(before_middle)
    load_rest.wait()
    pass_right(at_middle, 0)
    pass_right(at_middle, 1)
    pass_right_side(at_middle)

    @pl.when(early)
    def _():
        previous_right(0)
        previous_right(1)
        last_patches(0, 1)

    @pl.when(over_out)
    def _():
        pl.semaphore_wait(ready_sem.at[2], 1)

    send(over_out, side_out.at[1], b_side.at[2], to_back, 14)
    for i in range(LEVELS):
        send(over_out, a_own.at[i, low], b_right.at[i], to_back, 8 + i)

    pass_on(True, has_left, left_on, side_in.at[0], 10, b_side.at[1], 13)
    pass_right_side(upper)
    pass_left(0)
    pass_right(upper, 0)
    pl.when(at_middle)(begin_spectra)
    pass_left(1)
    pass_right(elsewhere & jnp.logical_not(upper), 0)
    pass_right(elsewhere, 1)
    pass_right_side(elsewhere & jnp.logical_not(upper))
    pl.when(elsewhere)(begin_spectra)

    settle(last_waits)
    arrived(has_prev, b_side.at[0], 12)
    arrived(has_right, b_side.at[2], 14)
    arrived(has_left, b_side.at[1], 13)
    for j in range(PC - 1):
        spec_later[j] = dot(table[1], patch_of(j, 1, a_own, a_left, a_right))
    a_flat, a_energy = centre(side[...], side_in[0], side_in[1])
    b_flat, b_energy = centre(b_side[0], b_side[1], b_side[2])
    pair = jnp.concatenate([a_flat, b_flat], axis=0).astype(bf16)
    even_part, odd_part = dot(pair, table[3]), dot(pair, table[4])
    a_e, b_e, a_o, b_o = even_part[:8], even_part[8:], odd_part[:8], odd_part[8:]
    both = jnp.concatenate([a_e * b_e + a_o * b_o, a_e * b_o - a_o * b_e], axis=0).astype(bf16)
    flat = dot(both, table[3])[:8] - dot(both, table[4])[8:]
    scale = 1.0 / (N * jnp.sqrt(a_energy + EPS) * jnp.sqrt(b_energy + EPS))
    rows[0:8] = flat * scale
    rows[8:16] = jnp.broadcast_to(scale, (8, N))
    rows_out[...] = rows[...]

    pl.when(not_early)(lambda: previous_right(0))
    arrived(has_left, b_left.at[0], 6)
    for j in range(PC - 1):
        spec_b[j] = dot(table[1], patch_of(j, 0, b_own, b_left, b_right))
    for j in range(PC - 1):
        cross(spec_a.at[j], spec_b.at[j], crossed.at[j])
    for j in range(PC - 1):
        turned_out[j] = dot(table[2], crossed[j]).astype(bf16)

    @pl.when(not_early)
    def _():
        previous_right(1)
        last_patches(0, 1)

    settle(started)
    arrived(has_left, b_left.at[1], 7)
    pl.when(left_on)(passed[1].wait_send)


def finished(turned, table, rows, p):
    product = lax.dot_general(
        table[5], turned, (((1,), (1,)), ((), ())), preferred_element_type=f32
    )
    return product * rows[8 + p : 9 + p] + rows[p : p + 1]


def last_kernel(
    before, rows, table, spec_a, b_own, b_left, b_right, out_hbm, spec_b, crossed, turned, maps, sem
):
    copies = []

    def write(source, p):
        copy = pltpu.make_async_copy(source, out_hbm.at[p], sem.at[p])
        copy.start()
        copies.append(copy)

    for j in range(PC - 1):
        spec_b[j] = dot(table[1], patch_of(j, 1, b_own, b_left, b_right))
    for j in range(PC + 1):
        p = j if j < PC else 2 * PC - 1
        maps[p] = finished(before[j], table, rows, p)
        write(maps.at[p], p)
    for j in range(PC - 1):
        cross(spec_a.at[j], spec_b.at[j], crossed.at[j])
        turned[j] = dot(table[2], crossed[j]).astype(bf16)
    for j in range(PC - 1):
        maps[PC + j] = finished(turned[j], table, rows, PC + j)
        write(maps.at[PC + j], PC + j)
    for copy in copies:
        copy.wait()


def local(n_sec, n_tile, sections, prior):
    x = jnp.swapaxes(sections[0], 1, 2)
    before = jnp.swapaxes(prior, 1, 2)
    hbm = pl.BlockSpec(memory_space=pltpu.HBM)
    vmem = pl.BlockSpec(memory_space=pltpu.VMEM)
    patches = LEVELS * PC
    columns = lambda rows: pltpu.VMEM((LEVELS, rows, N), bf16)
    held = lambda *shape: jax.ShapeDtypeStruct(shape, bf16)
    operands = (x, before, jnp.asarray(tables()))
    results = pl.pallas_call(
        functools.partial(first_kernel, n_sec, n_tile),
        out_shape=(
            held(PC + 1, N, N),
            jax.ShapeDtypeStruct((16, N), f32),
            held(6, N, N),
            jax.ShapeDtypeStruct((PC - 1, N, N), f32),
            held(LEVELS, COLS, N),
            held(LEVELS, EDGE, N),
            held(LEVELS, EDGE, N),
        ),
        in_specs=[hbm] * 3,
        out_specs=(vmem,) * 7,
        scratch_shapes=[
            pltpu.VMEM((LEVELS, COLS, N), f32),
            pltpu.VMEM((LEVELS, COLS, N), f32),
            columns(COLS),
            columns(EDGE),
            columns(EDGE),
            pltpu.VMEM((8, N), f32),
            pltpu.VMEM((4, 8, N), f32),
            pltpu.VMEM((2, 8, N), f32),
            pltpu.VMEM((3, 8, N), f32),
            columns(COLS),
            pltpu.VMEM((8, N), f32),
            pltpu.VMEM((PC - 1, N, N), f32),
            pltpu.VMEM((LEVELS, N, N), f32),
            pltpu.VMEM((PC + 1, N, N), f32),
            pltpu.VMEM((PC + 1, N, N), bf16),
            pltpu.VMEM((16, N), f32),
            pltpu.SemaphoreType.DMA((5,)),
            pltpu.SemaphoreType.DMA((47,)),
            pltpu.SemaphoreType.DMA((18,)),
            pltpu.SemaphoreType.REGULAR((3,)),
        ],
        compiler_params=pltpu.CompilerParams(
            collective_id=0, has_side_effects=True, vmem_limit_bytes=16 * 2**20
        ),
        name="spectra",
    )(*(pltpu.with_memory_space_constraint(v, pltpu.HBM) for v in operands))
    maps = pl.pallas_call(
        last_kernel,
        out_shape=jax.ShapeDtypeStruct((patches, N, N), f32),
        in_specs=[vmem] * 7,
        out_specs=hbm,
        scratch_shapes=[
            pltpu.VMEM((PC - 1, N, N), f32),
            pltpu.VMEM((PC - 1, N, N), bf16),
            pltpu.VMEM((PC - 1, N, N), bf16),
            pltpu.VMEM((patches, N, N), f32),
            pltpu.SemaphoreType.DMA((patches,)),
        ],
        compiler_params=pltpu.CompilerParams(vmem_limit_bytes=16 * 2**20),
        name="maps",
    )(*results)
    return maps.reshape(1, LEVELS, 1, PC, N, N)


def solution(mesh):
    return jax.shard_map(
        functools.partial(local, mesh.shape["sec"], mesh.shape["tile"]),
        mesh=mesh,
        in_specs=(P("sec", None, None, "tile"), P(None, None, "tile")),
        out_specs=P("sec", None, None, "tile", None, None),
        check_vma=False,
    )
```
